32 devices in a mesh: dp: 4 (over y, core), expert: 4 (over z), seq: 2 (over x).
Axes of the slice: x: 2, y: 2, z: 4, core: 2. Of those that a mesh axis runs over, the one named last changes fastest.
Arguments:
- inputs: bfloat16 [8, 1024, 2048], P('dp', ('expert', 'seq')), may hold values from -6 to 6
- lengths: int32 [8], P('dp'), may hold values from 256 to 1024, as said below
- attn_routes: int32 [8, 1024, 2], P('dp', ('expert', 'seq')), may hold values from 0 to 3, all different within a row
- mlp_routes: int32 [8, 1024, 2], P('dp', ('expert', 'seq')), may hold values from 0 to 3, all different within a row
- slot_order: int32 [4, 8, 256], P('dp', ('expert', 'seq')), may hold values from 0 to 255, each once within a row
- gain_attn: bfloat16 [2048], P(('dp', 'seq')), may hold values from 0.099609375 to 1.8984375
- router_attn: bfloat16 [2048, 4], P(('dp', 'seq')), may hold values from -0.09375 to 0.09375
- w_key: bfloat16 [2048, 2048], P(('dp', 'seq')), may hold values from -0.125 to 0.125
- w_value: bfloat16 [2048, 2048], P(('dp', 'seq')), may hold values from -0.125 to 0.125
- w_query: bfloat16 [4, 2048, 2048], P('expert', ('dp', 'seq')), may hold values from -0.125 to 0.125
- w_out: bfloat16 [4, 2048, 2048], P('expert', ('dp', 'seq')), may hold values from -1.5 to 1.5
- gain_mlp: bfloat16 [2048], P(('dp', 'seq')), may hold values from 0.099609375 to 1.8984375
- router_mlp: bfloat16 [2048, 4], P(('dp', 'seq')), may hold values from -0.09375 to 0.09375
- w_gate: bfloat16 [4, 2048, 5632], P('expert', None, ('dp', 'seq')), may hold values from -0.125 to 0.125
- w_up: bfloat16 [4, 2048, 5632], P('expert', None, ('dp', 'seq')), may hold values from -0.125 to 0.125
- w_down: bfloat16 [4, 5632, 2048], P('expert', ('dp', 'seq')), may hold values from -0.109375 to 0.109375
- d_out: bfloat16 [8, 1024, 2048], P('dp', ('expert', 'seq')), may hold values from -6 to 6
Outputs:
- block_out: bfloat16 [8, 1024, 2048], P('dp', ('expert', 'seq'))
- grad_x: bfloat16 [8, 1024, 2048], P('dp', ('expert', 'seq'))
- grad_gain_attn: float32 [2048], P(('dp', 'seq'))
- grad_router_attn: float32 [2048, 4], P(('dp', 'seq'))
- grad_w_key: float32 [2048, 2048], P(('dp', 'seq'))
- grad_w_value: float32 [2048, 2048], P(('dp', 'seq'))
- grad_w_query: float32 [4, 2048, 2048], P('expert', ('dp', 'seq'))
- grad_w_out: float32 [4, 2048, 2048], P('expert', ('dp', 'seq'))
- grad_gain_mlp: float32 [2048], P(('dp', 'seq'))
- grad_router_mlp: float32 [2048, 4], P(('dp', 'seq'))
- grad_w_gate: float32 [4, 2048, 5632], P('expert', None, ('dp', 'seq'))
- grad_w_up: float32 [4, 2048, 5632], P('expert', None, ('dp', 'seq'))
- grad_w_down: float32 [4, 5632, 2048], P('expert', ('dp', 'seq'))
The draws below stay inside these ranges and needn't reach their ends.
Inputs may be any that keep to these rules, and one draw needn't show every extreme that they name: `lengths`: in each group of 2 consecutive sequences one has exactly 1024 valid slots. `attn_routes`: each slot names 2 different experts; every expert is named by some slot. `mlp_routes`: each slot names 2 different experts; every expert is named by some slot. `slot_order`: the 256 values of each row are a permutation.
All inputs are finite; a program needn't handle non-finite values.
Results may differ from the reference program's by a relative error of at most 0.025.
Values may be sent and summed in bfloat16 or wider, within the bound.
No kernel may reach another device: no remote copies, remote signals or barrier semaphores. Data moves between devices by JAX's collectives and lax.ppermute only.
A program may use at most 384 MiB of HBM per device.

```python
import jax
import jax.numpy as jnp
from jax import lax

D = 2048
FF = 5632
HEAD = 128
TOP = 2
SEQ_GROUP = 2
H = 2048
EXPERTS = 4
LEN = 1024
STRETCH = 128
TOK_DEV = 256
CAP = 128
SEQS = 8
GROUPS = 4
BLOCKS = 8


def draw_lengths(key, part):
    key = jax.random.fold_in(key, 11)
    first_key, second_key = jax.random.split(key)
    groups = SEQS // SEQ_GROUP
    drawn = jax.random.randint(first_key, (groups, SEQ_GROUP), LEN // 4, LEN + 1)
    chosen = jax.random.randint(second_key, (groups, 1), 0, SEQ_GROUP)
    columns = jnp.arange(SEQ_GROUP, dtype=jnp.int32)[None, :]
    return jnp.where(columns == chosen, LEN, drawn).reshape(SEQS).astype(jnp.int32)


def level_of(stream_key, extent, cuts, low, top_value):
    level = 1.0
    for axis_at, blocks in cuts:
        steps = jax.random.uniform(jax.random.fold_in(jax.random.fold_in(stream_key, 6), axis_at), (blocks,), jnp.float32, low / len(cuts), top_value / len(cuts))
        level = level * jnp.repeat(jnp.exp(steps), extent[axis_at] // blocks).reshape((-1,) + (1,) * (len(extent) - 1 - axis_at))
    return level


def distinct(key, rows, count, top, lift):
    order = jax.random.permutation(jax.random.fold_in(key, 1), count)
    boost = order
    for power in range(3):
        boost = boost * boost // count
    boost = boost * lift // count
    chance = jax.random.randint(jax.random.fold_in(key, 2), (rows, count), 0, 4096) + boost
    fixed_rows = jax.random.permutation(jax.random.fold_in(key, 3), rows)[jnp.arange(count) % rows]
    chance = jnp.where(jnp.arange(rows)[:, None] == fixed_rows[None, :], 1 << 14, chance)
    score = chance * count + jnp.arange(count)
    return lax.top_k(score.astype(jnp.int32), top)[1].astype(jnp.int32)


def gaussian(stream_key, extent, deviation, reach, cuts=(), held_as=jnp.bfloat16):
    values = jax.random.normal(stream_key, extent, jnp.float32) * deviation
    if len(cuts) > 0:
        values = level_of(stream_key, extent, cuts, -0.22, 0.18) * values
    return jnp.clip(values, min=-reach, max=reach).astype(held_as)


def setup_inputs(seed: int = 0) -> dict:
    splits = jax.random.split(jax.random.key(seed), 18)
    inputs = gaussian(splits[0], (SEQS, LEN, D), 1.0, 6.0, ((0, 4), (1, 8)))
    lengths = draw_lengths(jax.random.fold_in(splits[17], 71), 0)
    attn_routes = distinct(splits[2], SEQS * LEN, EXPERTS, TOP, 4096).reshape((SEQS, LEN, TOP))
    mlp_routes = distinct(splits[3], SEQS * LEN, EXPERTS, TOP, 4096).reshape((SEQS, LEN, TOP))
    slot_order = jax.vmap(lambda own: jax.random.permutation(own, TOK_DEV))(jax.random.split(splits[4], GROUPS * BLOCKS)).reshape((GROUPS, BLOCKS, TOK_DEV)).astype(jnp.int32)
    gain_attn = jnp.clip(1.0 + 0.18 * jax.random.normal(splits[5], (D,), jnp.float32), 0.099609375, 1.8984375).astype(jnp.bfloat16)
    router_attn = gaussian(splits[6], (D, EXPERTS), (2 * D) ** -0.5, 0.09375, ((0, 8),))
    w_key = gaussian(splits[7], (D, H), D ** -0.5, 0.125, ((0, 8),))
    w_value = gaussian(splits[8], (D, H), D ** -0.5, 0.125, ((0, 8),))
    w_query = gaussian(splits[9], (EXPERTS, D, H), D ** -0.5, 0.125, ((0, 4), (1, 8)))
    w_out = gaussian(splits[10], (EXPERTS, H, D), (max(H // 128, 1)) ** -0.5, 1.5, ((0, 4), (1, 8)))
    gain_mlp = jnp.clip(1.0 + 0.18 * jax.random.normal(splits[11], (D,), jnp.float32), 0.099609375, 1.8984375).astype(jnp.bfloat16)
    router_mlp = gaussian(splits[12], (D, EXPERTS), (2 * D) ** -0.5, 0.09375, ((0, 8),))
    w_gate = gaussian(splits[13], (EXPERTS, D, FF), D ** -0.5, 0.125, ((0, 4), (2, 8)))
    w_up = gaussian(splits[14], (EXPERTS, D, FF), D ** -0.5, 0.125, ((0, 4), (2, 8)))
    w_down = gaussian(splits[15], (EXPERTS, FF, D), (FF // 2) ** -0.5, 0.109375, ((0, 4), (1, 8)))
    d_out = gaussian(splits[16], (SEQS, LEN, D), 1.0, 6.0, ((0, 4), (1, 8)))
    return dict(inputs=inputs, lengths=lengths, attn_routes=attn_routes, mlp_routes=mlp_routes, slot_order=slot_order, gain_attn=gain_attn, router_attn=router_attn, w_key=w_key, w_value=w_value, w_query=w_query, w_out=w_out, gain_mlp=gain_mlp, router_mlp=router_mlp, w_gate=w_gate, w_up=w_up, w_down=w_down, d_out=d_out)


EPS = 1e-06
NEG = -1e+30
HIGH = lax.Precision.HIGHEST

@jax.custom_vjp
def low(v):
    return lax.optimization_barrier(v.astype(jnp.bfloat16)).astype(jnp.float32)

@jax.custom_vjp
def low_back(v):
    return v

def low_keep(v):
    return (low(v), None)

def low_pass(kept, grad):
    return (grad,)

def back_keep(v):
    return (v, None)

def back_low(kept, grad):
    return (low(grad),)
low.defvjp(low_keep, low_pass)
low_back.defvjp(back_keep, back_low)

def matmul(left, right):
    return jnp.dot(left, right, precision=HIGH)

def rms_norm(values, gain):
    return values * lax.rsqrt(lax.optimization_barrier(jnp.mean(values * values, axis=-1, keepdims=True)) + EPS) * gain

def to_blocks(array):
    rest = array.shape[2:]
    groups = array.shape[0] // SEQ_GROUP
    blocks = array.shape[1] // STRETCH
    shaped = array.reshape((groups, SEQ_GROUP, blocks, STRETCH) + rest)
    return jnp.moveaxis(shaped, 2, 1).reshape((groups, blocks, SEQ_GROUP * STRETCH) + rest)

def from_blocks(array):
    rest = array.shape[3:]
    groups, blocks = (array.shape[0], array.shape[1])
    shaped = array.reshape((groups, blocks, SEQ_GROUP, STRETCH) + rest)
    return jnp.moveaxis(shaped, 1, 2).reshape((groups * SEQ_GROUP, blocks * STRETCH) + rest)

def sequence_order(array):
    groups, blocks = (array.shape[0], array.shape[1])
    shaped = array.reshape(groups, blocks, SEQ_GROUP, STRETCH, -1)
    return jnp.moveaxis(shaped, 1, 2).reshape(groups, SEQ_GROUP * blocks * STRETCH, -1)

def route_pairs(routes, order, is_valid):
    tokens_here, top_count = routes.shape
    pairs = tokens_here * top_count
    target = routes.reshape(pairs)
    second = lax.broadcasted_iota(jnp.int32, routes.shape, 1)
    priority = (order[:, None] * top_count + second).reshape(pairs)
    living = jnp.broadcast_to(is_valid[:, None], routes.shape).reshape(pairs)
    earlier = (target[:, None] == target[None, :]) & (priority[None, :] < priority[:, None]) & living[None, :]
    slot_index = lax.optimization_barrier(jnp.sum(earlier.astype(jnp.int32), axis=1, dtype=jnp.int32))
    kept_pair = living & (slot_index < CAP)
    expert_ids = lax.broadcasted_iota(jnp.int32, (1, EXPERTS, 1), 1)
    slot_ids = lax.broadcasted_iota(jnp.int32, (1, 1, CAP), 2)
    table = kept_pair[:, None, None] & (target[:, None, None] == expert_ids) & (slot_index[:, None, None] == slot_ids)
    pair_ids = lax.broadcasted_iota(jnp.int32, (pairs, 1, 1), 0)
    source_pair = lax.optimization_barrier(jnp.sum(jnp.where(table, pair_ids, 0), axis=0, dtype=jnp.int32))
    filled = jnp.any(table, axis=0)
    flat_slot = target * CAP + jnp.minimum(slot_index, CAP - 1)
    return (kept_pair.reshape(routes.shape), source_pair // top_count, filled, flat_slot.reshape(routes.shape))

def gate_values(normed, router, routes):
    logits = matmul(normed, router)
    chosen = jnp.take_along_axis(logits, routes, axis=-1)
    top = lax.optimization_barrier(jnp.max(chosen, axis=-1, keepdims=True))
    expo = jnp.exp(chosen - top)
    return expo / lax.optimization_barrier(jnp.sum(expo, axis=-1, keepdims=True))

def dispatch(normed, token, filled):
    groups, blocks = (token.shape[0], token.shape[1])
    index = token.reshape(groups, blocks, -1)
    rows = jnp.take_along_axis(normed, index[:, :, :, None], axis=2)
    rows = jnp.where(filled.reshape(groups, blocks, -1)[:, :, :, None], rows, 0.0)
    rows = low_back(rows)
    return rows.reshape(groups, blocks, EXPERTS, CAP, -1).transpose(2, 0, 1, 3, 4).reshape(EXPERTS, groups * blocks * CAP, -1)

def combine(slots_out, flat_slot, weight):
    groups, blocks = (flat_slot.shape[0], flat_slot.shape[1])
    arranged = slots_out.reshape(EXPERTS, groups, blocks, CAP, -1).transpose(1, 2, 0, 3, 4)
    arranged = arranged.reshape(groups, blocks, EXPERTS * CAP, -1)
    pairs = jnp.take_along_axis(arranged, flat_slot.reshape(groups, blocks, -1)[:, :, :, None], axis=2)
    pairs = pairs.reshape(groups, blocks, TOK_DEV, TOP, -1)
    return lax.optimization_barrier(jnp.sum(weight[..., None] * pairs, axis=3))

def attend_block(query, row_codes, keys, values, key_limit):
    count = query.shape[0]
    key_codes = lax.broadcasted_iota(jnp.int32, (1, keys.shape[0]), 1)
    visible = (key_codes // LEN == row_codes[:, None] // LEN) & (key_codes <= row_codes[:, None]) & (key_codes % LEN < key_limit[None, :])
    q_four = query.reshape(count, -1, HEAD)
    k_four = keys.reshape(keys.shape[0], -1, HEAD)
    v_four = values.reshape(values.shape[0], -1, HEAD)
    scores = low_back(jnp.einsum('rhd,khd->hrk', q_four, k_four, precision=HIGH) * HEAD ** (-0.5))
    scores = jnp.where(visible[None], scores, NEG)
    top = lax.optimization_barrier(jnp.max(scores, axis=2, keepdims=True))
    expo = jnp.exp(scores - top)
    probs = low(expo / lax.optimization_barrier(jnp.sum(expo, axis=2, keepdims=True)))
    mixed = jnp.einsum('hrk,khd->rhd', probs, v_four, precision=HIGH)
    return low_back(low(mixed.reshape(count, -1)))

def attend_group(parts):
    queries, row_codes, keys, values, key_limit = parts
    count = queries.shape[0]
    size = min(512, count)

    def one_block(item):
        return attend_block(item[0], item[1], keys, values, key_limit)
    mixed = lax.map(jax.checkpoint(one_block), (queries.reshape(count // size, size, -1), row_codes.reshape(count // size, size)))
    return mixed.reshape(count, -1)

def expert_mlp(parts):
    rows, gate_w, up_w, down_w = parts
    gate = low_back(matmul(rows, gate_w))
    upper = low_back(matmul(rows, up_w))
    hidden = low(jax.nn.silu(gate) * upper)
    return low_back(low(matmul(hidden, down_w)))

def reference(inputs, lengths, attn_routes, mlp_routes, slot_order, gain_attn, router_attn, w_key, w_value, w_query, w_out, gain_mlp, router_mlp, w_gate, w_up, w_down, d_out):
    groups = inputs.shape[0] // SEQ_GROUP
    blocks = inputs.shape[1] // STRETCH
    grid = (groups, blocks, TOK_DEV)
    block_ids = lax.broadcasted_iota(jnp.int32, grid, 1)
    local_ids = lax.broadcasted_iota(jnp.int32, grid, 2)
    seq_ids = local_ids // STRETCH
    place = block_ids * STRETCH + local_ids % STRETCH
    seq_lengths = lengths.reshape(groups, SEQ_GROUP)
    limit = jnp.take_along_axis(jnp.broadcast_to(seq_lengths[:, None, :], (groups, blocks, SEQ_GROUP)), seq_ids, axis=2)
    is_valid = place < limit
    codes = seq_ids * LEN + place
    attn_idx = to_blocks(attn_routes)
    mlp_idx = to_blocks(mlp_routes)
    router_fn = jax.vmap(jax.vmap(route_pairs))
    attn_kept, attn_token, attn_filled, attn_flat = router_fn(attn_idx, slot_order, is_valid)
    mlp_kept, mlp_token, mlp_filled, mlp_flat = router_fn(mlp_idx, slot_order, is_valid)
    attn_codes = jnp.take_along_axis(codes, attn_token.reshape(groups, blocks, -1), axis=2)
    attn_codes = jnp.where(attn_filled.reshape(groups, blocks, -1), attn_codes, 0)
    code_groups = attn_codes.reshape(groups, blocks, EXPERTS, CAP).transpose(0, 2, 1, 3).reshape(groups, -1)
    key_limits = jnp.repeat(seq_lengths, LEN, axis=1)
    attn_keep = attn_kept.astype(jnp.float32)
    mlp_keep = mlp_kept.astype(jnp.float32)

    def layer(x_in, norm_one, route_one, key_w, value_w, query_w, out_w, norm_two, route_two, gate_w, up_w, down_w):
        normed_one = low(rms_norm(x_in, norm_one))
        attn_gates = gate_values(normed_one, route_one, attn_idx)
        keys_here = low_back(low(matmul(normed_one, key_w)))
        values_here = low_back(low(matmul(normed_one, value_w)))
        attn_rows = dispatch(normed_one, attn_token, attn_filled)
        queries = low_back(low(jnp.einsum('erd,edh->erh', attn_rows, query_w, precision=HIGH)))
        q_groups = queries.reshape(EXPERTS, groups, -1, H).transpose(1, 0, 2, 3).reshape(groups, -1, H)
        mixed = lax.map(attend_group, (q_groups, code_groups, sequence_order(keys_here), sequence_order(values_here), key_limits))
        mixed = mixed.reshape(groups, EXPERTS, -1, H).transpose(1, 0, 2, 3).reshape(EXPERTS, -1, H)
        attn_out = low_back(low(jnp.einsum('erh,ehd->erd', mixed, out_w, precision=HIGH)))
        hidden = x_in + combine(attn_out, attn_flat, attn_gates * attn_keep)
        normed_two = low(rms_norm(hidden, norm_two))
        mlp_gates = gate_values(normed_two, route_two, mlp_idx)
        mlp_rows = dispatch(normed_two, mlp_token, mlp_filled)
        mlp_out = lax.map(jax.checkpoint(expert_mlp), (mlp_rows, gate_w, up_w, down_w))
        return hidden + combine(mlp_out, mlp_flat, mlp_gates * mlp_keep)
    x_dev = to_blocks(inputs).astype(jnp.float32)
    f32 = jnp.float32
    result, pull = jax.vjp(layer, x_dev, gain_attn.astype(f32), router_attn.astype(f32), w_key.astype(f32), w_value.astype(f32), w_query.astype(f32), w_out.astype(f32), gain_mlp.astype(f32), router_mlp.astype(f32), w_gate.astype(f32), w_up.astype(f32), w_down.astype(f32))
    grads = pull(to_blocks(d_out).astype(f32))
    block_out = from_blocks(result).astype(jnp.bfloat16)
    grad_x = from_blocks(grads[0]).astype(jnp.bfloat16)
    return (block_out, grad_x, grads[1], grads[2], grads[3], grads[4], grads[5], grads[6], grads[7], grads[8], grads[9], grads[10], grads[11])
```

```python
import functools

import jax
import jax.numpy as jnp
from jax import lax
from jax.experimental import pallas as pl
from jax.experimental.pallas import tpu as pltpu
from jax.sharding import PartitionSpec as P

HEAD = 128
EPS = 1e-06
NEG = -1e30
HIGH = lax.Precision.HIGHEST
BF = jnp.bfloat16
F32 = jnp.float32
LOG2E = 1.4426950408889634


def dot(left, right):
    return jnp.dot(left, right, preferred_element_type=F32)


def dot_t(left, right):
    return lax.dot_general(left, right, (((1,), (1,)), ((), ())), preferred_element_type=F32)


def t_dot(left, right):
    return lax.dot_general(left, right, (((0,), (0,)), ((), ())), preferred_element_type=F32)


def ring(count, shift):
    return [(j, (j + shift) % count) for j in range(count)]


def flip(count, bit):
    return [(j, j ^ bit) for j in range(count)]


def swap_x(value):
    return lax.ppermute(value, "seq", flip(2, 1))


def swap_core(value):
    return lax.ppermute(value, "dp", flip(lax.axis_size("dp"), 1))


def swap_y(value):
    return lax.ppermute(value, "dp", flip(4, 2))


def z_rounds(pieces, sign):
    count = lax.axis_size("expert")
    return [pieces[0]] + [
        lax.ppermute(pieces[r], "expert", ring(count, sign * r)) for r in range(1, count)
    ]


def is_small():
    return lax.axis_size("dp") == 4 and lax.axis_size("expert") == 4


def add_low(*terms):
    total = terms[0].astype(F32)
    for term in terms[1:]:
        total = total + term.astype(F32)
    return total.astype(terms[0].dtype)


def square_gather(piece):
    if not is_small():
        every = lax.all_gather(piece, ("dp", "seq"), axis=0, tiled=False)
        return [every[j] for j in range(every.shape[0])]
    half = piece.shape[0] // 2
    along_x = swap_x(piece)
    along_y = swap_y(piece)
    corner = jnp.concatenate([swap_y(along_x[:half]), swap_x(along_y[half:])], axis=0)
    own = [piece, along_x, along_y, corner]
    return own + [swap_core(part) for part in own]


def square_scatter(parts):
    if not is_small():
        return lax.psum_scatter(
            jnp.stack(parts), ("dp", "seq"), scatter_dimension=0, tiled=False
        )
    half = parts[0].shape[0] // 2
    corner = add_low(parts[3], swap_core(parts[7]))
    for_x = add_low(parts[1], swap_core(parts[5]))
    for_y = add_low(parts[2], swap_core(parts[6]))
    own = add_low(parts[0], swap_core(parts[4]))
    via_x = swap_x(corner[:half])
    via_y = swap_y(corner[half:])
    from_x = [swap_x(for_x[:half]), swap_x(add_low(for_x[half:], via_y))]
    from_y = [swap_y(for_y[half:]), swap_y(add_low(for_y[:half], via_x))]
    low = add_low(own[:half], from_x[0], from_y[1])
    high = add_low(own[half:], from_x[1], from_y[0])
    return jnp.concatenate([low, high], axis=0)


def group_gather(block):
    count = lax.axis_size("expert")
    if is_small():
        half = block.shape[0] // 2
        up = lax.ppermute(block, "expert", ring(count, -1))
        down = lax.ppermute(block, "expert", ring(count, 1))
        far = jnp.concatenate(
            [
                lax.ppermute(down[:half], "expert", ring(count, 1)),
                lax.ppermute(up[half:], "expert", ring(count, -1)),
            ],
            axis=0,
        )
        own = [block, up, far, down]
        return own + [swap_x(part) for part in own]
    e_at, s_at = lax.axis_index("expert"), lax.axis_index("seq")
    every = lax.all_gather(block, ("expert", "seq"), axis=0, tiled=False)
    wanted = [
        (lax.rem(e_at + r, count)) * 2 + lax.rem(s_at + sp, 2)
        for sp in range(2)
        for r in range(count)
    ]
    return [lax.dynamic_index_in_dim(every, at, 0, keepdims=False) for at in wanted]


def group_scatter(parts):
    count = lax.axis_size("expert")
    if not is_small():
        e_at, s_at = lax.axis_index("expert"), lax.axis_index("seq")
        stacked = jnp.stack(parts)
        spots = [
            (lax.rem(s_at + b % 2, 2)) * count + lax.rem(b // 2 - e_at + count, count)
            for b in range(2 * count)
        ]
        ordered = jnp.stack(
            [lax.dynamic_index_in_dim(stacked, at, 0, keepdims=False) for at in spots]
        )
        return lax.psum_scatter(ordered, ("expert", "seq"), scatter_dimension=0, tiled=False)
    half = parts[0].shape[0] // 2
    far = add_low(parts[2], swap_x(parts[6]))
    up = add_low(parts[1], swap_x(parts[5]))
    down = add_low(parts[3], swap_x(parts[7]))
    own = add_low(parts[0], swap_x(parts[4]))
    far_up = lax.ppermute(far[:half], "expert", ring(count, 1))
    far_down = lax.ppermute(far[half:], "expert", ring(count, -1))
    up_low = lax.ppermute(add_low(up[:half], far_up), "expert", ring(count, 1))
    up_high = lax.ppermute(up[half:], "expert", ring(count, 1))
    down_high = lax.ppermute(add_low(down[half:], far_down), "expert", ring(count, -1))
    down_low = lax.ppermute(down[:half], "expert", ring(count, -1))
    return jnp.concatenate(
        [add_low(own[:half], up_low, down_low), add_low(own[half:], up_high, down_high)], axis=0
    )


def dp_gather(piece):
    if not is_small():
        return lax.all_gather(piece, "dp", axis=0, tiled=True)
    at = lax.axis_index("dp")
    core, row = at % 2, at // 2
    along_y = swap_y(piece)
    beside, across = swap_core(piece), swap_core(along_y)
    here = jnp.where(
        core == 0,
        jnp.concatenate([piece, beside], axis=0),
        jnp.concatenate([beside, piece], axis=0),
    )
    there = jnp.where(
        core == 0,
        jnp.concatenate([along_y, across], axis=0),
        jnp.concatenate([across, along_y], axis=0),
    )
    return jnp.where(
        row == 0,
        jnp.concatenate([here, there], axis=0),
        jnp.concatenate([there, here], axis=0),
    )


def dp_scatter(part_of):
    count = lax.axis_size("dp")
    at = lax.axis_index("dp")
    if count != 4:
        parts = jnp.stack([part_of(jnp.int32(d)) for d in range(count)])
        return lax.psum_scatter(parts, "dp", scatter_dimension=0, tiled=False)
    beside, across = part_of(at ^ 1), part_of(at ^ 3)
    far, own = part_of(at ^ 2), part_of(at)
    far = add_low(far, swap_core(across))
    own = add_low(own, swap_core(beside))
    return add_low(own, swap_y(far))


def route_pairs(routes, order, is_valid, capacity):
    tokens_here, top_count = routes.shape
    pairs = tokens_here * top_count
    target = routes.reshape(pairs)
    second = lax.broadcasted_iota(jnp.int32, routes.shape, 1)
    priority = (order[:, None] * top_count + second).reshape(pairs)
    living = jnp.broadcast_to(is_valid[:, None], routes.shape).reshape(pairs)
    earlier = (
        (target[:, None] == target[None, :])
        & (priority[None, :] < priority[:, None])
        & living[None, :]
    )
    slot_index = jnp.sum(earlier.astype(jnp.int32), axis=1, dtype=jnp.int32)
    kept_pair = living & (slot_index < capacity)
    return (kept_pair.reshape(routes.shape), slot_index.reshape(routes.shape))


def spots(routes, kept, slot_index, experts, capacity):
    away = lax.rem(lax.axis_index("expert") - routes + experts, experts)
    flat = jnp.where(kept, away * capacity + slot_index, -1)
    slots = lax.broadcasted_iota(jnp.int32, (1, experts * capacity), 1)
    return [flat[:, k : k + 1] == slots for k in range(routes.shape[1])]


def weigh(hot, weight):
    return sum(jnp.where(hot[k], weight[:, k : k + 1], 0.0) for k in range(len(hot)))


def in_two(value):
    high = lax.reduce_precision(value, 8, 7)
    return high.astype(BF), (value - high).astype(BF)


def rms_norm(values, gain):
    return values * lax.rsqrt(jnp.mean(values * values, axis=-1, keepdims=True) + EPS) * gain


def norm_back(values, gain, grad):
    factor = lax.rsqrt(jnp.mean(values * values, axis=1, keepdims=True) + EPS)
    unit = values * factor
    gain_grad = jnp.sum(grad * unit, axis=0)
    scaled = grad * gain
    return (factor * (scaled - unit * jnp.mean(scaled * unit, axis=1, keepdims=True)), gain_grad)


def gate_values(normed, router, routes):
    logits = dot(normed, router)
    experts = lax.broadcasted_iota(jnp.int32, logits.shape, 1)
    chosen = jnp.concatenate(
        [
            jnp.sum(jnp.where(routes[:, k : k + 1] == experts, logits, 0.0), axis=1, keepdims=True)
            for k in range(routes.shape[1])
        ],
        axis=1,
    )
    top = jnp.max(chosen, axis=1, keepdims=True)
    expo = jnp.exp(chosen - top)
    return expo / jnp.sum(expo, axis=1, keepdims=True)


def gate_grads(normed, router, routes, gates, gate_grad):
    chosen = gates * (gate_grad - jnp.sum(gates * gate_grad, axis=1, keepdims=True))
    experts = lax.broadcasted_iota(jnp.int32, (1, 1, router.shape[1]), 2)
    logit_grad = jnp.sum(jnp.where(routes[:, :, None] == experts, chosen[:, :, None], 0.0), axis=1)
    router_grad = jnp.dot(normed.astype(F32).T, logit_grad, precision=HIGH)
    input_grad = jnp.dot(logit_grad, router.astype(F32).T, precision=HIGH)
    return (router_grad, input_grad)


def tile_bias(info, tile, blocks, tokens):
    stretch = tokens // 2
    row_seq, row_place = info[:, 0:1], info[:, 1:2]
    rows = info.shape[0]
    col = lax.broadcasted_iota(jnp.int32, (rows, tokens), 1)
    same = (col // stretch) == row_seq
    near = jnp.where(same, 0.0, NEG)
    place = lax.rem(col, stretch)
    diagonal = [
        jnp.where(same & (place + (tile * blocks + j) * stretch <= row_place), 0.0, NEG)
        for j in range(blocks)
    ]
    return jnp.concatenate([near] * (tile * blocks) + diagonal, axis=1)


def picked(ref, index, at, count):
    return jnp.concatenate([ref[index[at + j]] for j in range(count)], axis=0)


def attend_kernel(index, info, query, keys, values, mixed, logs, *, blocks):
    head = pl.program_id(0)
    total, capacity, _ = query.shape
    tokens = keys.shape[1]
    rate = HEAD ** (-0.5) * LOG2E
    lane = lax.broadcasted_iota(jnp.int32, (capacity, logs.shape[2]), 1)
    for tile in range(total // blocks):
        first = tile * blocks
        q = picked(query, index, first, blocks)
        k = picked(keys, index, 0, first + blocks)
        v = picked(values, index, 0, first + blocks)
        bias = tile_bias(picked(info, index, first, blocks), tile, blocks, tokens)
        scores = dot_t(q, k) + bias
        top = jnp.max(scores, axis=1, keepdims=True)
        expo = jnp.exp2((scores - top) * rate)
        norm = jnp.sum(expo, axis=1, keepdims=True)
        out = (dot(expo.astype(BF), v) / norm).astype(BF)
        log = top * rate + jnp.log2(norm)
        for j in range(blocks):
            rows = slice(j * capacity, (j + 1) * capacity)
            mixed[index[first + j]] = out[rows]
            held = logs[index[first + j]]
            logs[index[first + j]] = jnp.where(lane == head, log[rows], held)


def attend_back_kernel(
    index, info, query, keys, values, logs, mixed_grad, q_grad, k_grad, v_grad, k_sum, v_sum, *, blocks
):
    head = pl.program_id(0)
    total, capacity, _ = query.shape
    tokens = keys.shape[1]
    scale = HEAD ** (-0.5)
    rate = scale * LOG2E
    k_sum[...] = jnp.zeros_like(k_sum)
    v_sum[...] = jnp.zeros_like(v_sum)
    for tile in range(total // blocks):
        first = tile * blocks
        q = picked(query, index, first, blocks)
        k = picked(keys, index, 0, first + blocks)
        v = picked(values, index, 0, first + blocks)
        g = picked(mixed_grad, index, first, blocks)
        log = picked(logs, index, first, blocks)
        lane = lax.broadcasted_iota(jnp.int32, log.shape, 1)
        log = jnp.sum(jnp.where(lane == head, log, 0.0), axis=1, keepdims=True)
        bias = tile_bias(picked(info, index, first, blocks), tile, blocks, tokens)
        probs = jnp.exp2((dot_t(q, k) + bias) * rate - log)
        prob_grad = dot_t(g, v)
        center = jnp.sum(probs * prob_grad, axis=1, keepdims=True)
        score_grad = (probs * (prob_grad - center)).astype(BF)
        out = (dot(score_grad, k) * scale).astype(BF)
        for j in range(blocks):
            q_grad[index[first + j]] = out[j * capacity : (j + 1) * capacity]
        k_part = t_dot(score_grad, q)
        v_part = t_dot(probs.astype(BF), g)
        for j in range(first + blocks):
            rows = slice(j * tokens, (j + 1) * tokens)
            k_sum[index[j]] += k_part[rows]
            v_sum[index[j]] += v_part[rows]
    k_grad[...] = (k_sum[...] * scale).astype(BF)
    v_grad[...] = v_sum[...].astype(BF)


def head_spec(shape, skip=0):
    return pl.BlockSpec((shape[0], shape[1], HEAD), lambda h, index: (0, 0, h + skip))


def flat_spec(shape):
    return pl.BlockSpec(shape, lambda h, index: (0, 0, 0))


def attend(index, info, query, both):
    total, capacity, width = query.shape
    tokens = both.shape[1]
    heads = width // HEAD
    blocks = max(1, 256 // capacity)
    log_shape = (total, capacity, 128)
    flops = 4 * total * capacity * total * tokens * width
    return pl.pallas_call(
        functools.partial(attend_kernel, blocks=blocks),
        grid_spec=pltpu.PrefetchScalarGridSpec(
            num_scalar_prefetch=1,
            grid=(heads,),
            in_specs=[
                flat_spec(info.shape),
                head_spec(query.shape),
                head_spec(both.shape),
                head_spec(both.shape, heads),
            ],
            out_specs=[head_spec(query.shape), flat_spec(log_shape)],
        ),
        out_shape=[
            jax.ShapeDtypeStruct(query.shape, BF),
            jax.ShapeDtypeStruct(log_shape, F32),
        ],
        compiler_params=pltpu.CompilerParams(vmem_limit_bytes=50 << 20),
        cost_estimate=pl.CostEstimate(
            flops=flops, bytes_accessed=16 << 20, transcendentals=flops // 512
        ),
    )(index, info, query, both, both)


def attend_back(index, info, query, both, logs, mixed_grad):
    total, capacity, width = query.shape
    tokens = both.shape[1]
    heads = width // HEAD
    blocks = max(1, 256 // capacity)
    flops = 10 * total * capacity * total * tokens * width
    key_shape = (total, tokens, width)
    return pl.pallas_call(
        functools.partial(attend_back_kernel, blocks=blocks),
        grid_spec=pltpu.PrefetchScalarGridSpec(
            num_scalar_prefetch=1,
            grid=(heads,),
            in_specs=[
                flat_spec(info.shape),
                head_spec(query.shape),
                head_spec(both.shape),
                head_spec(both.shape, heads),
                flat_spec(logs.shape),
                head_spec(mixed_grad.shape),
            ],
            out_specs=[head_spec(query.shape), head_spec(key_shape), head_spec(key_shape)],
            scratch_shapes=[
                pltpu.VMEM((total, tokens, HEAD), F32),
                pltpu.VMEM((total, tokens, HEAD), F32),
            ],
        ),
        out_shape=[
            jax.ShapeDtypeStruct(query.shape, BF),
            jax.ShapeDtypeStruct(key_shape, BF),
            jax.ShapeDtypeStruct(key_shape, BF),
        ],
        compiler_params=pltpu.CompilerParams(vmem_limit_bytes=50 << 20),
        cost_estimate=pl.CostEstimate(
            flops=flops, bytes_accessed=32 << 20, transcendentals=flops // 1280
        ),
    )(index, info, query, both, both, logs, mixed_grad)


def body(
    inputs,
    lengths,
    attn_routes,
    mlp_routes,
    slot_order,
    gain_attn,
    router_attn,
    w_key,
    w_value,
    w_query,
    w_out,
    gain_mlp,
    router_mlp,
    w_gate,
    w_up,
    w_down,
    d_out,
):
    seq_count, stretch, width = inputs.shape
    tok = seq_count * stretch
    top_count = attn_routes.shape[2]
    experts = router_attn.shape[1]
    cap = top_count * tok // experts
    slots = experts * cap
    dps, seqs = lax.axis_size("dp"), lax.axis_size("seq")
    total = experts * seqs
    e_at, s_at, d_at = lax.axis_index("expert"), lax.axis_index("seq"), lax.axis_index("dp")
    block = e_at * seqs + s_at
    rows_own = w_key.shape[0]
    inner = w_key.shape[1]
    half = inner // seqs

    absolute = lax.broadcasted_iota(jnp.int32, (total,), 0)
    index = lax.rem(absolute % seqs - s_at + seqs, seqs) * experts + lax.rem(
        absolute // seqs - e_at + experts, experts
    )
    block_of = lax.rem(absolute % experts + e_at, experts) * seqs + lax.rem(
        absolute // experts + s_at, seqs
    )

    x_low = inputs.reshape(tok, width)
    x_blocks = group_gather(x_low)

    def halves(weight):
        split = weight.reshape(rows_own, dps, seqs, inner // (dps * seqs))
        return (
            lax.dynamic_index_in_dim(split, s_at, 2, keepdims=False).reshape(rows_own, half),
            lax.dynamic_index_in_dim(split, 1 - s_at, 2, keepdims=False).reshape(rows_own, half),
        )

    split_all = [halves(weight) for weight in (w_key, w_value, w_query[0])]
    w_keep = jnp.concatenate([pair[0] for pair in split_all], axis=1)
    w_give = jnp.concatenate([pair[1] for pair in split_all], axis=1)
    w_took = swap_x(w_give)
    w_pair = jnp.where(
        s_at == 0,
        jnp.concatenate([w_keep, w_took], axis=0),
        jnp.concatenate([w_took, w_keep], axis=0),
    )
    w_three = dp_gather(w_pair)
    out_w = dp_gather(w_out[0])

    small = jnp.concatenate(
        [gain_attn[None], router_attn.T, gain_mlp[None], router_mlp.T], axis=0
    )
    small = lax.all_gather(small, ("dp", "seq"), axis=1, tiled=True)
    norm_one = small[0].astype(F32)
    route_one = small[1 : 1 + experts].T
    norm_two = small[1 + experts].astype(F32)
    route_two = small[2 + experts :].T

    column = lax.broadcasted_iota(jnp.int32, (seq_count, stretch), 1)
    is_valid = (block * stretch + column < lengths[:, None]).reshape(tok)
    order = slot_order.reshape(tok)
    attn_idx = attn_routes.reshape(tok, top_count)
    mlp_idx = mlp_routes.reshape(tok, top_count)
    attn_kept, attn_slot = route_pairs(attn_idx, order, is_valid, cap)
    mlp_kept, mlp_slot = route_pairs(mlp_idx, order, is_valid, cap)
    attn_keep = attn_kept.astype(F32)
    mlp_keep = mlp_kept.astype(F32)
    attn_hot = spots(attn_idx, attn_kept, attn_slot, experts, cap)
    mlp_hot = spots(mlp_idx, mlp_kept, mlp_slot, experts, cap)
    attn_pick = (attn_hot[0] | attn_hot[1]).astype(BF)
    mlp_pick = (mlp_hot[0] | mlp_hot[1]).astype(BF)

    g_low = d_out.reshape(tok, width)
    grad_out = g_low.astype(F32)
    g_send = t_dot(mlp_pick, g_low).astype(BF).reshape(experts, cap, width)
    g_took = z_rounds([g_send[r] for r in range(experts)], -1)
    g_parts = square_gather(jnp.concatenate(g_took, axis=0))
    g_rows = jnp.concatenate(g_parts, axis=0)
    gate_w, up_w, down_w = w_gate[0], w_up[0], w_down[0]
    act_back = dot_t(g_rows, down_w)

    flat = jnp.where(attn_kept, attn_idx * cap + attn_slot, -1)
    slot_ids = lax.broadcasted_iota(jnp.int32, (1, slots), 1)
    tok_ids = lax.broadcasted_iota(jnp.int32, (tok, 1), 0) + 1
    table = sum(
        jnp.sum(jnp.where(flat[:, k : k + 1] == slot_ids, tok_ids, 0), axis=0, dtype=jnp.int32)
        for k in range(top_count)
    )
    tables = lax.all_gather(table.reshape(experts, cap), ("expert", "seq"), axis=0, tiled=False)
    tables = lax.dynamic_index_in_dim(tables, e_at, 1, keepdims=False)[block_of] - 1
    pick = (tables[:, :, None] == lax.broadcasted_iota(jnp.int32, (1, 1, tok), 2)).astype(BF)
    row_seq = jnp.where(tables >= 0, tables // stretch, 0)
    row_place = jnp.where(tables >= 0, block_of[:, None] * stretch + tables % stretch, 0)
    info = jnp.stack([row_seq, row_place], axis=2)

    x_all = jnp.concatenate(x_blocks, axis=0)
    normed_all = rms_norm(x_all.astype(F32), norm_one).astype(BF)
    both = dot(normed_all, w_three[:, : 2 * half]).astype(BF).reshape(total, tok, 2 * half)
    rows_one = jnp.einsum(
        "bct,btd->bcd", pick, normed_all.reshape(total, tok, width), preferred_element_type=F32
    ).astype(BF)
    query = dot(rows_one.reshape(total * cap, width), w_three[:, 2 * half :]).astype(BF)
    query = query.reshape(total, cap, half)
    mixed, logs = attend(index, info, query, both)
    partial = dot(mixed.reshape(total * cap, half), out_w).astype(BF)
    partial = partial.reshape(seqs, experts, cap, width)
    attn_out = [
        add_low(partial[0, r], swap_x(partial[1, r])) for r in range(experts)
    ]
    attn_pairs = jnp.concatenate(z_rounds(attn_out, 1), axis=0)

    x_in = x_low.astype(F32)
    normed_one = normed_all[:tok]
    attn_gates = gate_values(normed_one, route_one, attn_idx)
    attn_weight = attn_gates * attn_keep
    attn_mix = weigh(attn_hot, attn_weight)
    mix_high, mix_low = in_two(attn_mix)
    hidden = x_in + dot(mix_high, attn_pairs) + dot(mix_low, attn_pairs)
    normed_two = rms_norm(hidden, norm_two).astype(BF)
    mlp_gates = gate_values(normed_two, route_two, mlp_idx)
    mlp_weight = mlp_gates * mlp_keep
    mlp_mix = weigh(mlp_hot, mlp_weight)

    rows_send = t_dot(mlp_pick, normed_two).astype(BF).reshape(experts, cap, width)
    rows_took = z_rounds([rows_send[r] for r in range(experts)], -1)
    gates_send = jnp.sum(mlp_mix, axis=0).reshape(experts, cap)
    gates_took = z_rounds([gates_send[r : r + 1] for r in range(experts)], -1)
    rows_parts = square_gather(jnp.concatenate(rows_took, axis=0))
    gates_parts = square_gather(jnp.concatenate(gates_took, axis=0))
    rows = jnp.concatenate(rows_parts, axis=0)
    pair_gate = jnp.concatenate(gates_parts, axis=0).reshape(-1, 1)
    everyone = dps * seqs
    gate_pre = dot(rows, gate_w)
    up_pre = dot(rows, up_w)
    sigma = jax.nn.sigmoid(gate_pre)
    activated = gate_pre * sigma
    act = activated * up_pre
    act_low = act.astype(BF)
    gate_partial = jnp.sum(act * act_back, axis=1)
    hidden_grad = act_back * pair_gate
    gate_grad = (hidden_grad * up_pre * sigma * (1.0 + gate_pre * (1.0 - sigma))).astype(BF)
    up_grad = (hidden_grad * activated).astype(BF)
    act_scaled = (act * pair_gate).astype(BF)
    in_partial = (dot_t(gate_grad, gate_w) + dot_t(up_grad, up_w)).astype(BF)
    in_partial = in_partial.reshape(everyone, slots, width)
    in_sum = square_scatter([in_partial[j] for j in range(everyone)])
    gate_partial = gate_partial.reshape(everyone, experts, cap)
    gate_sum = square_scatter([gate_partial[j] for j in range(everyone)])
    out_partial = dot(act_low, down_w).astype(BF).reshape(everyone, slots, width)
    out_sum = square_scatter([out_partial[j] for j in range(everyone)])
    in_pairs = jnp.concatenate(
        z_rounds([in_sum[r * cap : (r + 1) * cap] for r in range(experts)], 1), axis=0
    )
    slot_grad = jnp.concatenate(
        z_rounds([gate_sum[r : r + 1] for r in range(experts)], 1), axis=0
    ).reshape(1, slots)
    out_pairs = jnp.concatenate(
        z_rounds([out_sum[r * cap : (r + 1) * cap] for r in range(experts)], 1), axis=0
    )
    grad_gate = t_dot(rows, gate_grad)
    grad_up = t_dot(rows, up_grad)
    grad_down = t_dot(act_scaled, g_rows)

    mlp_high, mlp_low = in_two(mlp_mix)
    output = hidden + dot(mlp_high, out_pairs) + dot(mlp_low, out_pairs)
    result_out = output.astype(BF).reshape(seq_count, stretch, width)

    mlp_gate_grad = jnp.concatenate(
        [jnp.sum(jnp.where(hot, slot_grad, 0.0), axis=1, keepdims=True) for hot in mlp_hot], axis=1
    )
    router_two_grad, router_two_input = gate_grads(
        normed_two, route_two, mlp_idx, mlp_gates, mlp_gate_grad
    )
    normed_two_grad = dot(mlp_pick, in_pairs) + router_two_input
    residual_grad, norm_two_grad = norm_back(hidden, norm_two, normed_two_grad)
    hidden_total = grad_out + residual_grad

    total_high, total_low = in_two(hidden_total)
    mix_t = attn_mix.T
    row_weight = jnp.sum(attn_mix, axis=0)[:, None]
    dh_send = (
        (t_dot(attn_pick, total_high) + t_dot(attn_pick, total_low)) * row_weight
    ).astype(BF).reshape(experts, cap, width)
    dh_own = z_rounds([dh_send[r] for r in range(experts)], -1)
    dh_other = [swap_x(part) for part in dh_own]
    dh_rows = jnp.concatenate(dh_own + dh_other, axis=0)
    slot_dots = dot_t(total_high, attn_pairs)
    attn_gate_grad = jnp.concatenate(
        [jnp.sum(jnp.where(hot, slot_dots, 0.0), axis=1, keepdims=True) for hot in attn_hot], axis=1
    )
    mixed_grad = dot_t(dh_rows, out_w).astype(BF).reshape(total, cap, half)
    grad_out_w = dp_scatter(
        lambda d: t_dot(
            lax.dynamic_slice_in_dim(
                mixed.reshape(total * cap, half), d * rows_own, rows_own, axis=1
            ),
            dh_rows,
        ).astype(BF)
    )
    q_grad, k_grad, v_grad = attend_back(index, info, query, both, logs, mixed_grad)
    q_slots = jnp.einsum("bct,bch->bth", pick, q_grad, preferred_element_type=F32).astype(BF)
    three_grad = jnp.concatenate([k_grad, v_grad, q_slots], axis=2)
    flat_three = three_grad.reshape(total * tok, 3 * half)
    in_one = dot_t(flat_three, w_three).astype(BF).reshape(total, tok, width)
    one_sum = group_scatter([in_one[j] for j in range(total)])

    feature_rows = rows_own * seqs
    w_grads = dp_scatter(
        lambda d: t_dot(
            lax.dynamic_slice_in_dim(normed_all, d * feature_rows, feature_rows, axis=1),
            flat_three,
        ).astype(BF)
    ).reshape(seqs, rows_own, 3 * half)
    w_mine = lax.dynamic_index_in_dim(w_grads, s_at, 0, keepdims=False)
    w_other = swap_x(lax.dynamic_index_in_dim(w_grads, 1 - s_at, 0, keepdims=False))

    def joined(mine, other):
        pieces = [part.reshape(rows_own, dps, inner // (dps * seqs)) for part in (mine, other)]
        pair = jnp.where(
            s_at == 0, jnp.stack(pieces, axis=2), jnp.stack(pieces[::-1], axis=2)
        )
        return pair.reshape(rows_own, inner)

    grad_query = joined(w_mine[:, 2 * half :], w_other[:, 2 * half :]).astype(F32)
    shared_grads = jnp.stack(
        [joined(w_mine[:, j * half : (j + 1) * half], w_other[:, j * half : (j + 1) * half]) for j in range(2)]
    )
    shared_grads = lax.psum(shared_grads, "expert").astype(F32)

    router_one_grad, router_one_input = gate_grads(
        normed_one, route_one, attn_idx, attn_gates, attn_gate_grad
    )
    normed_one_grad = one_sum.astype(F32) + router_one_input
    input_grad, norm_one_grad = norm_back(x_in, norm_one, normed_one_grad)
    grad_x = (hidden_total + input_grad).astype(BF).reshape(seq_count, stretch, width)

    little = jnp.concatenate(
        [norm_one_grad[None], router_one_grad.T, norm_two_grad[None], router_two_grad.T], axis=0
    )
    little = lax.psum(little, ("dp", "expert", "seq"))
    little = lax.dynamic_slice_in_dim(little, (d_at * seqs + s_at) * rows_own, rows_own, axis=1)
    return (
        result_out,
        grad_x,
        little[0],
        little[1 : 1 + experts].T,
        shared_grads[0],
        shared_grads[1],
        grad_query[None],
        grad_out_w.astype(F32)[None],
        little[1 + experts],
        little[2 + experts :].T,
        grad_gate[None],
        grad_up[None],
        grad_down[None],
    )


def solution(mesh):
    in_specs = (
        P("dp", ("expert", "seq"), None),
        P("dp"),
        P("dp", ("expert", "seq"), None),
        P("dp", ("expert", "seq"), None),
        P("dp", ("expert", "seq"), None),
        P(("dp", "seq")),
        P(("dp", "seq"), None),
        P(("dp", "seq"), None),
        P(("dp", "seq"), None),
        P("expert", ("dp", "seq"), None),
        P("expert", ("dp", "seq"), None),
        P(("dp", "seq")),
        P(("dp", "seq"), None),
        P("expert", None, ("dp", "seq")),
        P("expert", None, ("dp", "seq")),
        P("expert", ("dp", "seq"), None),
        P("dp", ("expert", "seq"), None),
    )
    out_specs = (
        P("dp", ("expert", "seq"), None),
        P("dp", ("expert", "seq"), None),
        P(("dp", "seq")),
        P(("dp", "seq"), None),
        P(("dp", "seq"), None),
        P(("dp", "seq"), None),
        P("expert", ("dp", "seq"), None),
        P("expert", ("dp", "seq"), None),
        P(("dp", "seq")),
        P(("dp", "seq"), None),
        P("expert", None, ("dp", "seq")),
        P("expert", None, ("dp", "seq")),
        P("expert", ("dp", "seq"), None),
    )
    return jax.shard_map(body, mesh=mesh, in_specs=in_specs, out_specs=out_specs, check_vma=False)
```

```python
import functools

import jax
import jax.numpy as jnp
from jax import lax
from jax.experimental import pallas as pl
from jax.experimental.pallas import tpu as pltpu
from jax.sharding import PartitionSpec as P

HEAD = 128
EPS = 1e-06
NEG = -1e30
HIGH = lax.Precision.HIGHEST
BF = jnp.bfloat16
F32 = jnp.float32
LOG2E = 1.4426950408889634


def dot(left, right):
    return jnp.dot(left, right, preferred_element_type=F32)


def dot_t(left, right):
    return lax.dot_general(left, right, (((1,), (1,)), ((), ())), preferred_element_type=F32)


def t_dot(left, right):
    return lax.dot_general(left, right, (((0,), (0,)), ((), ())), preferred_element_type=F32)


def after(value, *others):
    return lax.optimization_barrier((value, others))[0]


def ring(count, shift):
    return [(j, (j + shift) % count) for j in range(count)]


def flip(count, bit):
    return [(j, j ^ bit) for j in range(count)]


def swap_x(value):
    return lax.ppermute(value, "seq", flip(2, 1))


def swap_core(value):
    return lax.ppermute(value, "dp", flip(lax.axis_size("dp"), 1))


def swap_y(value):
    return lax.ppermute(value, "dp", flip(4, 2))


def z_rounds(pieces, sign):
    count = lax.axis_size("expert")
    return [pieces[0]] + [
        lax.ppermute(pieces[r], "expert", ring(count, sign * r)) for r in range(1, count)
    ]


def is_small():
    return lax.axis_size("dp") == 4 and lax.axis_size("expert") == 4


def add_low(*terms):
    total = terms[0].astype(F32)
    for term in terms[1:]:
        total = total + term.astype(F32)
    return total.astype(terms[0].dtype)


def square_gather(piece):
    return lax.all_gather(piece, ("dp", "seq"), axis=0, tiled=True)


def square_scatter(parts):
    return lax.psum_scatter(parts, ("dp", "seq"), scatter_dimension=0, tiled=True)


def group_gather(block):
    count = lax.axis_size("expert")
    if is_small():
        half = block.shape[0] // 2
        up = lax.ppermute(block, "expert", ring(count, -1))
        down = lax.ppermute(block, "expert", ring(count, 1))
        far = jnp.concatenate(
            [
                lax.ppermute(down[:half], "expert", ring(count, 1)),
                lax.ppermute(up[half:], "expert", ring(count, -1)),
            ],
            axis=0,
        )
        own = [block, up, far, down]
        return own + [swap_x(piece) for piece in own]
    e_at, s_at = lax.axis_index("expert"), lax.axis_index("seq")
    every = lax.all_gather(block, ("expert", "seq"), axis=0, tiled=False)
    wanted = [
        (lax.rem(e_at + r, count)) * 2 + lax.rem(s_at + sp, 2)
        for sp in range(2)
        for r in range(count)
    ]
    return [lax.dynamic_index_in_dim(every, at, 0, keepdims=False) for at in wanted]


def group_scatter(own, other):
    count = lax.axis_size("expert")
    if not is_small():
        e_at, s_at = lax.axis_index("expert"), lax.axis_index("seq")
        stacked = jnp.stack(list(own) + list(other))
        spots_of = [
            (lax.rem(s_at + b % 2, 2)) * count + lax.rem(b // 2 - e_at + count, count)
            for b in range(2 * count)
        ]
        ordered = jnp.stack(
            [lax.dynamic_index_in_dim(stacked, at, 0, keepdims=False) for at in spots_of]
        )
        total = lax.psum_scatter(ordered, ("expert", "seq"), scatter_dimension=0, tiled=False)
        return total.astype(F32), []
    half = own[0].shape[0] // 2
    halves = (slice(0, half), slice(half, 2 * half))
    far_took = swap_x(other[2])
    near_took = [swap_x(after(other[1], far_took)), swap_x(after(other[3], far_took))]
    own_took = swap_x(after(other[0], *near_took))
    far = [add_low(own[2][rows], far_took[rows]) for rows in halves]
    far_up = lax.ppermute(far[0], "expert", ring(count, 1))
    far_down = lax.ppermute(far[1], "expert", ring(count, -1))
    up = jnp.concatenate(
        [
            add_low(own[1][halves[0]], near_took[0][halves[0]], far_up),
            add_low(own[1][halves[1]], near_took[0][halves[1]]),
        ],
        axis=0,
    )
    down = jnp.concatenate(
        [
            add_low(own[3][halves[0]], near_took[1][halves[0]]),
            add_low(own[3][halves[1]], near_took[1][halves[1]], far_down),
        ],
        axis=0,
    )
    from_below = lax.ppermute(up, "expert", ring(count, 1))
    from_above = lax.ppermute(down, "expert", ring(count, -1))
    return add_low(own[0].astype(F32), own_took, from_below, from_above), [up, down]


def dp_first(parts):
    at = lax.axis_index("dp")
    core, row = at % 2, at // 2
    split = parts.reshape((2, 2) + parts.shape[1:])
    took = swap_core(lax.dynamic_index_in_dim(split, 1 - core, 1, keepdims=False))

    def of(y):
        mine = lax.dynamic_index_in_dim(split, y, 0, keepdims=False)
        mine = lax.dynamic_index_in_dim(mine, core, 0, keepdims=False)
        return add_low(mine, lax.dynamic_index_in_dim(took, y, 0, keepdims=False))

    return of(row), of(1 - row)


def tiny_scatter(value):
    if lax.axis_size("dp") != 4:
        shape = value.shape[2:]
        flat = lax.psum(value.reshape((-1,) + shape), ("dp", "seq"))
        at = lax.axis_index("dp") * 2 + lax.axis_index("seq")
        return lax.dynamic_index_in_dim(flat, at, 0, keepdims=False)
    at, s_at = lax.axis_index("dp"), lax.axis_index("seq")

    def fold(array, bit, axis, swap):
        mine = lax.dynamic_index_in_dim(array, bit, axis, keepdims=False)
        return mine + swap(lax.dynamic_index_in_dim(array, 1 - bit, axis, keepdims=False))

    value = fold(value, s_at, 1, swap_x)
    value = fold(value.reshape((2, 2) + value.shape[1:]), at % 2, 1, swap_core)
    return fold(value, at // 2, 0, swap_y)


def little_sum(value):
    rows, features = value.shape
    d_count, e_count = lax.axis_size("dp"), lax.axis_size("expert")
    own = features // (2 * d_count)
    held = tiny_scatter(value.reshape(rows, d_count, 2, own).transpose(1, 2, 0, 3))
    if e_count != 4:
        return lax.psum(held, "expert")
    held = held + lax.ppermute(held, "expert", flip(e_count, 1))
    return held + lax.ppermute(held, "expert", flip(e_count, 2))


def route_pairs(routes, order, is_valid, capacity):
    tokens_here, top_count = routes.shape
    pairs = tokens_here * top_count
    target = routes.reshape(pairs)
    second = lax.broadcasted_iota(jnp.int32, routes.shape, 1)
    priority = (order[:, None] * top_count + second).reshape(pairs)
    living = jnp.broadcast_to(is_valid[:, None], routes.shape).reshape(pairs)
    earlier = (
        (target[:, None] == target[None, :])
        & (priority[None, :] < priority[:, None])
        & living[None, :]
    )
    slot_index = jnp.sum(earlier.astype(jnp.int32), axis=1, dtype=jnp.int32)
    kept_pair = living & (slot_index < capacity)
    return (kept_pair.reshape(routes.shape), slot_index.reshape(routes.shape))


def spots(routes, kept, slot_index, experts, capacity):
    away = lax.rem(lax.axis_index("expert") - routes + experts, experts)
    part = capacity // 2
    place = (slot_index // part) * (experts * part) + away * part + slot_index % part
    flat = jnp.where(kept, place, -1)
    return flat


def hots(flat, experts, capacity):
    slots = lax.broadcasted_iota(jnp.int32, (1, experts * capacity), 1)
    return [flat[:, k : k + 1] == slots for k in range(flat.shape[1])]


def weigh(hot, weight):
    return sum(jnp.where(hot[k], weight[:, k : k + 1], 0.0) for k in range(len(hot)))


def in_two(value):
    high = lax.reduce_precision(value, 8, 7)
    return high.astype(BF), (value - high).astype(BF)


def in_columns(value):
    first = lax.reduce_precision(value, 8, 7)
    second = lax.reduce_precision(value - first, 8, 7)
    third = value - first - second
    columns = jnp.concatenate([first, second, third], axis=1).astype(BF)
    return jnp.pad(columns, ((0, 0), (0, 125)))


def rms_norm(values, gain):
    return values * lax.rsqrt(jnp.mean(values * values, axis=-1, keepdims=True) + EPS) * gain


def norm_back(values, gain, grad):
    factor = lax.rsqrt(jnp.mean(values * values, axis=1, keepdims=True) + EPS)
    unit = values * factor
    gain_grad = jnp.sum(grad * unit, axis=0)
    scaled = grad * gain
    return (factor * (scaled - unit * jnp.mean(scaled * unit, axis=1, keepdims=True)), gain_grad)


def gate_values(normed, router, routes):
    logits = dot(normed, router)
    experts = lax.broadcasted_iota(jnp.int32, logits.shape, 1)
    chosen = jnp.concatenate(
        [
            jnp.sum(jnp.where(routes[:, k : k + 1] == experts, logits, 0.0), axis=1, keepdims=True)
            for k in range(routes.shape[1])
        ],
        axis=1,
    )
    top = jnp.max(chosen, axis=1, keepdims=True)
    expo = jnp.exp(chosen - top)
    return expo / jnp.sum(expo, axis=1, keepdims=True)


def gate_grads(normed, router, routes, gates, gate_grad):
    chosen = gates * (gate_grad - jnp.sum(gates * gate_grad, axis=1, keepdims=True))
    experts = lax.broadcasted_iota(jnp.int32, (1, 1, router.shape[1]), 2)
    logit_grad = jnp.sum(jnp.where(routes[:, :, None] == experts, chosen[:, :, None], 0.0), axis=1)
    router_grad = jnp.dot(normed.astype(F32).T, logit_grad, precision=HIGH)
    input_grad = jnp.dot(logit_grad, router.astype(F32).T, precision=HIGH)
    return (router_grad, input_grad)


def tile_bias(info, tile, blocks, tokens):
    stretch = tokens // 2
    row_seq, row_place = info[:, 0:1], info[:, 1:2]
    rows = info.shape[0]
    col = lax.broadcasted_iota(jnp.int32, (rows, tokens), 1)
    same = (col // stretch) == row_seq
    near = jnp.where(same, 0.0, NEG)
    place = lax.rem(col, stretch)
    diagonal = [
        jnp.where(same & (place + (tile * blocks + j) * stretch <= row_place), 0.0, NEG)
        for j in range(blocks)
    ]
    return jnp.concatenate([near] * (tile * blocks) + diagonal, axis=1)


def picked(ref, index, at, count):
    return jnp.concatenate([ref[index[at + j]] for j in range(count)], axis=0)


def attend_kernel(index, info, query, keys, values, mixed, logs, *, blocks):
    head = pl.program_id(0)
    total, capacity, _ = query.shape
    tokens = keys.shape[1]
    rate = HEAD ** (-0.5) * LOG2E
    lane = lax.broadcasted_iota(jnp.int32, (capacity, logs.shape[2]), 1)
    for tile in range(total // blocks):
        first = tile * blocks
        q = picked(query, index, first, blocks)
        k = picked(keys, index, 0, first + blocks)
        v = picked(values, index, 0, first + blocks)
        bias = tile_bias(picked(info, index, first, blocks), tile, blocks, tokens)
        scores = dot_t(q, k) + bias
        top = jnp.max(scores, axis=1, keepdims=True)
        expo = jnp.exp2((scores - top) * rate)
        norm = jnp.sum(expo, axis=1, keepdims=True)
        out = (dot(expo.astype(BF), v) / norm).astype(BF)
        log = top * rate + jnp.log2(norm)
        for j in range(blocks):
            rows = slice(j * capacity, (j + 1) * capacity)
            mixed[index[first + j]] = out[rows]
            held = logs[index[first + j]]
            logs[index[first + j]] = jnp.where(lane == head, log[rows], held)


def attend_back_kernel(
    index, info, query, keys, values, logs, mixed_grad, q_grad, k_grad, v_grad, k_sum, v_sum, *, blocks
):
    head = pl.program_id(0)
    total, capacity, _ = query.shape
    tokens = keys.shape[1]
    scale = HEAD ** (-0.5)
    rate = scale * LOG2E
    k_sum[...] = jnp.zeros_like(k_sum)
    v_sum[...] = jnp.zeros_like(v_sum)
    for tile in range(total // blocks):
        first = tile * blocks
        q = picked(query, index, first, blocks)
        k = picked(keys, index, 0, first + blocks)
        v = picked(values, index, 0, first + blocks)
        g = picked(mixed_grad, index, first, blocks)
        log = picked(logs, index, first, blocks)
        lane = lax.broadcasted_iota(jnp.int32, log.shape, 1)
        log = jnp.sum(jnp.where(lane == head, log, 0.0), axis=1, keepdims=True)
        bias = tile_bias(picked(info, index, first, blocks), tile, blocks, tokens)
        probs = jnp.exp2((dot_t(q, k) + bias) * rate - log)
        prob_grad = dot_t(g, v)
        center = jnp.sum(probs * prob_grad, axis=1, keepdims=True)
        score_grad = (probs * (prob_grad - center)).astype(BF)
        out = (dot(score_grad, k) * scale).astype(BF)
        for j in range(blocks):
            q_grad[index[first + j]] = out[j * capacity : (j + 1) * capacity]
        k_part = t_dot(score_grad, q)
        v_part = t_dot(probs.astype(BF), g)
        for j in range(first + blocks):
            rows = slice(j * tokens, (j + 1) * tokens)
            k_sum[index[j]] += k_part[rows]
            v_sum[index[j]] += v_part[rows]
    k_grad[...] = (k_sum[...] * scale).astype(BF)
    v_grad[...] = v_sum[...].astype(BF)


def head_spec(shape, skip=0):
    return pl.BlockSpec((shape[0], shape[1], HEAD), lambda h, index: (0, 0, h + skip))


def flat_spec(shape):
    return pl.BlockSpec(shape, lambda h, index: (0, 0, 0))


def attend(index, info, query, both):
    total, capacity, width = query.shape
    tokens = both.shape[1]
    heads = width // HEAD
    blocks = max(1, 256 // capacity)
    log_shape = (total, capacity, 128)
    flops = 4 * total * capacity * total * tokens * width
    return pl.pallas_call(
        functools.partial(attend_kernel, blocks=blocks),
        grid_spec=pltpu.PrefetchScalarGridSpec(
            num_scalar_prefetch=1,
            grid=(heads,),
            in_specs=[
                flat_spec(info.shape),
                head_spec(query.shape),
                head_spec(both.shape),
                head_spec(both.shape, heads),
            ],
            out_specs=[head_spec(query.shape), flat_spec(log_shape)],
        ),
        out_shape=[
            jax.ShapeDtypeStruct(query.shape, BF),
            jax.ShapeDtypeStruct(log_shape, F32),
        ],
        compiler_params=pltpu.CompilerParams(vmem_limit_bytes=50 << 20),
        cost_estimate=pl.CostEstimate(
            flops=flops, bytes_accessed=16 << 20, transcendentals=flops // 512
        ),
    )(index, info, query, both, both)


def attend_back(index, info, query, both, logs, mixed_grad):
    total, capacity, width = query.shape
    tokens = both.shape[1]
    heads = width // HEAD
    blocks = max(1, 256 // capacity)
    flops = 10 * total * capacity * total * tokens * width
    return pl.pallas_call(
        functools.partial(attend_back_kernel, blocks=blocks),
        grid_spec=pltpu.PrefetchScalarGridSpec(
            num_scalar_prefetch=1,
            grid=(heads,),
            in_specs=[
                flat_spec(info.shape),
                head_spec(query.shape),
                head_spec(both.shape),
                head_spec(both.shape, heads),
                flat_spec(logs.shape),
                head_spec(mixed_grad.shape),
            ],
            out_specs=[head_spec(query.shape)] + [head_spec((total, tokens, width))] * 2,
            scratch_shapes=[
                pltpu.VMEM((total, tokens, HEAD), F32),
                pltpu.VMEM((total, tokens, HEAD), F32),
            ],
        ),
        out_shape=[
            jax.ShapeDtypeStruct(query.shape, BF),
        ]
        + [jax.ShapeDtypeStruct((total, tokens, width), BF)] * 2,
        compiler_params=pltpu.CompilerParams(vmem_limit_bytes=50 << 20),
        cost_estimate=pl.CostEstimate(
            flops=flops, bytes_accessed=32 << 20, transcendentals=flops // 1280
        ),
    )(index, info, query, both, both, logs, mixed_grad)


def held_spec(shape):
    return pl.BlockSpec(
        shape, lambda *at: (0,) * len(shape), pipeline_mode=pl.Buffered(buffer_count=1)
    )


def held_out(shape):
    return pl.BlockSpec(shape, lambda *at: (0,) * len(shape))


def step_spec(shape, skip=0):
    zeros = (0,) * (len(shape) - 1)
    return pl.BlockSpec(shape, lambda step, *rest: (step + skip,) + zeros)


def fetch(step, refs, target):
    for piece, ref in enumerate(refs):

        @pl.when(step == piece)
        def _(ref=ref):
            target[...] = ref[...]


def halves_kernel(place, *refs, count):
    small, keep, give = refs[2 * count :]
    step = pl.program_id(0)
    size = refs[0].shape[1]
    blocks = (keep.shape[1] - 128) // (count * size)
    for j in range(count):
        at = pl.ds(pl.multiple_of((j * blocks + step) * size, 128), size)
        keep[:, at] = refs[2 * j][...]
        give[:, at] = refs[2 * j + 1][...]
    keep[:, keep.shape[1] - 128 :] = small[...]
    give[:, keep.shape[1] - 128 :] = small[...]


def weight_halves(s_at, weights, small, blocks):
    rows, columns = weights[0].shape
    size = columns // (2 * blocks)
    count = len(weights)
    shape = (rows, count * blocks * size + 128)
    specs = []
    for _ in weights:
        specs.append(pl.BlockSpec((rows, size), lambda step, place: (0, 2 * step + place[0])))
        specs.append(pl.BlockSpec((rows, size), lambda step, place: (0, 2 * step + 1 - place[0])))
    return pl.pallas_call(
        functools.partial(halves_kernel, count=count),
        grid_spec=pltpu.PrefetchScalarGridSpec(
            num_scalar_prefetch=1,
            grid=(blocks,),
            in_specs=specs + [pl.BlockSpec((rows, 128), lambda step, place: (0, 0))],
            out_specs=[pl.BlockSpec(shape, lambda step, place: (0, 0))] * 2,
        ),
        out_shape=[jax.ShapeDtypeStruct(shape, BF)] * 2,
        compiler_params=pltpu.CompilerParams(vmem_limit_bytes=24 << 20),
        cost_estimate=pl.CostEstimate(flops=0, bytes_accessed=8 << 20, transcendentals=0),
    )(s_at[None], *[w for weight in weights for w in (weight, weight)], small)


def join_kernel(place, *refs, count, blocks):
    mine, other, outs = refs[:count], refs[count : 2 * count], refs[2 * count :]
    size = mine[0].shape[1] // blocks
    for j in range(count):
        for block in range(blocks):
            for seq, ref in enumerate((mine[j], other[j])):
                found = ref[:, block * size : (block + 1) * size].astype(outs[j].dtype)
                outs[j][:, block_at(place, block, seq, size)] = found


def join_columns(s_at, mine, other, blocks, dtype):
    rows, half = mine[0].shape
    count = len(mine)
    return pl.pallas_call(
        functools.partial(join_kernel, count=count, blocks=blocks),
        grid_spec=pltpu.PrefetchScalarGridSpec(
            num_scalar_prefetch=1,
            grid=(1,),
            in_specs=[held_spec((rows, half))] * 2 * count,
            out_specs=[held_out((rows, 2 * half))] * count,
        ),
        out_shape=[jax.ShapeDtypeStruct((rows, 2 * half), dtype)] * count,
        compiler_params=pltpu.CompilerParams(vmem_limit_bytes=40 << 20),
        cost_estimate=pl.CostEstimate(flops=0, bytes_accessed=4 << 20, transcendentals=0),
    )(s_at[None], *mine, *other)


def block_at(place, block, other, size):
    seq = 1 - place[0] if other else place[0]
    return pl.ds(pl.multiple_of((2 * block + seq) * size, 128), size)


def project_kernel(place, gain, pick, keep, took, *refs, x_count, dps):
    normed_out, both_out, query_out, held, low, rows = refs[x_count:]
    double, half = both_out.shape[2], query_out.shape[2]
    blocks, tok, width = normed_out.shape
    cap = query_out.shape[1]
    size = width // (2 * dps)
    step = pl.program_id(0)
    for j in range(blocks):
        fetch(step * blocks + j, refs[:x_count], held.at[pl.ds(j * tok, tok)])
    x = held[:, :width].astype(F32)
    factor = lax.rsqrt(jnp.mean(x * x, axis=1, keepdims=True) + EPS)
    normed = (x * factor * gain[...]).astype(BF)
    low[...] = normed
    for j in range(blocks):
        mine = normed[j * tok : (j + 1) * tok]
        normed_out[j] = mine
        rows[j * cap : (j + 1) * cap] = dot(pick[j], mine).astype(BF)
    both = query = None
    for other, weights in enumerate((keep, took)):
        left = jnp.concatenate([low[:, block_at(place, d, other, size)] for d in range(dps)], axis=1)
        right = jnp.concatenate([rows[:, block_at(place, d, other, size)] for d in range(dps)], axis=1)
        kv_part = dot(left, weights[:, :double])
        q_part = dot(right, weights[:, double : double + half])
        both = kv_part if both is None else both + kv_part
        query = q_part if query is None else query + q_part
    both, query = both.astype(BF), query.astype(BF)
    for j in range(blocks):
        both_out[j] = both[j * tok : (j + 1) * tok]
        query_out[j] = query[j * cap : (j + 1) * cap]


def project(s_at, gain, pick, x_parts, keep, took, half, dps):
    total, cap, tok = pick.shape
    width = gain.shape[1]
    blocks = 2
    flops = 2 * total * (tok * width * 2 * half + cap * width * half)
    return pl.pallas_call(
        functools.partial(project_kernel, x_count=len(x_parts), dps=dps),
        grid_spec=pltpu.PrefetchScalarGridSpec(
            num_scalar_prefetch=1,
            grid=(total // blocks,),
            in_specs=[
                held_spec((1, width)),
                step_spec((blocks, cap, tok)),
                held_spec(keep.shape),
                held_spec(took.shape),
            ]
            + [held_spec(part.shape) for part in x_parts],
            out_specs=[
                step_spec((blocks, tok, width)),
                step_spec((blocks, tok, 2 * half)),
                step_spec((blocks, cap, half)),
            ],
            scratch_shapes=[
                pltpu.VMEM((blocks * tok, x_parts[0].shape[1]), BF),
                pltpu.VMEM((blocks * tok, width), BF),
                pltpu.VMEM((blocks * cap, width), BF),
            ],
        ),
        out_shape=[
            jax.ShapeDtypeStruct((total, tok, width), BF),
            jax.ShapeDtypeStruct((total, tok, 2 * half), BF),
            jax.ShapeDtypeStruct((total, cap, half), BF),
        ],
        compiler_params=pltpu.CompilerParams(vmem_limit_bytes=58 << 20),
        cost_estimate=pl.CostEstimate(flops=flops, bytes_accessed=40 << 20, transcendentals=0),
    )(s_at[None], gain, pick, keep, took, *x_parts)


def back_kernel(place, k_grad, v_grad, slots, keep, took, *refs, dps):
    outs, held = refs[:-1], refs[-1]
    blocks, tok, half = slots.shape
    size = held.shape[1] // (2 * dps)
    q_rows = jnp.concatenate([slots[j] for j in range(blocks)], axis=0)
    k_rows = jnp.concatenate([k_grad[j] for j in range(blocks)], axis=0)
    v_rows = jnp.concatenate([v_grad[j] for j in range(blocks)], axis=0)
    for other, weights in enumerate((keep, took)):
        part = (
            dot_t(k_rows, weights[:, :half])
            + dot_t(v_rows, weights[:, half : 2 * half])
            + dot_t(q_rows, weights[:, 2 * half : 3 * half])
        ).astype(BF)
        for d in range(dps):
            held[:, block_at(place, d, other, size)] = part[:, d * size : (d + 1) * size]
    for j, out in enumerate(outs):

        @pl.when(pl.program_id(0) == j // blocks)
        def _(out=out, at=j % blocks * tok):
            out[...] = held[at : at + tok]


def project_back(s_at, both_grad, slots, keep, took, first, count, dps):
    total, tok, half = slots.shape
    width = 2 * keep.shape[0]
    blocks = 2
    skip = first // blocks
    whole = pl.BlockSpec((tok, width), lambda *at: (0, 0))
    return pl.pallas_call(
        functools.partial(back_kernel, dps=dps),
        grid_spec=pltpu.PrefetchScalarGridSpec(
            num_scalar_prefetch=1,
            grid=(count // blocks,),
            in_specs=[
                step_spec((blocks, tok, half), skip),
                step_spec((blocks, tok, half), skip),
                step_spec((blocks, tok, half), skip),
                held_spec(keep.shape),
                held_spec(took.shape),
            ],
            out_specs=[whole] * count,
            scratch_shapes=[pltpu.VMEM((blocks * tok, width), BF)],
        ),
        out_shape=[jax.ShapeDtypeStruct((tok, width), BF)] * count,
        compiler_params=pltpu.CompilerParams(vmem_limit_bytes=58 << 20),
        cost_estimate=pl.CostEstimate(
            flops=6 * count * tok * width * half, bytes_accessed=24 << 20, transcendentals=0
        ),
    )(s_at[None], *both_grad, slots, keep, took)


def expert_kernel(
    rows, act_back, gate_wt, up_wt, in_out, gate_out, up_out, scaled_out, act_out, dots_out
):
    width = gate_wt.shape[1]
    x = rows[:, :width]
    tail = rows[:, width : width + 128].astype(F32)
    weight = tail[:, 0:1] + tail[:, 1:2] + tail[:, 2:3]
    gate_pre = dot_t(x, gate_wt[...])
    up_pre = dot_t(x, up_wt[...])
    sigma = jax.nn.sigmoid(gate_pre)
    activated = gate_pre * sigma
    act = activated * up_pre
    back = act_back[...]
    dots_out[...] = jnp.sum(act * back, axis=1, keepdims=True)
    back = back * weight
    gate_grad = (back * up_pre * sigma * (1.0 + gate_pre * (1.0 - sigma))).astype(BF)
    up_grad = (back * activated).astype(BF)
    gate_out[...] = gate_grad
    up_out[...] = up_grad
    scaled_out[...] = (act * weight).astype(BF)
    act_out[...] = act.astype(BF)
    in_out[...] = (dot(gate_grad, gate_wt[...]) + dot(up_grad, up_wt[...])).astype(BF)


def expert_mlp(rows, act_back, gate_wt, up_wt):
    inner, width = gate_wt.shape
    every = rows.shape[0]
    size = min(512, every)
    return pl.pallas_call(
        expert_kernel,
        grid=(every // size,),
        in_specs=[step_spec((size, rows.shape[1])), step_spec((size, inner))]
        + [held_spec(w.shape) for w in (gate_wt, up_wt)],
        out_specs=[step_spec((size, width))]
        + [step_spec((size, inner))] * 4
        + [step_spec((size, 1))],
        out_shape=[jax.ShapeDtypeStruct((every, width), BF)]
        + [jax.ShapeDtypeStruct((every, inner), BF)] * 4
        + [jax.ShapeDtypeStruct((every, 1), F32)],
        compiler_params=pltpu.CompilerParams(vmem_limit_bytes=58 << 20),
        cost_estimate=pl.CostEstimate(
            flops=8 * every * width * inner,
            bytes_accessed=60 << 20,
            transcendentals=2 * every * inner,
        ),
    )(rows, act_back, gate_wt, up_wt)


def lanes_of(value):
    return lax.broadcasted_iota(jnp.int32, (value.shape[0], 128), 1)


def three_low(value):
    first = value.astype(BF)
    rest = value - first.astype(F32)
    second = rest.astype(BF)
    return first, second, (rest - second.astype(F32)).astype(BF)


def hot_of(flat, slots):
    ids = lax.broadcasted_iota(jnp.int32, (flat.shape[0], slots), 1)
    return [flat[:, k : k + 1] == ids for k in range(flat.shape[1])]


def combine_kernel(x, mix_high, mix_low, gain, router, routes, flat, *refs, count):
    pairs = jnp.concatenate([ref[...] for ref in refs[:count]], axis=0)
    hidden_out, normed_out, gates_out, mix_out = refs[count : count + 4]
    sends = refs[count + 4 :]
    part, width = refs[0].shape
    hidden = x[...].astype(F32) + dot(mix_high[...], pairs) + dot(mix_low[...], pairs)
    hidden_out[...] = hidden
    factor = lax.rsqrt(jnp.mean(hidden * hidden, axis=1, keepdims=True) + EPS)
    normed = (hidden * factor * gain[...]).astype(BF)
    normed_out[...] = normed
    logits = dot(normed, router[...])
    lanes = lanes_of(logits)
    ids, places = routes[...], flat[...]
    one, two = [
        jnp.sum(jnp.where(lanes == ids[:, k : k + 1], logits, 0.0), axis=1, keepdims=True)
        for k in range(2)
    ]
    top = jnp.maximum(one, two)
    one, two = jnp.exp(one - top), jnp.exp(two - top)
    gates = [one / (one + two), two / (one + two)]
    gates_out[...] = jnp.where(lanes == 0, gates[0], jnp.where(lanes == 1, gates[1], 0.0))
    hot = hot_of(places, part * count)
    mix = jnp.where(hot[0], gates[0], 0.0) + jnp.where(hot[1], gates[1], 0.0)
    mix_out[...] = mix
    pick = jnp.where(hot[0] | hot[1], 1.0, 0.0).astype(BF)
    rows = t_dot(pick, normed).astype(BF)
    ones = jnp.ones((hidden.shape[0], 128), BF)
    columns = [t_dot(term, ones) for term in three_low(mix)]
    lanes = lanes_of(columns[0])
    tail = jnp.where(lanes == 0, columns[0], 0.0)
    for j in (1, 2):
        tail = tail + jnp.where(lanes == j, columns[j], 0.0)
    tail = tail.astype(BF)
    for j, send in enumerate(sends):
        at = slice(j * part, (j + 1) * part)
        send[:, :width] = rows[at]
        send[:, width:] = tail[at]


def combine(x, mix_high, mix_low, gain, router, routes, flat, pairs):
    tok, width = x.shape
    part = pairs[0].shape[0]
    count = len(pairs)
    operands = (x, mix_high, mix_low, gain, router, routes, flat, *pairs)
    return pl.pallas_call(
        functools.partial(combine_kernel, count=count),
        grid=(1,),
        in_specs=[held_spec(operand.shape) for operand in operands],
        out_specs=[held_out((tok, width))] * 2
        + [held_out((tok, 128)), held_out((tok, part * count))]
        + [held_out((part, width + 128))] * count,
        out_shape=[
            jax.ShapeDtypeStruct((tok, width), F32),
            jax.ShapeDtypeStruct((tok, width), BF),
            jax.ShapeDtypeStruct((tok, 128), F32),
            jax.ShapeDtypeStruct((tok, part * count), F32),
        ]
        + [jax.ShapeDtypeStruct((part, width + 128), BF)] * count,
        compiler_params=pltpu.CompilerParams(vmem_limit_bytes=40 << 20),
        cost_estimate=pl.CostEstimate(
            flops=6 * tok * part * count * width, bytes_accessed=10 << 20, transcendentals=0
        ),
    )(*operands)


def between_kernel(
    hidden, normed, grad_out, gain, router, routes, flat, gates, attn_pick, weight, *refs, count
):
    parts = refs[:count]
    total_out, high_out, gain_out, logit_out = refs[count : count + 4]
    sends = refs[count + 4 :]
    part, width = sends[0].shape
    rows = jnp.concatenate([ref[:, :width] for ref in parts], axis=0)
    tail = jnp.concatenate([ref[:, width:] for ref in parts], axis=0)
    hot = hot_of(flat[...], part * count)
    ids, held = routes[...], gates[...]
    lanes = lanes_of(held)
    slot_grad = []
    for k in range(2):
        found = dot(jnp.where(hot[k], 1.0, 0.0).astype(BF), tail)
        slot_grad.append(jnp.sum(jnp.where(lanes < 3, found, 0.0), axis=1, keepdims=True))
    gate = [held[:, 0:1], held[:, 1:2]]
    center = gate[0] * slot_grad[0] + gate[1] * slot_grad[1]
    logit_grad = jnp.zeros(held.shape, F32)
    for k in range(2):
        chosen = gate[k] * (slot_grad[k] - center)
        logit_grad = logit_grad + jnp.where(lanes == ids[:, k : k + 1], chosen, 0.0)
    logit_out[...] = logit_grad
    pick = jnp.where(hot[0] | hot[1], 1.0, 0.0).astype(BF)
    grad = dot(pick, rows)
    for term in three_low(logit_grad):
        grad = grad + dot_t(term, router[...])
    values = hidden[...]
    factor = lax.rsqrt(jnp.mean(values * values, axis=1, keepdims=True) + EPS)
    unit = values * factor
    gain_out[...] = jnp.sum(grad * unit, axis=0, keepdims=True)
    scaled = grad * gain[...]
    back = factor * (scaled - unit * jnp.mean(scaled * unit, axis=1, keepdims=True))
    total = grad_out[...].astype(F32) + back
    total_out[...] = total
    high = total.astype(BF)
    low = (total - high.astype(F32)).astype(BF)
    high_out[...] = high
    picked_rows = t_dot(attn_pick[...], high) + t_dot(attn_pick[...], low)
    picked_rows = (picked_rows * weight[...]).astype(BF)
    for j, send in enumerate(sends):
        send[...] = picked_rows[j * part : (j + 1) * part]


def between(hidden, normed, grad_out, gain, router, routes, flat, gates, attn_pick, weight, parts):
    tok, width = hidden.shape
    part = parts[0].shape[0]
    count = len(parts)
    operands = (
        hidden, normed, grad_out, gain, router, routes, flat, gates, attn_pick, weight, *parts
    )
    return pl.pallas_call(
        functools.partial(between_kernel, count=count),
        grid=(1,),
        in_specs=[held_spec(operand.shape) for operand in operands],
        out_specs=[held_out((tok, width))] * 2
        + [held_out((1, width)), held_out((tok, 128))]
        + [held_out((part, width))] * count,
        out_shape=[
            jax.ShapeDtypeStruct((tok, width), F32),
            jax.ShapeDtypeStruct((tok, width), BF),
            jax.ShapeDtypeStruct((1, width), F32),
            jax.ShapeDtypeStruct((tok, 128), F32),
        ]
        + [jax.ShapeDtypeStruct((part, width), BF)] * count,
        compiler_params=pltpu.CompilerParams(vmem_limit_bytes=40 << 20),
        cost_estimate=pl.CostEstimate(
            flops=6 * tok * part * count * width, bytes_accessed=12 << 20, transcendentals=0
        ),
    )(*operands)


def act_back_kernel(grads, down_w, out):
    out[...] = dot_t(grads[...], down_w[...])


def expert_act_back(grads, down_w):
    every, width = grads.shape
    inner = down_w.shape[0]
    size = min(512, every)
    return pl.pallas_call(
        act_back_kernel,
        grid=(every // size,),
        in_specs=[step_spec((size, width)), held_spec(down_w.shape)],
        out_specs=step_spec((size, inner)),
        out_shape=jax.ShapeDtypeStruct((every, inner), F32),
        compiler_params=pltpu.CompilerParams(vmem_limit_bytes=40 << 20),
        cost_estimate=pl.CostEstimate(
            flops=2 * every * width * inner, bytes_accessed=18 << 20, transcendentals=0
        ),
    )(grads, down_w)


def body(
    inputs,
    lengths,
    attn_routes,
    mlp_routes,
    slot_order,
    gain_attn,
    router_attn,
    w_key,
    w_value,
    w_query,
    w_out,
    gain_mlp,
    router_mlp,
    w_gate,
    w_up,
    w_down,
    d_out,
):
    seq_count, stretch, width = inputs.shape
    tok = seq_count * stretch
    top_count = attn_routes.shape[2]
    experts = router_attn.shape[1]
    cap = top_count * tok // experts
    slots = experts * cap
    dps, seqs = lax.axis_size("dp"), lax.axis_size("seq")
    total = experts * seqs
    e_at, s_at = lax.axis_index("expert"), lax.axis_index("seq")
    block = e_at * seqs + s_at
    rows_own = w_key.shape[0]
    inner = w_key.shape[1]
    half = inner // seqs

    absolute = lax.broadcasted_iota(jnp.int32, (total,), 0)
    index = lax.rem(absolute % seqs - s_at + seqs, seqs) * experts + lax.rem(
        absolute // seqs - e_at + experts, experts
    )
    block_of = lax.rem(absolute % experts + e_at, experts) * seqs + lax.rem(
        absolute // experts + s_at, seqs
    )

    x_low = inputs.reshape(tok, width)
    attn_idx = attn_routes.reshape(tok, top_count)
    mlp_idx = mlp_routes.reshape(tok, top_count)
    order = slot_order.reshape(tok)
    marks = jnp.concatenate([attn_idx, order[:, None]], axis=1).astype(BF)
    marks = jnp.pad(marks, ((0, 0), (0, 128 - marks.shape[1])))
    x_marked = jnp.concatenate([x_low, marks], axis=1)

    small = [gain_attn[:, None], router_attn, gain_mlp[:, None], router_mlp]
    small.append(jnp.zeros((rows_own, 128 - 2 - 2 * experts), BF))
    w_keep, w_give = weight_halves(
        s_at, (w_key, w_value, w_query[0]), jnp.concatenate(small, axis=1), dps
    )
    x_parts = group_gather(x_marked)
    w_keep = lax.all_gather(w_keep, "dp", axis=0, tiled=True)
    w_took = lax.all_gather(swap_x(w_give), "dp", axis=0, tiled=True)
    out_w = lax.all_gather(w_out[0], "dp", axis=0, tiled=True)

    def feature_rows(first, last):
        pair = [w[:, 3 * half + first : 3 * half + last] for w in (w_keep, w_took)]
        pair = [w.reshape(dps, rows_own, last - first) for w in pair]
        pair = jnp.where(s_at == 0, jnp.stack(pair, axis=1), jnp.stack(pair[::-1], axis=1))
        return pair.reshape(width, last - first)

    small = feature_rows(0, 2 + 2 * experts)
    norm_one = small[:, 0].astype(F32)[None]
    route_one = small[:, 1 : 1 + experts]
    norm_two = small[:, 1 + experts].astype(F32)[None]
    route_two = jnp.pad(small[:, 2 + experts :], ((0, 0), (0, 128 - experts)))

    column = lax.broadcasted_iota(jnp.int32, (seq_count, stretch), 1)
    is_valid = (block * stretch + column < lengths[:, None]).reshape(tok)
    attn_kept, attn_slot = route_pairs(attn_idx, order, is_valid, cap)
    mlp_kept, mlp_slot = route_pairs(mlp_idx, order, is_valid, cap)
    attn_keep = attn_kept.astype(F32)
    attn_flat = spots(attn_idx, attn_kept, attn_slot, experts, cap)
    mlp_flat = spots(mlp_idx, mlp_kept, mlp_slot, experts, cap)
    attn_hot = hots(attn_flat, experts, cap)
    mlp_hot = hots(mlp_flat, experts, cap)
    attn_pick = (attn_hot[0] | attn_hot[1]).astype(BF)
    mlp_pick = (mlp_hot[0] | mlp_hot[1]).astype(BF)

    part = cap // 2
    chunk = experts * part
    chunks = [slice(c * chunk, (c + 1) * chunk) for c in range(2)]

    def pieces_of(array):
        return [array[r * part : (r + 1) * part] for r in range(experts)]

    g_low = d_out.reshape(tok, width)
    gate_wt, up_wt, down_w = w_gate[0].T, w_up[0].T, w_down[0]
    found = jnp.stack(
        [rows[:, width : width + 3] for rows in x_parts]
    ).astype(jnp.int32)
    tok_ids = lax.broadcasted_iota(jnp.int32, (1, tok), 1)
    places = block_of[:, None] * stretch + tok_ids % stretch
    limits = jnp.where(tok_ids // stretch == 0, lengths[0], lengths[1])
    mine = ((found[:, :, 0] == e_at) | (found[:, :, 1] == e_at)) & (places < limits)
    ranks = found[:, :, 2]
    ahead = mine[:, None, :] & (ranks[:, None, :] < ranks[:, :, None])
    ahead = jnp.sum(ahead.astype(jnp.int32), axis=2, dtype=jnp.int32)
    ahead = jnp.where(mine, ahead, cap)
    chosen = ahead[:, None, :] == lax.broadcasted_iota(jnp.int32, (1, cap, 1), 1)
    pick = chosen.astype(BF)
    row_seq = jnp.sum(jnp.where(chosen, (tok_ids // stretch)[:, None], 0), axis=2, dtype=jnp.int32)
    row_place = jnp.sum(jnp.where(chosen, places[:, None], 0), axis=2, dtype=jnp.int32)
    info = jnp.stack([row_seq, row_place], axis=2)

    normed_all, both, query = project(s_at, norm_one, pick, x_parts, w_keep, w_took, half, dps)
    g_send = t_dot(mlp_pick, g_low).astype(BF).reshape(2, experts, part, width)
    g_send = after(g_send, x_parts)
    g_took = z_rounds([g_send[:, r] for r in range(experts)], -1)
    g_took = jnp.stack(after(g_took, query), axis=1)
    g_rows = [square_gather(g_took[c].reshape(chunk, width)) for c in range(2)]
    act_back = [expert_act_back(rows, down_w) for rows in g_rows]
    mixed, logs = attend(index, info, query, both)
    mixed_parts = mixed.reshape(seqs, experts, 2, part, half)
    attn_pairs, took_before = [], []
    for c in range(2):
        partial = dot(mixed_parts[:, :, c].reshape(seqs * chunk, half), out_w).astype(BF)
        took = swap_x(after(partial[chunk:], *took_before))
        took_before = [took]
        attn_out = [
            add_low(mine, other) for mine, other in zip(pieces_of(partial[:chunk]), pieces_of(took))
        ]
        attn_pairs += z_rounds(attn_out, 1)
    attn_pairs, act_back = lax.optimization_barrier((attn_pairs, act_back))

    x_in = x_low.astype(F32)
    normed_one = normed_all[0]
    attn_gates = gate_values(normed_one, route_one, attn_idx)
    attn_weight = attn_gates * attn_keep
    attn_mix = weigh(attn_hot, attn_weight)
    mix_high, mix_low = in_two(attn_mix)
    hidden, normed_two, mlp_gates, mlp_mix, *rows_sends = combine(
        x_low, mix_high, mix_low, norm_two, route_two, mlp_idx, mlp_flat, attn_pairs
    )

    expert_out, rows_before = [], []
    for c in range(2):
        rows_send = after(rows_sends[c * experts : (c + 1) * experts], *rows_before)
        rows_took = jnp.concatenate(z_rounds(rows_send, -1), axis=0)
        rows_before = [rows_took]
        rows = square_gather(rows_took)
        expert_out.append(
            (rows,) + tuple(expert_mlp(rows, act_back[c], gate_wt, up_wt))
        )
    in_pairs, out_parts = [], []
    grads = []
    for c in range(2):
        found = expert_out[c]
        grads.append(
            [
                t_dot(found[0][:, :width], found[2]),
                t_dot(found[0][:, :width], found[3]),
                t_dot(found[4], g_rows[c]),
            ]
        )
        if c == 1:
            grads = [low + high for low, high in zip(*grads)]
        in_sum = square_scatter(found[1])
        out_parts.append(dot(after(found[5], expert_out[1][1]), down_w).astype(BF))
        if c == 1:
            in_sum, grads, out_parts = lax.optimization_barrier((in_sum, grads, out_parts))
        dots = tiny_scatter(found[6].reshape(dps, seqs, chunk))
        in_sum = jnp.concatenate([in_sum, in_columns(dots[:, None])], axis=1)
        in_pairs += z_rounds(pieces_of(in_sum), 1)
    grad_gate, grad_up, grad_down = grads

    attn_columns = jnp.sum(attn_mix, axis=0)[:, None]
    hidden_total, total_high, norm_two_grad, logit_grad, *dh_sends = between(
        hidden, normed_two, g_low, norm_two, route_two, mlp_idx, mlp_flat, mlp_gates, attn_pick,
        attn_columns, in_pairs,
    )
    router_two_grad = jnp.dot(
        normed_two.astype(F32).T, logit_grad[:, :experts], precision=HIGH
    )

    dh_own, dh_other = [], []
    for c in range(2):
        dh_send = after(dh_sends[c * experts : (c + 1) * experts], *dh_own)
        dh_own.append(jnp.concatenate(z_rounds(dh_send, -1), axis=0))
        dh_other.append(swap_x(after(dh_own[-1], *dh_other)))
    dh_rows = jnp.stack([jnp.stack(dh_own), jnp.stack(dh_other)])
    dh_rows = dh_rows.reshape(seqs, 2, experts, part, width).transpose(0, 2, 1, 3, 4)
    dh_rows = dh_rows.reshape(total * cap, width)

    out_sums = [
        square_scatter(out_parts[0]),
        square_scatter(after(out_parts[1], dh_rows)),
    ]

    slot_dots = dot_t(total_high, jnp.concatenate(attn_pairs, axis=0))
    attn_gate_grad = jnp.concatenate(
        [jnp.sum(jnp.where(hot, slot_dots, 0.0), axis=1, keepdims=True) for hot in attn_hot], axis=1
    )
    mixed_grad = dot_t(dh_rows, out_w).astype(BF).reshape(total, cap, half)
    grad_out_w = t_dot(mixed.reshape(total * cap, half), dh_rows).astype(BF)
    mixed_grad, grad_out_w = lax.optimization_barrier((mixed_grad, grad_out_w))
    mixed_grad = after(mixed_grad, out_sums[0])
    grad_out_w = lax.psum_scatter(grad_out_w, "dp", scatter_dimension=0, tiled=True)
    q_grad, *both_grad = attend_back(index, info, query, both, logs, mixed_grad)

    flat_normed = normed_all.reshape(total * tok, width)
    both_dots = [
        t_dot(flat_normed, array.reshape(total * tok, half))
        .astype(BF)
        .reshape(dps, seqs * rows_own, half)
        for array in both_grad
    ]
    q_grad, both_grad = after((q_grad, both_grad), out_sums[1])
    if is_small():
        firsts = [dp_first(dots) for dots in both_dots]
        q_grad, both_grad = after((q_grad, both_grad), [far for _, far in firsts])
    q_slots = jnp.einsum("bct,bch->bth", pick, q_grad, preferred_element_type=F32).astype(BF)
    query_grads = t_dot(flat_normed, q_slots.reshape(total * tok, half)).astype(BF)
    q_slots = after(q_slots, query_grads)
    query_grads = lax.psum_scatter(query_grads, "dp", scatter_dimension=0, tiled=True)

    in_other = project_back(s_at, both_grad, q_slots, w_keep, w_took, experts, experts, dps)
    if is_small():
        both_grads = [after(add_low(mine, swap_y(far)), in_other) for mine, far in firsts]
    else:
        both_grads = [
            lax.psum_scatter(dots, "dp", scatter_dimension=0, tiled=False) for dots in both_dots
        ]
    q_slots = after(q_slots, both_grads)
    in_own = project_back(s_at, both_grad, q_slots, w_keep, w_took, 0, experts, dps)
    one_sum, _ = group_scatter(in_own, in_other)
    shared = lax.psum(jnp.stack(both_grads), "expert")

    out_sums = after(out_sums, both_grads)
    out_pairs = []
    for out_sum in out_sums:
        out_pairs += z_rounds(pieces_of(out_sum), 1)
    out_pairs = jnp.concatenate(out_pairs, axis=0)
    mlp_high, mlp_low = in_two(mlp_mix)
    output = hidden + dot(mlp_high, out_pairs) + dot(mlp_low, out_pairs)
    result_out = output.astype(BF).reshape(seq_count, stretch, width)

    def joined(arrays):
        arrays = [array.reshape(seqs, rows_own, half) for array in arrays]
        mine = [lax.dynamic_index_in_dim(array, s_at, 0, keepdims=False) for array in arrays]
        give = [lax.dynamic_index_in_dim(array, 1 - s_at, 0, keepdims=False) for array in arrays]
        return join_columns(s_at, mine, [swap_x(array) for array in give], dps, F32)

    (grad_query,) = joined([query_grads])
    shared_grads = joined([shared[0], shared[1]])

    router_one_grad, router_one_input = gate_grads(
        normed_one, route_one, attn_idx, attn_gates, attn_gate_grad
    )
    normed_one_grad = one_sum + router_one_input
    input_grad, norm_one_grad = norm_back(x_in, norm_one, normed_one_grad)
    grad_x = (hidden_total + input_grad).astype(BF).reshape(seq_count, stretch, width)

    little = little_sum(
        jnp.concatenate(
            [norm_one_grad[None], router_one_grad.T, norm_two_grad, router_two_grad.T], axis=0
        )
    )
    return (
        result_out,
        grad_x,
        little[0],
        little[1 : 1 + experts].T,
        shared_grads[0],
        shared_grads[1],
        grad_query[None],
        grad_out_w.astype(F32)[None],
        little[1 + experts],
        little[2 + experts :].T,
        grad_gate[None],
        grad_up[None],
        grad_down[None],
    )


def solution(mesh):
    in_specs = (
        P("dp", ("expert", "seq"), None),
        P("dp"),
        P("dp", ("expert", "seq"), None),
        P("dp", ("expert", "seq"), None),
        P("dp", ("expert", "seq"), None),
        P(("dp", "seq")),
        P(("dp", "seq"), None),
        P(("dp", "seq"), None),
        P(("dp", "seq"), None),
        P("expert", ("dp", "seq"), None),
        P("expert", ("dp", "seq"), None),
        P(("dp", "seq")),
        P(("dp", "seq"), None),
        P("expert", None, ("dp", "seq")),
        P("expert", None, ("dp", "seq")),
        P("expert", ("dp", "seq"), None),
        P("dp", ("expert", "seq"), None),
    )
    out_specs = (
        P("dp", ("expert", "seq"), None),
        P("dp", ("expert", "seq"), None),
        P(("dp", "seq")),
        P(("dp", "seq"), None),
        P(("dp", "seq"), None),
        P(("dp", "seq"), None),
        P("expert", ("dp", "seq"), None),
        P("expert", ("dp", "seq"), None),
        P(("dp", "seq")),
        P(("dp", "seq"), None),
        P("expert", None, ("dp", "seq")),
        P("expert", None, ("dp", "seq")),
        P("expert", ("dp", "seq"), None),
    )
    return jax.shard_map(body, mesh=mesh, in_specs=in_specs, out_specs=out_specs, check_vma=False)
```

```python
import functools

import jax
import jax.numpy as jnp
from jax import lax
from jax.experimental import pallas as pl
from jax.experimental.pallas import tpu as pltpu
from jax.sharding import PartitionSpec as P

HEAD = 128
EPS = 1e-06
NEG = -1e30
HIGH = lax.Precision.HIGHEST
BF = jnp.bfloat16
F32 = jnp.float32
LOG2E = 1.4426950408889634


def dot(left, right):
    return jnp.dot(left, right, preferred_element_type=F32)


def dot_t(left, right):
    return lax.dot_general(left, right, (((1,), (1,)), ((), ())), preferred_element_type=F32)


def t_dot(left, right):
    return lax.dot_general(left, right, (((0,), (0,)), ((), ())), preferred_element_type=F32)


def after(value, *others):
    return lax.optimization_barrier((value, others))[0]


def ring(count, shift):
    return [(j, (j + shift) % count) for j in range(count)]


def flip(count, bit):
    return [(j, j ^ bit) for j in range(count)]


def swap_x(value):
    return lax.ppermute(value, "seq", flip(2, 1))


def swap_core(value):
    return lax.ppermute(value, "dp", flip(lax.axis_size("dp"), 1))


def swap_y(value):
    return lax.ppermute(value, "dp", flip(4, 2))


def z_rounds(pieces, sign):
    count = lax.axis_size("expert")
    return [pieces[0]] + [
        lax.ppermute(pieces[r], "expert", ring(count, sign * r)) for r in range(1, count)
    ]


def is_small():
    return lax.axis_size("dp") == 4 and lax.axis_size("expert") == 4


def add_low(*terms):
    total = terms[0].astype(F32)
    for term in terms[1:]:
        total = total + term.astype(F32)
    return total.astype(terms[0].dtype)


def square_gather(piece):
    return lax.all_gather(piece, ("dp", "seq"), axis=0, tiled=True)


def square_scatter(parts):
    return lax.psum_scatter(parts, ("dp", "seq"), scatter_dimension=0, tiled=True)


def group_gather(block):
    count = lax.axis_size("expert")
    if is_small():
        half = block.shape[0] // 2
        up = lax.ppermute(block, "expert", ring(count, -1))
        down = lax.ppermute(block, "expert", ring(count, 1))
        far = jnp.concatenate(
            [
                lax.ppermute(down[:half], "expert", ring(count, 1)),
                lax.ppermute(up[half:], "expert", ring(count, -1)),
            ],
            axis=0,
        )
        own = [block, up, far, down]
        return own + [swap_x(piece) for piece in own], [up, down]
    e_at, s_at = lax.axis_index("expert"), lax.axis_index("seq")
    every = lax.all_gather(block, ("expert", "seq"), axis=0, tiled=False)
    wanted = [
        (lax.rem(e_at + r, count)) * 2 + lax.rem(s_at + sp, 2)
        for sp in range(2)
        for r in range(count)
    ]
    return [lax.dynamic_index_in_dim(every, at, 0, keepdims=False) for at in wanted], []


def group_scatter(own, other):
    count = lax.axis_size("expert")
    if not is_small():
        e_at, s_at = lax.axis_index("expert"), lax.axis_index("seq")
        stacked = jnp.stack(list(own) + list(other))
        spots_of = [
            (lax.rem(s_at + b % 2, 2)) * count + lax.rem(b // 2 - e_at + count, count)
            for b in range(2 * count)
        ]
        ordered = jnp.stack(
            [lax.dynamic_index_in_dim(stacked, at, 0, keepdims=False) for at in spots_of]
        )
        total = lax.psum_scatter(ordered, ("expert", "seq"), scatter_dimension=0, tiled=False)
        return total.astype(F32), []
    half = own[0].shape[0] // 2
    halves = (slice(0, half), slice(half, 2 * half))
    far_took = swap_x(other[2])
    near_took = [swap_x(after(other[1], far_took)), swap_x(after(other[3], far_took))]
    own_took = swap_x(after(other[0], *near_took))
    far = [add_low(own[2][rows], far_took[rows]) for rows in halves]
    far_up = lax.ppermute(far[0], "expert", ring(count, 1))
    far_down = lax.ppermute(far[1], "expert", ring(count, -1))
    up = jnp.concatenate(
        [
            add_low(own[1][halves[0]], near_took[0][halves[0]], far_up),
            add_low(own[1][halves[1]], near_took[0][halves[1]]),
        ],
        axis=0,
    )
    down = jnp.concatenate(
        [
            add_low(own[3][halves[0]], near_took[1][halves[0]]),
            add_low(own[3][halves[1]], near_took[1][halves[1]], far_down),
        ],
        axis=0,
    )
    from_below = lax.ppermute(up, "expert", ring(count, 1))
    from_above = lax.ppermute(down, "expert", ring(count, -1))
    return add_low(own[0].astype(F32), own_took, from_below, from_above), [up, down]


def dp_first(parts):
    at = lax.axis_index("dp")
    core, row = at % 2, at // 2
    split = parts.reshape((2, 2) + parts.shape[1:])
    took = swap_core(lax.dynamic_index_in_dim(split, 1 - core, 1, keepdims=False))

    def of(y):
        mine = lax.dynamic_index_in_dim(split, y, 0, keepdims=False)
        mine = lax.dynamic_index_in_dim(mine, core, 0, keepdims=False)
        return add_low(mine, lax.dynamic_index_in_dim(took, y, 0, keepdims=False))

    return of(row), of(1 - row)


def tiny_scatter(value):
    if lax.axis_size("dp") != 4:
        shape = value.shape[2:]
        flat = lax.psum(value.reshape((-1,) + shape), ("dp", "seq"))
        at = lax.axis_index("dp") * 2 + lax.axis_index("seq")
        return lax.dynamic_index_in_dim(flat, at, 0, keepdims=False)
    at, s_at = lax.axis_index("dp"), lax.axis_index("seq")

    def fold(array, bit, axis, swap):
        mine = lax.dynamic_index_in_dim(array, bit, axis, keepdims=False)
        return mine + swap(lax.dynamic_index_in_dim(array, 1 - bit, axis, keepdims=False))

    value = fold(value, s_at, 1, swap_x)
    value = fold(value.reshape((2, 2) + value.shape[1:]), at % 2, 1, swap_core)
    return fold(value, at // 2, 0, swap_y)


def little_sum(value):
    rows, features = value.shape
    d_count, e_count = lax.axis_size("dp"), lax.axis_size("expert")
    own = features // (2 * d_count)
    held = tiny_scatter(value.reshape(rows, d_count, 2, own).transpose(1, 2, 0, 3))
    if e_count != 4:
        return lax.psum(held, "expert")
    held = held + lax.ppermute(held, "expert", flip(e_count, 1))
    return held + lax.ppermute(held, "expert", flip(e_count, 2))


def route_pairs(routes, order, is_valid, capacity):
    tokens_here, top_count = routes.shape
    pairs = tokens_here * top_count
    target = routes.reshape(pairs)
    second = lax.broadcasted_iota(jnp.int32, routes.shape, 1)
    priority = (order[:, None] * top_count + second).reshape(pairs)
    living = jnp.broadcast_to(is_valid[:, None], routes.shape).reshape(pairs)
    earlier = (
        (target[:, None] == target[None, :])
        & (priority[None, :] < priority[:, None])
        & living[None, :]
    )
    slot_index = jnp.sum(earlier.astype(jnp.int32), axis=1, dtype=jnp.int32)
    kept_pair = living & (slot_index < capacity)
    return (kept_pair.reshape(routes.shape), slot_index.reshape(routes.shape))


def spots(routes, kept, slot_index, experts, capacity):
    away = lax.rem(lax.axis_index("expert") - routes + experts, experts)
    part = capacity // 2
    place = (slot_index // part) * (experts * part) + away * part + slot_index % part
    flat = jnp.where(kept, place, -1)
    return flat


def hots(flat, experts, capacity):
    slots = lax.broadcasted_iota(jnp.int32, (1, experts * capacity), 1)
    return [flat[:, k : k + 1] == slots for k in range(flat.shape[1])]


def weigh(hot, weight):
    return sum(jnp.where(hot[k], weight[:, k : k + 1], 0.0) for k in range(len(hot)))


def in_two(value):
    high = lax.reduce_precision(value, 8, 7)
    return high.astype(BF), (value - high).astype(BF)


def in_columns(value):
    first = lax.reduce_precision(value, 8, 7)
    second = lax.reduce_precision(value - first, 8, 7)
    third = value - first - second
    columns = jnp.concatenate([first, second, third], axis=1).astype(BF)
    return jnp.pad(columns, ((0, 0), (0, 125)))


def rms_norm(values, gain):
    return values * lax.rsqrt(jnp.mean(values * values, axis=-1, keepdims=True) + EPS) * gain


def norm_back(values, gain, grad):
    factor = lax.rsqrt(jnp.mean(values * values, axis=1, keepdims=True) + EPS)
    unit = values * factor
    gain_grad = jnp.sum(grad * unit, axis=0)
    scaled = grad * gain
    return (factor * (scaled - unit * jnp.mean(scaled * unit, axis=1, keepdims=True)), gain_grad)


def gate_values(normed, router, routes):
    logits = dot(normed, router)
    experts = lax.broadcasted_iota(jnp.int32, logits.shape, 1)
    chosen = jnp.concatenate(
        [
            jnp.sum(jnp.where(routes[:, k : k + 1] == experts, logits, 0.0), axis=1, keepdims=True)
            for k in range(routes.shape[1])
        ],
        axis=1,
    )
    top = jnp.max(chosen, axis=1, keepdims=True)
    expo = jnp.exp(chosen - top)
    return expo / jnp.sum(expo, axis=1, keepdims=True)


def gate_grads(normed, router, routes, gates, gate_grad):
    chosen = gates * (gate_grad - jnp.sum(gates * gate_grad, axis=1, keepdims=True))
    experts = lax.broadcasted_iota(jnp.int32, (1, 1, router.shape[1]), 2)
    logit_grad = jnp.sum(jnp.where(routes[:, :, None] == experts, chosen[:, :, None], 0.0), axis=1)
    router_grad = jnp.dot(normed.astype(F32).T, logit_grad, precision=HIGH)
    input_grad = jnp.dot(logit_grad, router.astype(F32).T, precision=HIGH)
    return (router_grad, input_grad)


def tile_bias(info, tile, blocks, tokens):
    stretch = tokens // 2
    row_seq, row_place = info[:, 0:1], info[:, 1:2]
    rows = info.shape[0]
    col = lax.broadcasted_iota(jnp.int32, (rows, tokens), 1)
    same = (col // stretch) == row_seq
    near = jnp.where(same, 0.0, NEG)
    place = lax.rem(col, stretch)
    diagonal = [
        jnp.where(same & (place + (tile * blocks + j) * stretch <= row_place), 0.0, NEG)
        for j in range(blocks)
    ]
    return jnp.concatenate([near] * (tile * blocks) + diagonal, axis=1)


def picked(ref, index, at, count):
    return jnp.concatenate([ref[index[at + j]] for j in range(count)], axis=0)


def attend_kernel(index, info, query, keys, values, mixed, logs, *, blocks):
    head = pl.program_id(0)
    total, capacity, _ = query.shape
    tokens = keys.shape[1]
    rate = HEAD ** (-0.5) * LOG2E
    lane = lax.broadcasted_iota(jnp.int32, (capacity, logs.shape[2]), 1)
    for tile in range(total // blocks):
        first = tile * blocks
        q = picked(query, index, first, blocks)
        k = picked(keys, index, 0, first + blocks)
        v = picked(values, index, 0, first + blocks)
        bias = tile_bias(picked(info, index, first, blocks), tile, blocks, tokens)
        scores = dot_t(q, k) + bias
        top = jnp.max(scores, axis=1, keepdims=True)
        expo = jnp.exp2((scores - top) * rate)
        norm = jnp.sum(expo, axis=1, keepdims=True)
        out = (dot(expo.astype(BF), v) / norm).astype(BF)
        log = top * rate + jnp.log2(norm)
        for j in range(blocks):
            rows = slice(j * capacity, (j + 1) * capacity)
            mixed[index[first + j]] = out[rows]
            held = logs[index[first + j]]
            logs[index[first + j]] = jnp.where(lane == head, log[rows], held)


def attend_back_kernel(
    index, info, query, keys, values, logs, mixed_grad, q_grad, k_grad, v_grad, k_sum, v_sum, *, blocks
):
    head = pl.program_id(0)
    total, capacity, _ = query.shape
    tokens = keys.shape[1]
    scale = HEAD ** (-0.5)
    rate = scale * LOG2E
    k_sum[...] = jnp.zeros_like(k_sum)
    v_sum[...] = jnp.zeros_like(v_sum)
    for tile in range(total // blocks):
        first = tile * blocks
        q = picked(query, index, first, blocks)
        k = picked(keys, index, 0, first + blocks)
        v = picked(values, index, 0, first + blocks)
        g = picked(mixed_grad, index, first, blocks)
        log = picked(logs, index, first, blocks)
        lane = lax.broadcasted_iota(jnp.int32, log.shape, 1)
        log = jnp.sum(jnp.where(lane == head, log, 0.0), axis=1, keepdims=True)
        bias = tile_bias(picked(info, index, first, blocks), tile, blocks, tokens)
        probs = jnp.exp2((dot_t(q, k) + bias) * rate - log)
        prob_grad = dot_t(g, v)
        center = jnp.sum(probs * prob_grad, axis=1, keepdims=True)
        score_grad = (probs * (prob_grad - center)).astype(BF)
        out = (dot(score_grad, k) * scale).astype(BF)
        for j in range(blocks):
            q_grad[index[first + j]] = out[j * capacity : (j + 1) * capacity]
        k_part = t_dot(score_grad, q)
        v_part = t_dot(probs.astype(BF), g)
        for j in range(first + blocks):
            rows = slice(j * tokens, (j + 1) * tokens)
            k_sum[index[j]] += k_part[rows]
            v_sum[index[j]] += v_part[rows]
    k_grad[...] = (k_sum[...] * scale).astype(BF)
    v_grad[...] = v_sum[...].astype(BF)


def head_spec(shape, skip=0):
    return pl.BlockSpec((shape[0], shape[1], HEAD), lambda h, index: (0, 0, h + skip))


def flat_spec(shape):
    return pl.BlockSpec(shape, lambda h, index: (0, 0, 0))


def attend(index, info, query, both):
    total, capacity, width = query.shape
    tokens = both.shape[1]
    heads = width // HEAD
    blocks = max(1, 256 // capacity)
    log_shape = (total, capacity, 128)
    flops = 4 * total * capacity * total * tokens * width
    return pl.pallas_call(
        functools.partial(attend_kernel, blocks=blocks),
        grid_spec=pltpu.PrefetchScalarGridSpec(
            num_scalar_prefetch=1,
            grid=(heads,),
            in_specs=[
                flat_spec(info.shape),
                head_spec(query.shape),
                head_spec(both.shape),
                head_spec(both.shape, heads),
            ],
            out_specs=[head_spec(query.shape), flat_spec(log_shape)],
        ),
        out_shape=[
            jax.ShapeDtypeStruct(query.shape, BF),
            jax.ShapeDtypeStruct(log_shape, F32),
        ],
        compiler_params=pltpu.CompilerParams(vmem_limit_bytes=60 << 20),
        cost_estimate=pl.CostEstimate(
            flops=flops, bytes_accessed=16 << 20, transcendentals=flops // 512
        ),
    )(index, info, query, both, both)


def attend_back(index, info, query, both, logs, mixed_grad):
    total, capacity, width = query.shape
    tokens = both.shape[1]
    heads = width // HEAD
    blocks = max(1, 256 // capacity)
    flops = 10 * total * capacity * total * tokens * width
    return pl.pallas_call(
        functools.partial(attend_back_kernel, blocks=blocks),
        grid_spec=pltpu.PrefetchScalarGridSpec(
            num_scalar_prefetch=1,
            grid=(heads,),
            in_specs=[
                flat_spec(info.shape),
                head_spec(query.shape),
                head_spec(both.shape),
                head_spec(both.shape, heads),
                flat_spec(logs.shape),
                head_spec(mixed_grad.shape),
            ],
            out_specs=[head_spec(query.shape)] + [head_spec((total, tokens, width))] * 2,
            scratch_shapes=[
                pltpu.VMEM((total, tokens, HEAD), F32),
                pltpu.VMEM((total, tokens, HEAD), F32),
            ],
        ),
        out_shape=[
            jax.ShapeDtypeStruct(query.shape, BF),
        ]
        + [jax.ShapeDtypeStruct((total, tokens, width), BF)] * 2,
        compiler_params=pltpu.CompilerParams(vmem_limit_bytes=60 << 20),
        cost_estimate=pl.CostEstimate(
            flops=flops, bytes_accessed=32 << 20, transcendentals=flops // 1280
        ),
    )(index, info, query, both, both, logs, mixed_grad)


def held_spec(shape):
    return pl.BlockSpec(
        shape, lambda *at: (0,) * len(shape), pipeline_mode=pl.Buffered(buffer_count=1)
    )


def held_out(shape):
    return pl.BlockSpec(shape, lambda *at: (0,) * len(shape))


def step_spec(shape, skip=0):
    zeros = (0,) * (len(shape) - 1)
    return pl.BlockSpec(shape, lambda step, *rest: (step + skip,) + zeros)


def fetch(step, refs, target):
    for piece, ref in enumerate(refs):

        @pl.when(step == piece)
        def _(ref=ref):
            target[...] = ref[...]


def halves_kernel(place, *refs, count):
    small, keep, give = refs[2 * count :]
    step = pl.program_id(0)
    size = refs[0].shape[1]
    blocks = (keep.shape[1] - 128) // (count * size)
    for j in range(count):
        at = pl.ds(pl.multiple_of((j * blocks + step) * size, 128), size)
        keep[:, at] = refs[2 * j][...]
        give[:, at] = refs[2 * j + 1][...]
    keep[:, keep.shape[1] - 128 :] = small[...]
    give[:, keep.shape[1] - 128 :] = small[...]


def weight_halves(s_at, weights, small, blocks):
    rows, columns = weights[0].shape
    size = columns // (2 * blocks)
    count = len(weights)
    shape = (rows, count * blocks * size + 128)
    specs = []
    for _ in weights:
        specs.append(pl.BlockSpec((rows, size), lambda step, place: (0, 2 * step + place[0])))
        specs.append(pl.BlockSpec((rows, size), lambda step, place: (0, 2 * step + 1 - place[0])))
    return pl.pallas_call(
        functools.partial(halves_kernel, count=count),
        grid_spec=pltpu.PrefetchScalarGridSpec(
            num_scalar_prefetch=1,
            grid=(blocks,),
            in_specs=specs + [pl.BlockSpec((rows, 128), lambda step, place: (0, 0))],
            out_specs=[pl.BlockSpec(shape, lambda step, place: (0, 0))] * 2,
        ),
        out_shape=[jax.ShapeDtypeStruct(shape, BF)] * 2,
        compiler_params=pltpu.CompilerParams(vmem_limit_bytes=24 << 20),
        cost_estimate=pl.CostEstimate(flops=0, bytes_accessed=8 << 20, transcendentals=0),
    )(s_at[None], *[w for weight in weights for w in (weight, weight)], small)


def join_kernel(place, *refs, count, blocks):
    mine, other, outs = refs[:count], refs[count : 2 * count], refs[2 * count :]
    size = mine[0].shape[1] // blocks
    for j in range(count):
        for block in range(blocks):
            for seq, ref in enumerate((mine[j], other[j])):
                found = ref[:, block * size : (block + 1) * size].astype(outs[j].dtype)
                outs[j][:, block_at(place, block, seq, size)] = found


def join_columns(s_at, mine, other, blocks, dtype):
    rows, half = mine[0].shape
    count = len(mine)
    return pl.pallas_call(
        functools.partial(join_kernel, count=count, blocks=blocks),
        grid_spec=pltpu.PrefetchScalarGridSpec(
            num_scalar_prefetch=1,
            grid=(1,),
            in_specs=[held_spec((rows, half))] * 2 * count,
            out_specs=[held_out((rows, 2 * half))] * count,
        ),
        out_shape=[jax.ShapeDtypeStruct((rows, 2 * half), dtype)] * count,
        compiler_params=pltpu.CompilerParams(vmem_limit_bytes=60 << 20),
        cost_estimate=pl.CostEstimate(flops=0, bytes_accessed=4 << 20, transcendentals=0),
    )(s_at[None], *mine, *other)


def block_at(place, block, other, size):
    seq = 1 - place[0] if other else place[0]
    return pl.ds(pl.multiple_of((2 * block + seq) * size, 128), size)


def project_kernel(place, gain, pick, keep, took, *refs, x_count, dps):
    normed_out, both_out, query_out, held, low, rows = refs[x_count:]
    double, half = both_out.shape[2], query_out.shape[2]
    blocks, tok, width = normed_out.shape
    cap = query_out.shape[1]
    size = width // (2 * dps)
    step = pl.program_id(0)
    for j in range(blocks):
        fetch(step * blocks + j, refs[:x_count], held.at[pl.ds(j * tok, tok)])
    x = held[:, :width].astype(F32)
    factor = lax.rsqrt(jnp.mean(x * x, axis=1, keepdims=True) + EPS)
    normed = (x * factor * gain[...]).astype(BF)
    low[...] = normed
    for j in range(blocks):
        mine = normed[j * tok : (j + 1) * tok]
        normed_out[j] = mine
        rows[j * cap : (j + 1) * cap] = dot(pick[j], mine).astype(BF)
    both = query = None
    for other, weights in enumerate((keep, took)):
        left = jnp.concatenate([low[:, block_at(place, d, other, size)] for d in range(dps)], axis=1)
        right = jnp.concatenate([rows[:, block_at(place, d, other, size)] for d in range(dps)], axis=1)
        kv_part = dot(left, weights[:, :double])
        q_part = dot(right, weights[:, double : double + half])
        both = kv_part if both is None else both + kv_part
        query = q_part if query is None else query + q_part
    both, query = both.astype(BF), query.astype(BF)
    for j in range(blocks):
        both_out[j] = both[j * tok : (j + 1) * tok]
        query_out[j] = query[j * cap : (j + 1) * cap]


def project(s_at, gain, pick, x_parts, keep, took, half, dps):
    total, cap, tok = pick.shape
    width = gain.shape[1]
    blocks = 2
    flops = 2 * total * (tok * width * 2 * half + cap * width * half)
    return pl.pallas_call(
        functools.partial(project_kernel, x_count=len(x_parts), dps=dps),
        grid_spec=pltpu.PrefetchScalarGridSpec(
            num_scalar_prefetch=1,
            grid=(total // blocks,),
            in_specs=[
                held_spec((1, width)),
                step_spec((blocks, cap, tok)),
                held_spec(keep.shape),
                held_spec(took.shape),
            ]
            + [held_spec(part.shape) for part in x_parts],
            out_specs=[
                step_spec((blocks, tok, width)),
                step_spec((blocks, tok, 2 * half)),
                step_spec((blocks, cap, half)),
            ],
            scratch_shapes=[
                pltpu.VMEM((blocks * tok, x_parts[0].shape[1]), BF),
                pltpu.VMEM((blocks * tok, width), BF),
                pltpu.VMEM((blocks * cap, width), BF),
            ],
        ),
        out_shape=[
            jax.ShapeDtypeStruct((total, tok, width), BF),
            jax.ShapeDtypeStruct((total, tok, 2 * half), BF),
            jax.ShapeDtypeStruct((total, cap, half), BF),
        ],
        compiler_params=pltpu.CompilerParams(vmem_limit_bytes=60 << 20),
        cost_estimate=pl.CostEstimate(flops=flops, bytes_accessed=40 << 20, transcendentals=0),
    )(s_at[None], gain, pick, keep, took, *x_parts)


def back_kernel(place, k_grad, v_grad, slots, keep, took, *refs, dps):
    outs, held = refs[:-1], refs[-1]
    blocks, tok, half = slots.shape
    size = held.shape[1] // (2 * dps)
    q_rows = jnp.concatenate([slots[j] for j in range(blocks)], axis=0)
    k_rows = jnp.concatenate([k_grad[j] for j in range(blocks)], axis=0)
    v_rows = jnp.concatenate([v_grad[j] for j in range(blocks)], axis=0)
    for other, weights in enumerate((keep, took)):
        part = (
            dot_t(k_rows, weights[:, :half])
            + dot_t(v_rows, weights[:, half : 2 * half])
            + dot_t(q_rows, weights[:, 2 * half : 3 * half])
        ).astype(BF)
        for d in range(dps):
            held[:, block_at(place, d, other, size)] = part[:, d * size : (d + 1) * size]
    for j, out in enumerate(outs):

        @pl.when(pl.program_id(0) == j // blocks)
        def _(out=out, at=j % blocks * tok):
            out[...] = held[at : at + tok]


def project_back(s_at, both_grad, slots, keep, took, first, count, dps):
    total, tok, half = slots.shape
    width = 2 * keep.shape[0]
    blocks = 2
    skip = first // blocks
    whole = pl.BlockSpec((tok, width), lambda *at: (0, 0))
    return pl.pallas_call(
        functools.partial(back_kernel, dps=dps),
        grid_spec=pltpu.PrefetchScalarGridSpec(
            num_scalar_prefetch=1,
            grid=(count // blocks,),
            in_specs=[
                step_spec((blocks, tok, half), skip),
                step_spec((blocks, tok, half), skip),
                step_spec((blocks, tok, half), skip),
                held_spec(keep.shape),
                held_spec(took.shape),
            ],
            out_specs=[whole] * count,
            scratch_shapes=[pltpu.VMEM((blocks * tok, width), BF)],
        ),
        out_shape=[jax.ShapeDtypeStruct((tok, width), BF)] * count,
        compiler_params=pltpu.CompilerParams(vmem_limit_bytes=60 << 20),
        cost_estimate=pl.CostEstimate(
            flops=6 * count * tok * width * half, bytes_accessed=24 << 20, transcendentals=0
        ),
    )(s_at[None], *both_grad, slots, keep, took)


def expert_kernel(
    rows, act_back, gate_wt, up_wt, in_out, gate_out, up_out, scaled_out, act_out, dots_out
):
    width = gate_wt.shape[1]
    x = rows[:, :width]
    tail = rows[:, width : width + 128].astype(F32)
    weight = tail[:, 0:1] + tail[:, 1:2] + tail[:, 2:3]
    gate_pre = dot_t(x, gate_wt[...])
    up_pre = dot_t(x, up_wt[...])
    sigma = jax.nn.sigmoid(gate_pre)
    activated = gate_pre * sigma
    act = activated * up_pre
    back = act_back[...]
    dots_out[...] = jnp.sum(act * back, axis=1, keepdims=True)
    back = back * weight
    gate_grad = (back * up_pre * sigma * (1.0 + gate_pre * (1.0 - sigma))).astype(BF)
    up_grad = (back * activated).astype(BF)
    gate_out[...] = gate_grad
    up_out[...] = up_grad
    scaled_out[...] = (act * weight).astype(BF)
    act_out[...] = act.astype(BF)
    in_out[...] = (dot(gate_grad, gate_wt[...]) + dot(up_grad, up_wt[...])).astype(BF)


def expert_mlp(rows, act_back, gate_wt, up_wt):
    inner, width = gate_wt.shape
    every = rows.shape[0]
    size = min(512, every)
    return pl.pallas_call(
        expert_kernel,
        grid=(every // size,),
        in_specs=[step_spec((size, rows.shape[1])), step_spec((size, inner))]
        + [held_spec(w.shape) for w in (gate_wt, up_wt)],
        out_specs=[step_spec((size, width))]
        + [step_spec((size, inner))] * 4
        + [step_spec((size, 1))],
        out_shape=[jax.ShapeDtypeStruct((every, width), BF)]
        + [jax.ShapeDtypeStruct((every, inner), BF)] * 4
        + [jax.ShapeDtypeStruct((every, 1), F32)],
        compiler_params=pltpu.CompilerParams(vmem_limit_bytes=60 << 20),
        cost_estimate=pl.CostEstimate(
            flops=8 * every * width * inner,
            bytes_accessed=60 << 20,
            transcendentals=2 * every * inner,
        ),
    )(rows, act_back, gate_wt, up_wt)


def lanes_of(value):
    return lax.broadcasted_iota(jnp.int32, (value.shape[0], 128), 1)


def three_low(value):
    first = value.astype(BF)
    rest = value - first.astype(F32)
    second = rest.astype(BF)
    return first, second, (rest - second.astype(F32)).astype(BF)


def hot_of(flat, slots):
    ids = lax.broadcasted_iota(jnp.int32, (flat.shape[0], slots), 1)
    return [flat[:, k : k + 1] == ids for k in range(flat.shape[1])]


def combine_kernel(x, mix_high, mix_low, gain, router, routes, flat, *refs, count):
    pairs = jnp.concatenate([ref[...] for ref in refs[:count]], axis=0)
    hidden_out, normed_out, gates_out, mix_out = refs[count : count + 4]
    sends = refs[count + 4 :]
    part, width = refs[0].shape
    hidden = x[...].astype(F32) + dot(mix_high[...], pairs) + dot(mix_low[...], pairs)
    hidden_out[...] = hidden
    factor = lax.rsqrt(jnp.mean(hidden * hidden, axis=1, keepdims=True) + EPS)
    normed = (hidden * factor * gain[...]).astype(BF)
    normed_out[...] = normed
    logits = dot(normed, router[...])
    lanes = lanes_of(logits)
    ids, places = routes[...], flat[...]
    one, two = [
        jnp.sum(jnp.where(lanes == ids[:, k : k + 1], logits, 0.0), axis=1, keepdims=True)
        for k in range(2)
    ]
    top = jnp.maximum(one, two)
    one, two = jnp.exp(one - top), jnp.exp(two - top)
    gates = [one / (one + two), two / (one + two)]
    gates_out[...] = jnp.where(lanes == 0, gates[0], jnp.where(lanes == 1, gates[1], 0.0))
    hot = hot_of(places, part * count)
    mix = jnp.where(hot[0], gates[0], 0.0) + jnp.where(hot[1], gates[1], 0.0)
    mix_out[...] = mix
    pick = jnp.where(hot[0] | hot[1], 1.0, 0.0).astype(BF)
    rows = t_dot(pick, normed).astype(BF)
    ones = jnp.ones((hidden.shape[0], 128), BF)
    columns = [t_dot(term, ones) for term in three_low(mix)]
    lanes = lanes_of(columns[0])
    tail = jnp.where(lanes == 0, columns[0], 0.0)
    for j in (1, 2):
        tail = tail + jnp.where(lanes == j, columns[j], 0.0)
    tail = tail.astype(BF)
    for j, send in enumerate(sends):
        at = slice(j * part, (j + 1) * part)
        send[:, :width] = rows[at]
        send[:, width:] = tail[at]


def combine(x, mix_high, mix_low, gain, router, routes, flat, pairs):
    tok, width = x.shape
    part = pairs[0].shape[0]
    count = len(pairs)
    operands = (x, mix_high, mix_low, gain, router, routes, flat, *pairs)
    return pl.pallas_call(
        functools.partial(combine_kernel, count=count),
        grid=(1,),
        in_specs=[held_spec(operand.shape) for operand in operands],
        out_specs=[held_out((tok, width))] * 2
        + [held_out((tok, 128)), held_out((tok, part * count))]
        + [held_out((part, width + 128))] * count,
        out_shape=[
            jax.ShapeDtypeStruct((tok, width), F32),
            jax.ShapeDtypeStruct((tok, width), BF),
            jax.ShapeDtypeStruct((tok, 128), F32),
            jax.ShapeDtypeStruct((tok, part * count), F32),
        ]
        + [jax.ShapeDtypeStruct((part, width + 128), BF)] * count,
        compiler_params=pltpu.CompilerParams(vmem_limit_bytes=60 << 20),
        cost_estimate=pl.CostEstimate(
            flops=6 * tok * part * count * width, bytes_accessed=10 << 20, transcendentals=0
        ),
    )(*operands)


def between_kernel(
    hidden, normed, grad_out, gain, router, routes, flat, gates, attn_pick, weight, *refs, count
):
    parts = refs[:count]
    total_out, high_out, gain_out, logit_out = refs[count : count + 4]
    sends = refs[count + 4 :]
    part, width = sends[0].shape
    rows = jnp.concatenate([ref[:, :width] for ref in parts], axis=0)
    tail = jnp.concatenate([ref[:, width:] for ref in parts], axis=0)
    hot = hot_of(flat[...], part * count)
    ids, held = routes[...], gates[...]
    lanes = lanes_of(held)
    slot_grad = []
    for k in range(2):
        found = dot(jnp.where(hot[k], 1.0, 0.0).astype(BF), tail)
        slot_grad.append(jnp.sum(jnp.where(lanes < 3, found, 0.0), axis=1, keepdims=True))
    gate = [held[:, 0:1], held[:, 1:2]]
    center = gate[0] * slot_grad[0] + gate[1] * slot_grad[1]
    logit_grad = jnp.zeros(held.shape, F32)
    for k in range(2):
        chosen = gate[k] * (slot_grad[k] - center)
        logit_grad = logit_grad + jnp.where(lanes == ids[:, k : k + 1], chosen, 0.0)
    logit_out[...] = logit_grad
    pick = jnp.where(hot[0] | hot[1], 1.0, 0.0).astype(BF)
    grad = dot(pick, rows)
    for term in three_low(logit_grad):
        grad = grad + dot_t(term, router[...])
    values = hidden[...]
    factor = lax.rsqrt(jnp.mean(values * values, axis=1, keepdims=True) + EPS)
    unit = values * factor
    gain_out[...] = jnp.sum(grad * unit, axis=0, keepdims=True)
    scaled = grad * gain[...]
    back = factor * (scaled - unit * jnp.mean(scaled * unit, axis=1, keepdims=True))
    total = grad_out[...].astype(F32) + back
    total_out[...] = total
    high = total.astype(BF)
    low = (total - high.astype(F32)).astype(BF)
    high_out[...] = high
    picked_rows = t_dot(attn_pick[...], high) + t_dot(attn_pick[...], low)
    picked_rows = (picked_rows * weight[...]).astype(BF)
    for j, send in enumerate(sends):
        send[...] = picked_rows[j * part : (j + 1) * part]


def between(hidden, normed, grad_out, gain, router, routes, flat, gates, attn_pick, weight, parts):
    tok, width = hidden.shape
    part = parts[0].shape[0]
    count = len(parts)
    operands = (
        hidden, normed, grad_out, gain, router, routes, flat, gates, attn_pick, weight, *parts
    )
    return pl.pallas_call(
        functools.partial(between_kernel, count=count),
        grid=(1,),
        in_specs=[held_spec(operand.shape) for operand in operands],
        out_specs=[held_out((tok, width))] * 2
        + [held_out((1, width)), held_out((tok, 128))]
        + [held_out((part, width))] * count,
        out_shape=[
            jax.ShapeDtypeStruct((tok, width), F32),
            jax.ShapeDtypeStruct((tok, width), BF),
            jax.ShapeDtypeStruct((1, width), F32),
            jax.ShapeDtypeStruct((tok, 128), F32),
        ]
        + [jax.ShapeDtypeStruct((part, width), BF)] * count,
        compiler_params=pltpu.CompilerParams(vmem_limit_bytes=60 << 20),
        cost_estimate=pl.CostEstimate(
            flops=6 * tok * part * count * width, bytes_accessed=12 << 20, transcendentals=0
        ),
    )(*operands)


def act_back_kernel(grads, down_w, out):
    out[...] = dot_t(grads[...], down_w[...])


def expert_act_back(grads, down_w):
    every, width = grads.shape
    inner = down_w.shape[0]
    size = min(512, every)
    return pl.pallas_call(
        act_back_kernel,
        grid=(every // size,),
        in_specs=[step_spec((size, width)), held_spec(down_w.shape)],
        out_specs=step_spec((size, inner)),
        out_shape=jax.ShapeDtypeStruct((every, inner), F32),
        compiler_params=pltpu.CompilerParams(vmem_limit_bytes=60 << 20),
        cost_estimate=pl.CostEstimate(
            flops=2 * every * width * inner, bytes_accessed=18 << 20, transcendentals=0
        ),
    )(grads, down_w)


def body(
    inputs,
    lengths,
    attn_routes,
    mlp_routes,
    slot_order,
    gain_attn,
    router_attn,
    w_key,
    w_value,
    w_query,
    w_out,
    gain_mlp,
    router_mlp,
    w_gate,
    w_up,
    w_down,
    d_out,
):
    seq_count, stretch, width = inputs.shape
    tok = seq_count * stretch
    top_count = attn_routes.shape[2]
    experts = router_attn.shape[1]
    cap = top_count * tok // experts
    slots = experts * cap
    dps, seqs = lax.axis_size("dp"), lax.axis_size("seq")
    total = experts * seqs
    e_at, s_at = lax.axis_index("expert"), lax.axis_index("seq")
    block = e_at * seqs + s_at
    rows_own = w_key.shape[0]
    inner = w_key.shape[1]
    half = inner // seqs

    absolute = lax.broadcasted_iota(jnp.int32, (total,), 0)
    index = lax.rem(absolute % seqs - s_at + seqs, seqs) * experts + lax.rem(
        absolute // seqs - e_at + experts, experts
    )
    block_of = lax.rem(absolute % experts + e_at, experts) * seqs + lax.rem(
        absolute // experts + s_at, seqs
    )

    x_low = inputs.reshape(tok, width)
    attn_idx = attn_routes.reshape(tok, top_count)
    mlp_idx = mlp_routes.reshape(tok, top_count)
    order = slot_order.reshape(tok)
    marks = jnp.concatenate([attn_idx, order[:, None]], axis=1).astype(BF)
    marks = jnp.pad(marks, ((0, 0), (0, 128 - marks.shape[1])))
    x_marked = jnp.concatenate([x_low, marks], axis=1)

    small = [gain_attn[:, None], router_attn, gain_mlp[:, None], router_mlp]
    small.append(jnp.zeros((rows_own, 128 - 2 - 2 * experts), BF))
    w_keep, w_give = weight_halves(
        s_at, (w_key, w_value, w_query[0]), jnp.concatenate(small, axis=1), dps
    )
    x_parts, x_near = group_gather(x_marked)
    w_keep = lax.all_gather(w_keep, "dp", axis=0, tiled=True)
    w_took = lax.all_gather(after(swap_x(w_give), x_near), "dp", axis=0, tiled=True)
    out_w = lax.all_gather(w_out[0], "dp", axis=0, tiled=True)

    def feature_rows(first, last):
        pair = [w[:, 3 * half + first : 3 * half + last] for w in (w_keep, w_took)]
        pair = [w.reshape(dps, rows_own, last - first) for w in pair]
        pair = jnp.where(s_at == 0, jnp.stack(pair, axis=1), jnp.stack(pair[::-1], axis=1))
        return pair.reshape(width, last - first)

    small = feature_rows(0, 2 + 2 * experts)
    norm_one = small[:, 0].astype(F32)[None]
    route_one = small[:, 1 : 1 + experts]
    norm_two = small[:, 1 + experts].astype(F32)[None]
    route_two = jnp.pad(small[:, 2 + experts :], ((0, 0), (0, 128 - experts)))

    column = lax.broadcasted_iota(jnp.int32, (seq_count, stretch), 1)
    is_valid = (block * stretch + column < lengths[:, None]).reshape(tok)
    attn_kept, attn_slot = route_pairs(attn_idx, order, is_valid, cap)
    mlp_kept, mlp_slot = route_pairs(mlp_idx, order, is_valid, cap)
    attn_keep = attn_kept.astype(F32)
    attn_flat = spots(attn_idx, attn_kept, attn_slot, experts, cap)
    mlp_flat = spots(mlp_idx, mlp_kept, mlp_slot, experts, cap)
    attn_hot = hots(attn_flat, experts, cap)
    mlp_hot = hots(mlp_flat, experts, cap)
    attn_pick = (attn_hot[0] | attn_hot[1]).astype(BF)
    mlp_pick = (mlp_hot[0] | mlp_hot[1]).astype(BF)

    part = cap // 2
    chunk = experts * part
    chunks = [slice(c * chunk, (c + 1) * chunk) for c in range(2)]

    def pieces_of(array):
        return [array[r * part : (r + 1) * part] for r in range(experts)]

    g_low = d_out.reshape(tok, width)
    gate_wt, up_wt, down_w = w_gate[0].T, w_up[0].T, w_down[0]
    found = jnp.stack(
        [rows[:, width : width + 3] for rows in x_parts]
    ).astype(jnp.int32)
    tok_ids = lax.broadcasted_iota(jnp.int32, (1, tok), 1)
    places = block_of[:, None] * stretch + tok_ids % stretch
    limits = jnp.where(tok_ids // stretch == 0, lengths[0], lengths[1])
    mine = ((found[:, :, 0] == e_at) | (found[:, :, 1] == e_at)) & (places < limits)
    ranks = found[:, :, 2]
    ahead = mine[:, None, :] & (ranks[:, None, :] < ranks[:, :, None])
    ahead = jnp.sum(ahead.astype(jnp.int32), axis=2, dtype=jnp.int32)
    ahead = jnp.where(mine, ahead, cap)
    chosen = ahead[:, None, :] == lax.broadcasted_iota(jnp.int32, (1, cap, 1), 1)
    pick = chosen.astype(BF)
    row_seq = jnp.sum(jnp.where(chosen, (tok_ids // stretch)[:, None], 0), axis=2, dtype=jnp.int32)
    row_place = jnp.sum(jnp.where(chosen, places[:, None], 0), axis=2, dtype=jnp.int32)
    info = jnp.stack([row_seq, row_place], axis=2)

    normed_all, both, query = project(s_at, norm_one, pick, x_parts, w_keep, w_took, half, dps)
    g_send = t_dot(mlp_pick, g_low).astype(BF).reshape(2, experts, part, width)
    g_send = after(g_send, x_parts)
    g_took = z_rounds([g_send[:, r] for r in range(experts)], -1)
    g_took = jnp.stack(after(g_took, query), axis=1)
    g_rows = [square_gather(g_took[c].reshape(chunk, width)) for c in range(2)]
    act_back = [expert_act_back(rows, down_w) for rows in g_rows]
    mixed, logs = attend(index, info, query, both)
    mixed_parts = mixed.reshape(seqs, experts, 2, part, half)
    attn_pairs, took_before = [], []
    for c in range(2):
        partial = dot(mixed_parts[:, :, c].reshape(seqs * chunk, half), out_w).astype(BF)
        took = swap_x(after(partial[chunk:], *took_before))
        took_before = [took]
        attn_out = [
            add_low(mine, other) for mine, other in zip(pieces_of(partial[:chunk]), pieces_of(took))
        ]
        attn_pairs += z_rounds(attn_out, 1)
    attn_pairs, act_back = lax.optimization_barrier((attn_pairs, act_back))

    x_in = x_low.astype(F32)
    normed_one = normed_all[0]
    attn_gates = gate_values(normed_one, route_one, attn_idx)
    attn_weight = attn_gates * attn_keep
    attn_mix = weigh(attn_hot, attn_weight)
    mix_high, mix_low = in_two(attn_mix)
    hidden, normed_two, mlp_gates, mlp_mix, *rows_sends = combine(
        x_low, mix_high, mix_low, norm_two, route_two, mlp_idx, mlp_flat, attn_pairs
    )

    expert_out, rows_before = [], []
    for c in range(2):
        rows_send = after(rows_sends[c * experts : (c + 1) * experts], *rows_before)
        rows_took = jnp.concatenate(z_rounds(rows_send, -1), axis=0)
        rows_before = [rows_took]
        rows = square_gather(rows_took)
        expert_out.append(
            (rows,) + tuple(expert_mlp(rows, act_back[c], gate_wt, up_wt))
        )
    in_pairs, out_parts = [], []
    grads = []
    for c in range(2):
        found, g_part = expert_out[c], g_rows[c]
        if c == 1:
            found, g_part = after((found, g_part), in_pairs)
        grads.append(
            [
                t_dot(found[0][:, :width], found[2]),
                t_dot(found[0][:, :width], found[3]),
                t_dot(found[4], g_part),
            ]
        )
        if c == 1:
            grads = [low + high for low, high in zip(*grads)]
        in_sum = square_scatter(expert_out[c][1])
        out_parts.append(dot(after(expert_out[c][5], expert_out[1][1]), down_w).astype(BF))
        in_sum, grads, out_parts = lax.optimization_barrier((in_sum, grads, out_parts))
        dots = tiny_scatter(expert_out[c][6].reshape(dps, seqs, chunk))
        in_sum = jnp.concatenate([in_sum, in_columns(dots[:, None])], axis=1)
        in_pairs += z_rounds(pieces_of(in_sum), 1)
    grad_gate, grad_up, grad_down = grads

    attn_columns = jnp.sum(attn_mix, axis=0)[:, None]
    hidden_total, total_high, norm_two_grad, logit_grad, *dh_sends = between(
        hidden, normed_two, g_low, norm_two, route_two, mlp_idx, mlp_flat, mlp_gates, attn_pick,
        attn_columns, in_pairs,
    )
    router_two_grad = jnp.dot(
        normed_two.astype(F32).T, logit_grad[:, :experts], precision=HIGH
    )

    dh_own, dh_other = [], []
    for c in range(2):
        dh_send = after(dh_sends[c * experts : (c + 1) * experts], *dh_own)
        dh_own.append(jnp.concatenate(z_rounds(dh_send, -1), axis=0))
        dh_other.append(swap_x(after(dh_own[-1], *dh_other)))
    dh_rows = jnp.stack([jnp.stack(dh_own), jnp.stack(dh_other)])
    dh_rows = dh_rows.reshape(seqs, 2, experts, part, width).transpose(0, 2, 1, 3, 4)
    dh_rows = dh_rows.reshape(total * cap, width)

    out_sums = [
        square_scatter(out_parts[0]),
        square_scatter(after(out_parts[1], dh_rows)),
    ]

    slot_dots = dot_t(total_high, jnp.concatenate(attn_pairs, axis=0))
    attn_gate_grad = jnp.concatenate(
        [jnp.sum(jnp.where(hot, slot_dots, 0.0), axis=1, keepdims=True) for hot in attn_hot], axis=1
    )
    mixed_grad = dot_t(dh_rows, out_w).astype(BF).reshape(total, cap, half)
    mixed_grad = after(mixed_grad, out_sums[0])
    out_pairs = z_rounds(pieces_of(out_sums[0]), 1)
    q_grad, *both_grad = attend_back(index, info, query, both, logs, mixed_grad)
    both_grad = after(both_grad, out_pairs)

    flat_normed = normed_all.reshape(total * tok, width)
    both_dots = [
        t_dot(flat_normed, array.reshape(total * tok, half))
        .astype(BF)
        .reshape(dps, seqs * rows_own, half)
        for array in both_grad
    ]
    q_grad, both_grad = after((q_grad, both_grad), out_sums[1])
    if is_small():
        firsts = [dp_first(dots) for dots in both_dots]
        q_grad, both_grad = after((q_grad, both_grad), [far for _, far in firsts])
    q_slots = jnp.einsum("bct,bch->bth", pick, q_grad, preferred_element_type=F32).astype(BF)
    query_grads = t_dot(flat_normed, q_slots.reshape(total * tok, half)).astype(BF)
    q_slots = after(q_slots, query_grads)
    query_grads = lax.psum_scatter(query_grads, "dp", scatter_dimension=0, tiled=True)

    in_other = project_back(s_at, both_grad, q_slots, w_keep, w_took, experts, experts, dps)
    if is_small():
        both_grads = [after(add_low(mine, swap_y(far)), in_other) for mine, far in firsts]
    else:
        both_grads = [
            lax.psum_scatter(dots, "dp", scatter_dimension=0, tiled=False) for dots in both_dots
        ]
    out_pairs += z_rounds(pieces_of(out_sums[1]), 1)
    both_grads = after(both_grads, query_grads)
    q_slots = after(q_slots, both_grads, out_pairs)
    in_own = project_back(s_at, both_grad, q_slots, w_keep, w_took, 0, experts, dps)
    one_sum, _ = group_scatter(in_own, in_other)
    shared = lax.psum(jnp.stack(both_grads), "expert")
    dh_rows = after(dh_rows, in_own)
    grad_out_w = t_dot(mixed.reshape(total * cap, half), dh_rows).astype(BF)
    grad_out_w = lax.psum_scatter(grad_out_w, "dp", scatter_dimension=0, tiled=True)

    out_pairs = jnp.concatenate(out_pairs, axis=0)
    mlp_high, mlp_low = in_two(mlp_mix)
    output = hidden + dot(mlp_high, out_pairs) + dot(mlp_low, out_pairs)
    result_out = output.astype(BF).reshape(seq_count, stretch, width)

    def joined(arrays):
        arrays = [array.reshape(seqs, rows_own, half) for array in arrays]
        mine = [lax.dynamic_index_in_dim(array, s_at, 0, keepdims=False) for array in arrays]
        give = [lax.dynamic_index_in_dim(array, 1 - s_at, 0, keepdims=False) for array in arrays]
        return join_columns(s_at, mine, [swap_x(array) for array in give], dps, F32)

    (grad_query,) = joined([query_grads])
    shared_grads = joined([shared[0], shared[1]])

    router_one_grad, router_one_input = gate_grads(
        normed_one, route_one, attn_idx, attn_gates, attn_gate_grad
    )
    normed_one_grad = one_sum + router_one_input
    input_grad, norm_one_grad = norm_back(x_in, norm_one, normed_one_grad)
    grad_x = (hidden_total + input_grad).astype(BF).reshape(seq_count, stretch, width)

    norm_one_grad = after(norm_one_grad, shared)
    little = little_sum(
        jnp.concatenate(
            [norm_one_grad[None], router_one_grad.T, norm_two_grad, router_two_grad.T], axis=0
        )
    )
    return (
        result_out,
        grad_x,
        little[0],
        little[1 : 1 + experts].T,
        shared_grads[0],
        shared_grads[1],
        grad_query[None],
        grad_out_w.astype(F32)[None],
        little[1 + experts],
        little[2 + experts :].T,
        grad_gate[None],
        grad_up[None],
        grad_down[None],
    )


def solution(mesh):
    in_specs = (
        P("dp", ("expert", "seq"), None),
        P("dp"),
        P("dp", ("expert", "seq"), None),
        P("dp", ("expert", "seq"), None),
        P("dp", ("expert", "seq"), None),
        P(("dp", "seq")),
        P(("dp", "seq"), None),
        P(("dp", "seq"), None),
        P(("dp", "seq"), None),
        P("expert", ("dp", "seq"), None),
        P("expert", ("dp", "seq"), None),
        P(("dp", "seq")),
        P(("dp", "seq"), None),
        P("expert", None, ("dp", "seq")),
        P("expert", None, ("dp", "seq")),
        P("expert", ("dp", "seq"), None),
        P("dp", ("expert", "seq"), None),
    )
    out_specs = (
        P("dp", ("expert", "seq"), None),
        P("dp", ("expert", "seq"), None),
        P(("dp", "seq")),
        P(("dp", "seq"), None),
        P(("dp", "seq"), None),
        P(("dp", "seq"), None),
        P("expert", ("dp", "seq"), None),
        P("expert", ("dp", "seq"), None),
        P(("dp", "seq")),
        P(("dp", "seq"), None),
        P("expert", None, ("dp", "seq")),
        P("expert", None, ("dp", "seq")),
        P("expert", ("dp", "seq"), None),
    )
    return jax.shard_map(body, mesh=mesh, in_specs=in_specs, out_specs=out_specs, check_vma=False)
```

```python
import functools

import jax
import jax.numpy as jnp
from jax import lax
from jax.experimental import pallas as pl
from jax.experimental.pallas import tpu as pltpu
from jax.sharding import PartitionSpec as P

HEAD = 128
EPS = 1e-06
NEG = -1e30
HIGH = lax.Precision.HIGHEST
BF = jnp.bfloat16
F32 = jnp.float32
LOG2E = 1.4426950408889634


def dot(left, right):
    return jnp.dot(left, right, preferred_element_type=F32)


def dot_t(left, right):
    return lax.dot_general(left, right, (((1,), (1,)), ((), ())), preferred_element_type=F32)


def t_dot(left, right):
    return lax.dot_general(left, right, (((0,), (0,)), ((), ())), preferred_element_type=F32)


def after(value, *others):
    return lax.optimization_barrier((value, others))[0]


def ring(count, shift):
    return [(j, (j + shift) % count) for j in range(count)]


def flip(count, bit):
    return [(j, j ^ bit) for j in range(count)]


def swap_x(value):
    return lax.ppermute(value, "seq", flip(2, 1))


def swap_core(value):
    return lax.ppermute(value, "dp", flip(lax.axis_size("dp"), 1))


def swap_y(value):
    return lax.ppermute(value, "dp", flip(4, 2))


def z_rounds(pieces, sign):
    count = lax.axis_size("expert")
    return [pieces[0]] + [
        lax.ppermute(pieces[r], "expert", ring(count, sign * r)) for r in range(1, count)
    ]


def is_small():
    return lax.axis_size("dp") == 4 and lax.axis_size("expert") == 4


def add_low(*terms):
    total = terms[0].astype(F32)
    for term in terms[1:]:
        total = total + term.astype(F32)
    return total.astype(terms[0].dtype)


def square_gather(piece):
    return lax.all_gather(piece, ("dp", "seq"), axis=0, tiled=True)


def square_scatter(parts):
    return lax.psum_scatter(parts, ("dp", "seq"), scatter_dimension=0, tiled=True)


def group_gather(block):
    count = lax.axis_size("expert")
    if is_small():
        half = block.shape[0] // 2
        up = lax.ppermute(block, "expert", ring(count, -1))
        down = lax.ppermute(block, "expert", ring(count, 1))
        far = jnp.concatenate(
            [
                lax.ppermute(down[:half], "expert", ring(count, 1)),
                lax.ppermute(up[half:], "expert", ring(count, -1)),
            ],
            axis=0,
        )
        own = [block, up, far, down]
        return own + [swap_x(piece) for piece in own], [up, down]
    e_at, s_at = lax.axis_index("expert"), lax.axis_index("seq")
    every = lax.all_gather(block, ("expert", "seq"), axis=0, tiled=False)
    wanted = [
        (lax.rem(e_at + r, count)) * 2 + lax.rem(s_at + sp, 2)
        for sp in range(2)
        for r in range(count)
    ]
    return [lax.dynamic_index_in_dim(every, at, 0, keepdims=False) for at in wanted], []


def far_swap(other):
    return swap_x(other[2]) if is_small() else None


def group_scatter(own, other, far_took):
    count = lax.axis_size("expert")
    if not is_small():
        e_at, s_at = lax.axis_index("expert"), lax.axis_index("seq")
        stacked = jnp.stack(list(own) + list(other))
        spots_of = [
            (lax.rem(s_at + b % 2, 2)) * count + lax.rem(b // 2 - e_at + count, count)
            for b in range(2 * count)
        ]
        ordered = jnp.stack(
            [lax.dynamic_index_in_dim(stacked, at, 0, keepdims=False) for at in spots_of]
        )
        total = lax.psum_scatter(ordered, ("expert", "seq"), scatter_dimension=0, tiled=False)
        return total.astype(F32), []
    half = own[0].shape[0] // 2
    halves = (slice(0, half), slice(half, 2 * half))
    near_took = [swap_x(after(other[1], far_took)), swap_x(after(other[3], far_took))]
    own_took = swap_x(after(other[0], *near_took))
    far = [add_low(own[2][rows], far_took[rows]) for rows in halves]
    far_up = lax.ppermute(far[0], "expert", ring(count, 1))
    far_down = lax.ppermute(far[1], "expert", ring(count, -1))
    up = jnp.concatenate(
        [
            add_low(own[1][halves[0]], near_took[0][halves[0]], far_up),
            add_low(own[1][halves[1]], near_took[0][halves[1]]),
        ],
        axis=0,
    )
    down = jnp.concatenate(
        [
            add_low(own[3][halves[0]], near_took[1][halves[0]]),
            add_low(own[3][halves[1]], near_took[1][halves[1]], far_down),
        ],
        axis=0,
    )
    from_below = lax.ppermute(up, "expert", ring(count, 1))
    from_above = lax.ppermute(down, "expert", ring(count, -1))
    return add_low(own[0].astype(F32), own_took, from_below, from_above), [up, down]


def dp_first(parts):
    at = lax.axis_index("dp")
    core, row = at % 2, at // 2
    split = parts.reshape((2, 2) + parts.shape[1:])
    took = swap_core(lax.dynamic_index_in_dim(split, 1 - core, 1, keepdims=False))

    def of(y):
        mine = lax.dynamic_index_in_dim(split, y, 0, keepdims=False)
        mine = lax.dynamic_index_in_dim(mine, core, 0, keepdims=False)
        return add_low(mine, lax.dynamic_index_in_dim(took, y, 0, keepdims=False))

    return of(row), of(1 - row)


def tiny_scatter(value):
    if lax.axis_size("dp") != 4:
        shape = value.shape[2:]
        flat = lax.psum(value.reshape((-1,) + shape), ("dp", "seq"))
        at = lax.axis_index("dp") * 2 + lax.axis_index("seq")
        return lax.dynamic_index_in_dim(flat, at, 0, keepdims=False)
    at, s_at = lax.axis_index("dp"), lax.axis_index("seq")

    def fold(array, bit, axis, swap):
        mine = lax.dynamic_index_in_dim(array, bit, axis, keepdims=False)
        return mine + swap(lax.dynamic_index_in_dim(array, 1 - bit, axis, keepdims=False))

    value = fold(value, s_at, 1, swap_x)
    value = fold(value.reshape((2, 2) + value.shape[1:]), at % 2, 1, swap_core)
    return fold(value, at // 2, 0, swap_y)


def little_sum(value):
    rows, features = value.shape
    d_count, e_count = lax.axis_size("dp"), lax.axis_size("expert")
    own = features // (2 * d_count)
    held = tiny_scatter(value.reshape(rows, d_count, 2, own).transpose(1, 2, 0, 3))
    if e_count != 4:
        return lax.psum(held, "expert")
    held = held + lax.ppermute(held, "expert", flip(e_count, 1))
    return held + lax.ppermute(held, "expert", flip(e_count, 2))


def route_pairs(routes, order, is_valid, capacity):
    tokens_here, top_count = routes.shape
    pairs = tokens_here * top_count
    target = routes.reshape(pairs)
    second = lax.broadcasted_iota(jnp.int32, routes.shape, 1)
    priority = (order[:, None] * top_count + second).reshape(pairs)
    living = jnp.broadcast_to(is_valid[:, None], routes.shape).reshape(pairs)
    earlier = (
        (target[:, None] == target[None, :])
        & (priority[None, :] < priority[:, None])
        & living[None, :]
    )
    slot_index = jnp.sum(earlier.astype(jnp.int32), axis=1, dtype=jnp.int32)
    kept_pair = living & (slot_index < capacity)
    return (kept_pair.reshape(routes.shape), slot_index.reshape(routes.shape))


def spots(routes, kept, slot_index, experts, capacity):
    away = lax.rem(lax.axis_index("expert") - routes + experts, experts)
    part = capacity // 2
    place = (slot_index // part) * (experts * part) + away * part + slot_index % part
    flat = jnp.where(kept, place, -1)
    return flat


def hots(flat, experts, capacity):
    slots = lax.broadcasted_iota(jnp.int32, (1, experts * capacity), 1)
    return [flat[:, k : k + 1] == slots for k in range(flat.shape[1])]


def weigh(hot, weight):
    return sum(jnp.where(hot[k], weight[:, k : k + 1], 0.0) for k in range(len(hot)))


def in_two(value):
    high = lax.reduce_precision(value, 8, 7)
    return high.astype(BF), (value - high).astype(BF)


def in_columns(value):
    first = lax.reduce_precision(value, 8, 7)
    second = lax.reduce_precision(value - first, 8, 7)
    third = value - first - second
    columns = jnp.concatenate([first, second, third], axis=1).astype(BF)
    return jnp.pad(columns, ((0, 0), (0, 125)))


def rms_norm(values, gain):
    return values * lax.rsqrt(jnp.mean(values * values, axis=-1, keepdims=True) + EPS) * gain


def norm_back(values, gain, grad):
    factor = lax.rsqrt(jnp.mean(values * values, axis=1, keepdims=True) + EPS)
    unit = values * factor
    gain_grad = jnp.sum(grad * unit, axis=0)
    scaled = grad * gain
    return (factor * (scaled - unit * jnp.mean(scaled * unit, axis=1, keepdims=True)), gain_grad)


def gate_values(normed, router, routes):
    logits = dot(normed, router)
    experts = lax.broadcasted_iota(jnp.int32, logits.shape, 1)
    chosen = jnp.concatenate(
        [
            jnp.sum(jnp.where(routes[:, k : k + 1] == experts, logits, 0.0), axis=1, keepdims=True)
            for k in range(routes.shape[1])
        ],
        axis=1,
    )
    top = jnp.max(chosen, axis=1, keepdims=True)
    expo = jnp.exp(chosen - top)
    return expo / jnp.sum(expo, axis=1, keepdims=True)


def gate_grads(normed, router, routes, gates, gate_grad):
    chosen = gates * (gate_grad - jnp.sum(gates * gate_grad, axis=1, keepdims=True))
    experts = lax.broadcasted_iota(jnp.int32, (1, 1, router.shape[1]), 2)
    logit_grad = jnp.sum(jnp.where(routes[:, :, None] == experts, chosen[:, :, None], 0.0), axis=1)
    router_grad = jnp.dot(normed.astype(F32).T, logit_grad, precision=HIGH)
    input_grad = jnp.dot(logit_grad, router.astype(F32).T, precision=HIGH)
    return (router_grad, input_grad)


def tile_bias(info, tile, blocks, tokens):
    stretch = tokens // 2
    row_seq, row_place = info[:, 0:1], info[:, 1:2]
    rows = info.shape[0]
    col = lax.broadcasted_iota(jnp.int32, (rows, tokens), 1)
    same = (col // stretch) == row_seq
    near = jnp.where(same, 0.0, NEG)
    place = lax.rem(col, stretch)
    diagonal = [
        jnp.where(same & (place + (tile * blocks + j) * stretch <= row_place), 0.0, NEG)
        for j in range(blocks)
    ]
    return jnp.concatenate([near] * (tile * blocks) + diagonal, axis=1)


def picked(ref, index, at, count):
    return jnp.concatenate([ref[index[at + j]] for j in range(count)], axis=0)


def attend_kernel(index, info, query, keys, values, mixed, logs, *, blocks):
    head = pl.program_id(0)
    total, capacity, _ = query.shape
    tokens = keys.shape[1]
    rate = HEAD ** (-0.5) * LOG2E
    lane = lax.broadcasted_iota(jnp.int32, (capacity, logs.shape[2]), 1)
    for tile in range(total // blocks):
        first = tile * blocks
        q = picked(query, index, first, blocks)
        k = picked(keys, index, 0, first + blocks)
        v = picked(values, index, 0, first + blocks)
        bias = tile_bias(picked(info, index, first, blocks), tile, blocks, tokens)
        scores = dot_t(q, k) + bias
        top = jnp.max(scores, axis=1, keepdims=True)
        expo = jnp.exp2((scores - top) * rate)
        norm = jnp.sum(expo, axis=1, keepdims=True)
        out = (dot(expo.astype(BF), v) / norm).astype(BF)
        log = top * rate + jnp.log2(norm)
        for j in range(blocks):
            rows = slice(j * capacity, (j + 1) * capacity)
            mixed[index[first + j]] = out[rows]
            held = logs[index[first + j]]
            logs[index[first + j]] = jnp.where(lane == head, log[rows], held)


def attend_back_kernel(
    index, info, query, keys, values, logs, mixed_grad, q_grad, k_grad, v_grad, k_sum, v_sum, *, blocks
):
    head = pl.program_id(0)
    total, capacity, _ = query.shape
    tokens = keys.shape[1]
    scale = HEAD ** (-0.5)
    rate = scale * LOG2E
    k_sum[...] = jnp.zeros_like(k_sum)
    v_sum[...] = jnp.zeros_like(v_sum)
    for tile in range(total // blocks):
        first = tile * blocks
        q = picked(query, index, first, blocks)
        k = picked(keys, index, 0, first + blocks)
        v = picked(values, index, 0, first + blocks)
        g = picked(mixed_grad, index, first, blocks)
        log = picked(logs, index, first, blocks)
        lane = lax.broadcasted_iota(jnp.int32, log.shape, 1)
        log = jnp.sum(jnp.where(lane == head, log, 0.0), axis=1, keepdims=True)
        bias = tile_bias(picked(info, index, first, blocks), tile, blocks, tokens)
        probs = jnp.exp2((dot_t(q, k) + bias) * rate - log)
        prob_grad = dot_t(g, v)
        center = jnp.sum(probs * prob_grad, axis=1, keepdims=True)
        score_grad = (probs * (prob_grad - center)).astype(BF)
        out = (dot(score_grad, k) * scale).astype(BF)
        for j in range(blocks):
            q_grad[index[first + j]] = out[j * capacity : (j + 1) * capacity]
        k_part = t_dot(score_grad, q)
        v_part = t_dot(probs.astype(BF), g)
        for j in range(first + blocks):
            rows = slice(j * tokens, (j + 1) * tokens)
            k_sum[index[j]] += k_part[rows]
            v_sum[index[j]] += v_part[rows]
    k_grad[...] = (k_sum[...] * scale).astype(BF)
    v_grad[...] = v_sum[...].astype(BF)


def head_spec(shape, skip=0):
    return pl.BlockSpec((shape[0], shape[1], HEAD), lambda h, index: (0, 0, h + skip))


def flat_spec(shape):
    return pl.BlockSpec(shape, lambda h, index: (0, 0, 0))


def attend(index, info, query, both):
    total, capacity, width = query.shape
    tokens = both.shape[1]
    heads = width // HEAD
    blocks = max(1, 256 // capacity)
    log_shape = (total, capacity, 128)
    flops = 4 * total * capacity * total * tokens * width
    return pl.pallas_call(
        functools.partial(attend_kernel, blocks=blocks),
        grid_spec=pltpu.PrefetchScalarGridSpec(
            num_scalar_prefetch=1,
            grid=(heads,),
            in_specs=[
                flat_spec(info.shape),
                head_spec(query.shape),
                head_spec(both.shape),
                head_spec(both.shape, heads),
            ],
            out_specs=[head_spec(query.shape), flat_spec(log_shape)],
        ),
        out_shape=[
            jax.ShapeDtypeStruct(query.shape, BF),
            jax.ShapeDtypeStruct(log_shape, F32),
        ],
        compiler_params=pltpu.CompilerParams(vmem_limit_bytes=60 << 20),
        cost_estimate=pl.CostEstimate(
            flops=flops, bytes_accessed=16 << 20, transcendentals=flops // 512
        ),
    )(index, info, query, both, both)


def attend_back(index, info, query, both, logs, mixed_grad):
    total, capacity, width = query.shape
    tokens = both.shape[1]
    heads = width // HEAD
    blocks = max(1, 256 // capacity)
    flops = 10 * total * capacity * total * tokens * width
    return pl.pallas_call(
        functools.partial(attend_back_kernel, blocks=blocks),
        grid_spec=pltpu.PrefetchScalarGridSpec(
            num_scalar_prefetch=1,
            grid=(heads,),
            in_specs=[
                flat_spec(info.shape),
                head_spec(query.shape),
                head_spec(both.shape),
                head_spec(both.shape, heads),
                flat_spec(logs.shape),
                head_spec(mixed_grad.shape),
            ],
            out_specs=[head_spec(query.shape)] + [head_spec((total, tokens, width))] * 2,
            scratch_shapes=[
                pltpu.VMEM((total, tokens, HEAD), F32),
                pltpu.VMEM((total, tokens, HEAD), F32),
            ],
        ),
        out_shape=[
            jax.ShapeDtypeStruct(query.shape, BF),
        ]
        + [jax.ShapeDtypeStruct((total, tokens, width), BF)] * 2,
        compiler_params=pltpu.CompilerParams(vmem_limit_bytes=60 << 20),
        cost_estimate=pl.CostEstimate(
            flops=flops, bytes_accessed=32 << 20, transcendentals=flops // 1280
        ),
    )(index, info, query, both, both, logs, mixed_grad)


def held_spec(shape):
    return pl.BlockSpec(
        shape, lambda *at: (0,) * len(shape), pipeline_mode=pl.Buffered(buffer_count=1)
    )


def held_out(shape):
    return pl.BlockSpec(shape, lambda *at: (0,) * len(shape))


def step_spec(shape, skip=0):
    zeros = (0,) * (len(shape) - 1)
    return pl.BlockSpec(shape, lambda step, *rest: (step + skip,) + zeros)


def fetch(step, refs, target):
    for piece, ref in enumerate(refs):

        @pl.when(step == piece)
        def _(ref=ref):
            target[...] = ref[...]


def halves_kernel(place, *refs, count):
    small, keep, give = refs[2 * count :]
    step = pl.program_id(0)
    size = refs[0].shape[1]
    blocks = (keep.shape[1] - 128) // (count * size)
    for j in range(count):
        at = pl.ds(pl.multiple_of((j * blocks + step) * size, 128), size)
        keep[:, at] = refs[2 * j][...]
        give[:, at] = refs[2 * j + 1][...]
    keep[:, keep.shape[1] - 128 :] = small[...]
    give[:, keep.shape[1] - 128 :] = small[...]


def weight_halves(s_at, weights, small, blocks):
    rows, columns = weights[0].shape
    size = columns // (2 * blocks)
    count = len(weights)
    shape = (rows, count * blocks * size + 128)
    specs = []
    for _ in weights:
        specs.append(pl.BlockSpec((rows, size), lambda step, place: (0, 2 * step + place[0])))
        specs.append(pl.BlockSpec((rows, size), lambda step, place: (0, 2 * step + 1 - place[0])))
    return pl.pallas_call(
        functools.partial(halves_kernel, count=count),
        grid_spec=pltpu.PrefetchScalarGridSpec(
            num_scalar_prefetch=1,
            grid=(blocks,),
            in_specs=specs + [pl.BlockSpec((rows, 128), lambda step, place: (0, 0))],
            out_specs=[pl.BlockSpec(shape, lambda step, place: (0, 0))] * 2,
        ),
        out_shape=[jax.ShapeDtypeStruct(shape, BF)] * 2,
        compiler_params=pltpu.CompilerParams(vmem_limit_bytes=24 << 20),
        cost_estimate=pl.CostEstimate(flops=0, bytes_accessed=8 << 20, transcendentals=0),
    )(s_at[None], *[w for weight in weights for w in (weight, weight)], small)


def join_kernel(place, *refs, count, blocks):
    mine, other, outs = refs[:count], refs[count : 2 * count], refs[2 * count :]
    size = mine[0].shape[1] // blocks
    for j in range(count):
        for block in range(blocks):
            for seq, ref in enumerate((mine[j], other[j])):
                found = ref[:, block * size : (block + 1) * size].astype(outs[j].dtype)
                outs[j][:, block_at(place, block, seq, size)] = found


def join_columns(s_at, mine, other, blocks, dtype):
    rows, half = mine[0].shape
    count = len(mine)
    return pl.pallas_call(
        functools.partial(join_kernel, count=count, blocks=blocks),
        grid_spec=pltpu.PrefetchScalarGridSpec(
            num_scalar_prefetch=1,
            grid=(1,),
            in_specs=[held_spec((rows, half))] * 2 * count,
            out_specs=[held_out((rows, 2 * half))] * count,
        ),
        out_shape=[jax.ShapeDtypeStruct((rows, 2 * half), dtype)] * count,
        compiler_params=pltpu.CompilerParams(vmem_limit_bytes=60 << 20),
        cost_estimate=pl.CostEstimate(flops=0, bytes_accessed=4 << 20, transcendentals=0),
    )(s_at[None], *mine, *other)


def block_at(place, block, other, size):
    seq = 1 - place[0] if other else place[0]
    return pl.ds(pl.multiple_of((2 * block + seq) * size, 128), size)


def project_kernel(place, gain, pick, keep, took, *refs, x_count, dps):
    normed_out, both_out, query_out, held, low, rows = refs[x_count:]
    double, half = both_out.shape[2], query_out.shape[2]
    blocks, tok, width = normed_out.shape
    cap = query_out.shape[1]
    size = width // (2 * dps)
    step = pl.program_id(0)
    for j in range(blocks):
        fetch(step * blocks + j, refs[:x_count], held.at[pl.ds(j * tok, tok)])
    x = held[:, :width].astype(F32)
    factor = lax.rsqrt(jnp.mean(x * x, axis=1, keepdims=True) + EPS)
    normed = (x * factor * gain[...]).astype(BF)
    low[...] = normed
    for j in range(blocks):
        mine = normed[j * tok : (j + 1) * tok]
        normed_out[j] = mine
        rows[j * cap : (j + 1) * cap] = dot(pick[j], mine).astype(BF)
    both = query = None
    for other, weights in enumerate((keep, took)):
        left = jnp.concatenate([low[:, block_at(place, d, other, size)] for d in range(dps)], axis=1)
        right = jnp.concatenate([rows[:, block_at(place, d, other, size)] for d in range(dps)], axis=1)
        kv_part = dot(left, weights[:, :double])
        q_part = dot(right, weights[:, double : double + half])
        both = kv_part if both is None else both + kv_part
        query = q_part if query is None else query + q_part
    both, query = both.astype(BF), query.astype(BF)
    for j in range(blocks):
        both_out[j] = both[j * tok : (j + 1) * tok]
        query_out[j] = query[j * cap : (j + 1) * cap]


def project(s_at, gain, pick, x_parts, keep, took, half, dps):
    total, cap, tok = pick.shape
    width = gain.shape[1]
    blocks = 2
    flops = 2 * total * (tok * width * 2 * half + cap * width * half)
    return pl.pallas_call(
        functools.partial(project_kernel, x_count=len(x_parts), dps=dps),
        grid_spec=pltpu.PrefetchScalarGridSpec(
            num_scalar_prefetch=1,
            grid=(total // blocks,),
            in_specs=[
                held_spec((1, width)),
                step_spec((blocks, cap, tok)),
                held_spec(keep.shape),
                held_spec(took.shape),
            ]
            + [held_spec(part.shape) for part in x_parts],
            out_specs=[
                step_spec((blocks, tok, width)),
                step_spec((blocks, tok, 2 * half)),
                step_spec((blocks, cap, half)),
            ],
            scratch_shapes=[
                pltpu.VMEM((blocks * tok, x_parts[0].shape[1]), BF),
                pltpu.VMEM((blocks * tok, width), BF),
                pltpu.VMEM((blocks * cap, width), BF),
            ],
        ),
        out_shape=[
            jax.ShapeDtypeStruct((total, tok, width), BF),
            jax.ShapeDtypeStruct((total, tok, 2 * half), BF),
            jax.ShapeDtypeStruct((total, cap, half), BF),
        ],
        compiler_params=pltpu.CompilerParams(vmem_limit_bytes=60 << 20),
        cost_estimate=pl.CostEstimate(flops=flops, bytes_accessed=40 << 20, transcendentals=0),
    )(s_at[None], gain, pick, keep, took, *x_parts)


def back_kernel(place, k_grad, v_grad, slots, keep, took, *refs, dps):
    outs, held = refs[:-1], refs[-1]
    blocks, tok, half = slots.shape
    size = held.shape[1] // (2 * dps)
    q_rows = jnp.concatenate([slots[j] for j in range(blocks)], axis=0)
    k_rows = jnp.concatenate([k_grad[j] for j in range(blocks)], axis=0)
    v_rows = jnp.concatenate([v_grad[j] for j in range(blocks)], axis=0)
    for other, weights in enumerate((keep, took)):
        part = (
            dot_t(k_rows, weights[:, :half])
            + dot_t(v_rows, weights[:, half : 2 * half])
            + dot_t(q_rows, weights[:, 2 * half : 3 * half])
        ).astype(BF)
        for d in range(dps):
            held[:, block_at(place, d, other, size)] = part[:, d * size : (d + 1) * size]
    for j, out in enumerate(outs):

        @pl.when(pl.program_id(0) == j // blocks)
        def _(out=out, at=j % blocks * tok):
            out[...] = held[at : at + tok]


def project_back(s_at, both_grad, slots, keep, took, first, count, dps):
    total, tok, half = slots.shape
    width = 2 * keep.shape[0]
    blocks = 2
    skip = first // blocks
    whole = pl.BlockSpec((tok, width), lambda *at: (0, 0))
    return pl.pallas_call(
        functools.partial(back_kernel, dps=dps),
        grid_spec=pltpu.PrefetchScalarGridSpec(
            num_scalar_prefetch=1,
            grid=(count // blocks,),
            in_specs=[
                step_spec((blocks, tok, half), skip),
                step_spec((blocks, tok, half), skip),
                step_spec((blocks, tok, half), skip),
                held_spec(keep.shape),
                held_spec(took.shape),
            ],
            out_specs=[whole] * count,
            scratch_shapes=[pltpu.VMEM((blocks * tok, width), BF)],
        ),
        out_shape=[jax.ShapeDtypeStruct((tok, width), BF)] * count,
        compiler_params=pltpu.CompilerParams(vmem_limit_bytes=60 << 20),
        cost_estimate=pl.CostEstimate(
            flops=6 * count * tok * width * half, bytes_accessed=24 << 20, transcendentals=0
        ),
    )(s_at[None], *both_grad, slots, keep, took)


def expert_kernel(
    rows, act_back, gate_wt, up_wt, in_out, gate_out, up_out, scaled_out, act_out, dots_out
):
    width = gate_wt.shape[1]
    x = rows[:, :width]
    tail = rows[:, width : width + 128].astype(F32)
    weight = tail[:, 0:1] + tail[:, 1:2] + tail[:, 2:3]
    gate_pre = dot_t(x, gate_wt[...])
    up_pre = dot_t(x, up_wt[...])
    sigma = jax.nn.sigmoid(gate_pre)
    activated = gate_pre * sigma
    act = activated * up_pre
    back = act_back[...]
    dots_out[...] = jnp.sum(act * back, axis=1, keepdims=True)
    back = back * weight
    gate_grad = (back * up_pre * sigma * (1.0 + gate_pre * (1.0 - sigma))).astype(BF)
    up_grad = (back * activated).astype(BF)
    gate_out[...] = gate_grad
    up_out[...] = up_grad
    scaled_out[...] = (act * weight).astype(BF)
    act_out[...] = act.astype(BF)
    in_out[...] = (dot(gate_grad, gate_wt[...]) + dot(up_grad, up_wt[...])).astype(BF)


def expert_mlp(rows, act_back, gate_wt, up_wt):
    inner, width = gate_wt.shape
    every = rows.shape[0]
    size = min(512, every)
    return pl.pallas_call(
        expert_kernel,
        grid=(every // size,),
        in_specs=[step_spec((size, rows.shape[1])), step_spec((size, inner))]
        + [held_spec(w.shape) for w in (gate_wt, up_wt)],
        out_specs=[step_spec((size, width))]
        + [step_spec((size, inner))] * 4
        + [step_spec((size, 1))],
        out_shape=[jax.ShapeDtypeStruct((every, width), BF)]
        + [jax.ShapeDtypeStruct((every, inner), BF)] * 4
        + [jax.ShapeDtypeStruct((every, 1), F32)],
        compiler_params=pltpu.CompilerParams(vmem_limit_bytes=60 << 20),
        cost_estimate=pl.CostEstimate(
            flops=8 * every * width * inner,
            bytes_accessed=60 << 20,
            transcendentals=2 * every * inner,
        ),
    )(rows, act_back, gate_wt, up_wt)


def lanes_of(value):
    return lax.broadcasted_iota(jnp.int32, (value.shape[0], 128), 1)


def three_low(value):
    first = value.astype(BF)
    rest = value - first.astype(F32)
    second = rest.astype(BF)
    return first, second, (rest - second.astype(F32)).astype(BF)


def hot_of(flat, slots):
    ids = lax.broadcasted_iota(jnp.int32, (flat.shape[0], slots), 1)
    return [flat[:, k : k + 1] == ids for k in range(flat.shape[1])]


def combine_kernel(x, mix_high, mix_low, gain, router, routes, flat, *refs, count):
    pairs = jnp.concatenate([ref[...] for ref in refs[:count]], axis=0)
    hidden_out, normed_out, gates_out, mix_out = refs[count : count + 4]
    sends = refs[count + 4 :]
    part, width = refs[0].shape
    hidden = x[...].astype(F32) + dot(mix_high[...], pairs) + dot(mix_low[...], pairs)
    hidden_out[...] = hidden
    factor = lax.rsqrt(jnp.mean(hidden * hidden, axis=1, keepdims=True) + EPS)
    normed = (hidden * factor * gain[...]).astype(BF)
    normed_out[...] = normed
    logits = dot(normed, router[...])
    lanes = lanes_of(logits)
    ids, places = routes[...], flat[...]
    one, two = [
        jnp.sum(jnp.where(lanes == ids[:, k : k + 1], logits, 0.0), axis=1, keepdims=True)
        for k in range(2)
    ]
    top = jnp.maximum(one, two)
    one, two = jnp.exp(one - top), jnp.exp(two - top)
    gates = [one / (one + two), two / (one + two)]
    gates_out[...] = jnp.where(lanes == 0, gates[0], jnp.where(lanes == 1, gates[1], 0.0))
    hot = hot_of(places, part * count)
    mix = jnp.where(hot[0], gates[0], 0.0) + jnp.where(hot[1], gates[1], 0.0)
    mix_out[...] = mix
    pick = jnp.where(hot[0] | hot[1], 1.0, 0.0).astype(BF)
    rows = t_dot(pick, normed).astype(BF)
    ones = jnp.ones((hidden.shape[0], 128), BF)
    columns = [t_dot(term, ones) for term in three_low(mix)]
    lanes = lanes_of(columns[0])
    tail = jnp.where(lanes == 0, columns[0], 0.0)
    for j in (1, 2):
        tail = tail + jnp.where(lanes == j, columns[j], 0.0)
    tail = tail.astype(BF)
    for j, send in enumerate(sends):
        at = slice(j * part, (j + 1) * part)
        send[:, :width] = rows[at]
        send[:, width:] = tail[at]


def combine(x, mix_high, mix_low, gain, router, routes, flat, pairs):
    tok, width = x.shape
    part = pairs[0].shape[0]
    count = len(pairs)
    operands = (x, mix_high, mix_low, gain, router, routes, flat, *pairs)
    return pl.pallas_call(
        functools.partial(combine_kernel, count=count),
        grid=(1,),
        in_specs=[held_spec(operand.shape) for operand in operands],
        out_specs=[held_out((tok, width))] * 2
        + [held_out((tok, 128)), held_out((tok, part * count))]
        + [held_out((part, width + 128))] * count,
        out_shape=[
            jax.ShapeDtypeStruct((tok, width), F32),
            jax.ShapeDtypeStruct((tok, width), BF),
            jax.ShapeDtypeStruct((tok, 128), F32),
            jax.ShapeDtypeStruct((tok, part * count), F32),
        ]
        + [jax.ShapeDtypeStruct((part, width + 128), BF)] * count,
        compiler_params=pltpu.CompilerParams(vmem_limit_bytes=60 << 20),
        cost_estimate=pl.CostEstimate(
            flops=6 * tok * part * count * width, bytes_accessed=10 << 20, transcendentals=0
        ),
    )(*operands)


def between_kernel(
    hidden, normed, grad_out, gain, router, routes, flat, gates, attn_pick, weight, *refs, count
):
    parts = refs[:count]
    total_out, high_out, gain_out, logit_out = refs[count : count + 4]
    sends = refs[count + 4 :]
    part, width = sends[0].shape
    rows = jnp.concatenate([ref[:, :width] for ref in parts], axis=0)
    tail = jnp.concatenate([ref[:, width:] for ref in parts], axis=0)
    hot = hot_of(flat[...], part * count)
    ids, held = routes[...], gates[...]
    lanes = lanes_of(held)
    slot_grad = []
    for k in range(2):
        found = dot(jnp.where(hot[k], 1.0, 0.0).astype(BF), tail)
        slot_grad.append(jnp.sum(jnp.where(lanes < 3, found, 0.0), axis=1, keepdims=True))
    gate = [held[:, 0:1], held[:, 1:2]]
    center = gate[0] * slot_grad[0] + gate[1] * slot_grad[1]
    logit_grad = jnp.zeros(held.shape, F32)
    for k in range(2):
        chosen = gate[k] * (slot_grad[k] - center)
        logit_grad = logit_grad + jnp.where(lanes == ids[:, k : k + 1], chosen, 0.0)
    logit_out[...] = logit_grad
    pick = jnp.where(hot[0] | hot[1], 1.0, 0.0).astype(BF)
    grad = dot(pick, rows)
    for term in three_low(logit_grad):
        grad = grad + dot_t(term, router[...])
    values = hidden[...]
    factor = lax.rsqrt(jnp.mean(values * values, axis=1, keepdims=True) + EPS)
    unit = values * factor
    gain_out[...] = jnp.sum(grad * unit, axis=0, keepdims=True)
    scaled = grad * gain[...]
    back = factor * (scaled - unit * jnp.mean(scaled * unit, axis=1, keepdims=True))
    total = grad_out[...].astype(F32) + back
    total_out[...] = total
    high = total.astype(BF)
    low = (total - high.astype(F32)).astype(BF)
    high_out[...] = high
    picked_rows = t_dot(attn_pick[...], high) + t_dot(attn_pick[...], low)
    picked_rows = (picked_rows * weight[...]).astype(BF)
    for j, send in enumerate(sends):
        send[...] = picked_rows[j * part : (j + 1) * part]


def between(hidden, normed, grad_out, gain, router, routes, flat, gates, attn_pick, weight, parts):
    tok, width = hidden.shape
    part = parts[0].shape[0]
    count = len(parts)
    operands = (
        hidden, normed, grad_out, gain, router, routes, flat, gates, attn_pick, weight, *parts
    )
    return pl.pallas_call(
        functools.partial(between_kernel, count=count),
        grid=(1,),
        in_specs=[held_spec(operand.shape) for operand in operands],
        out_specs=[held_out((tok, width))] * 2
        + [held_out((1, width)), held_out((tok, 128))]
        + [held_out((part, width))] * count,
        out_shape=[
            jax.ShapeDtypeStruct((tok, width), F32),
            jax.ShapeDtypeStruct((tok, width), BF),
            jax.ShapeDtypeStruct((1, width), F32),
            jax.ShapeDtypeStruct((tok, 128), F32),
        ]
        + [jax.ShapeDtypeStruct((part, width), BF)] * count,
        compiler_params=pltpu.CompilerParams(vmem_limit_bytes=60 << 20),
        cost_estimate=pl.CostEstimate(
            flops=6 * tok * part * count * width, bytes_accessed=12 << 20, transcendentals=0
        ),
    )(*operands)


def act_back_kernel(grads, down_w, out):
    out[...] = dot_t(grads[...], down_w[...])


def expert_act_back(grads, down_w):
    every, width = grads.shape
    inner = down_w.shape[0]
    size = min(512, every)
    return pl.pallas_call(
        act_back_kernel,
        grid=(every // size,),
        in_specs=[step_spec((size, width)), held_spec(down_w.shape)],
        out_specs=step_spec((size, inner)),
        out_shape=jax.ShapeDtypeStruct((every, inner), F32),
        compiler_params=pltpu.CompilerParams(vmem_limit_bytes=60 << 20),
        cost_estimate=pl.CostEstimate(
            flops=2 * every * width * inner, bytes_accessed=18 << 20, transcendentals=0
        ),
    )(grads, down_w)


def body(
    inputs,
    lengths,
    attn_routes,
    mlp_routes,
    slot_order,
    gain_attn,
    router_attn,
    w_key,
    w_value,
    w_query,
    w_out,
    gain_mlp,
    router_mlp,
    w_gate,
    w_up,
    w_down,
    d_out,
):
    seq_count, stretch, width = inputs.shape
    tok = seq_count * stretch
    top_count = attn_routes.shape[2]
    experts = router_attn.shape[1]
    cap = top_count * tok // experts
    slots = experts * cap
    dps, seqs = lax.axis_size("dp"), lax.axis_size("seq")
    total = experts * seqs
    e_at, s_at = lax.axis_index("expert"), lax.axis_index("seq")
    block = e_at * seqs + s_at
    rows_own = w_key.shape[0]
    inner = w_key.shape[1]
    half = inner // seqs

    absolute = lax.broadcasted_iota(jnp.int32, (total,), 0)
    index = lax.rem(absolute % seqs - s_at + seqs, seqs) * experts + lax.rem(
        absolute // seqs - e_at + experts, experts
    )
    block_of = lax.rem(absolute % experts + e_at, experts) * seqs + lax.rem(
        absolute // experts + s_at, seqs
    )

    x_low = inputs.reshape(tok, width)
    attn_idx = attn_routes.reshape(tok, top_count)
    mlp_idx = mlp_routes.reshape(tok, top_count)
    order = slot_order.reshape(tok)
    marks = jnp.concatenate([attn_idx, order[:, None]], axis=1).astype(BF)
    marks = jnp.pad(marks, ((0, 0), (0, 128 - marks.shape[1])))
    x_marked = jnp.concatenate([x_low, marks], axis=1)

    small = [gain_attn[:, None], router_attn, gain_mlp[:, None], router_mlp]
    small.append(jnp.zeros((rows_own, 128 - 2 - 2 * experts), BF))
    w_keep, w_give = weight_halves(
        s_at, (w_key, w_value, w_query[0]), jnp.concatenate(small, axis=1), dps
    )
    x_parts, x_near = group_gather(x_marked)
    w_keep = lax.all_gather(w_keep, "dp", axis=0, tiled=True)
    w_took = lax.all_gather(after(swap_x(w_give), x_near), "dp", axis=0, tiled=True)
    out_w = lax.all_gather(w_out[0], "dp", axis=0, tiled=True)

    def feature_rows(first, last):
        pair = [w[:, 3 * half + first : 3 * half + last] for w in (w_keep, w_took)]
        pair = [w.reshape(dps, rows_own, last - first) for w in pair]
        pair = jnp.where(s_at == 0, jnp.stack(pair, axis=1), jnp.stack(pair[::-1], axis=1))
        return pair.reshape(width, last - first)

    small = feature_rows(0, 2 + 2 * experts)
    norm_one = small[:, 0].astype(F32)[None]
    route_one = small[:, 1 : 1 + experts]
    norm_two = small[:, 1 + experts].astype(F32)[None]
    route_two = jnp.pad(small[:, 2 + experts :], ((0, 0), (0, 128 - experts)))

    column = lax.broadcasted_iota(jnp.int32, (seq_count, stretch), 1)
    is_valid = (block * stretch + column < lengths[:, None]).reshape(tok)
    attn_kept, attn_slot = route_pairs(attn_idx, order, is_valid, cap)
    mlp_kept, mlp_slot = route_pairs(mlp_idx, order, is_valid, cap)
    attn_keep = attn_kept.astype(F32)
    attn_flat = spots(attn_idx, attn_kept, attn_slot, experts, cap)
    mlp_flat = spots(mlp_idx, mlp_kept, mlp_slot, experts, cap)
    attn_hot = hots(attn_flat, experts, cap)
    mlp_hot = hots(mlp_flat, experts, cap)
    attn_pick = (attn_hot[0] | attn_hot[1]).astype(BF)
    mlp_pick = (mlp_hot[0] | mlp_hot[1]).astype(BF)

    part = cap // 2
    chunk = experts * part
    chunks = [slice(c * chunk, (c + 1) * chunk) for c in range(2)]

    def pieces_of(array):
        return [array[r * part : (r + 1) * part] for r in range(experts)]

    g_low = d_out.reshape(tok, width)
    gate_wt, up_wt, down_w = w_gate[0].T, w_up[0].T, w_down[0]
    found = jnp.stack(
        [rows[:, width : width + 3] for rows in x_parts]
    ).astype(jnp.int32)
    tok_ids = lax.broadcasted_iota(jnp.int32, (1, tok), 1)
    places = block_of[:, None] * stretch + tok_ids % stretch
    limits = jnp.where(tok_ids // stretch == 0, lengths[0], lengths[1])
    mine = ((found[:, :, 0] == e_at) | (found[:, :, 1] == e_at)) & (places < limits)
    ranks = found[:, :, 2]
    ahead = mine[:, None, :] & (ranks[:, None, :] < ranks[:, :, None])
    ahead = jnp.sum(ahead.astype(jnp.int32), axis=2, dtype=jnp.int32)
    ahead = jnp.where(mine, ahead, cap)
    chosen = ahead[:, None, :] == lax.broadcasted_iota(jnp.int32, (1, cap, 1), 1)
    pick = chosen.astype(BF)
    row_seq = jnp.sum(jnp.where(chosen, (tok_ids // stretch)[:, None], 0), axis=2, dtype=jnp.int32)
    row_place = jnp.sum(jnp.where(chosen, places[:, None], 0), axis=2, dtype=jnp.int32)
    info = jnp.stack([row_seq, row_place], axis=2)

    normed_all, both, query = project(s_at, norm_one, pick, x_parts, w_keep, w_took, half, dps)
    g_send = t_dot(mlp_pick, g_low).astype(BF).reshape(2, experts, part, width)
    g_send = after(g_send, x_parts)
    g_took = z_rounds([g_send[:, r] for r in range(experts)], -1)
    g_took = jnp.stack(after(g_took, query), axis=1)
    g_rows = [square_gather(g_took[c].reshape(chunk, width)) for c in range(2)]
    act_back = [expert_act_back(rows, down_w) for rows in g_rows]
    mixed, logs = attend(index, info, query, both)
    mixed_parts = mixed.reshape(seqs, experts, 2, part, half)
    attn_pairs, took_before = [], []
    for c in range(2):
        partial = dot(mixed_parts[:, :, c].reshape(seqs * chunk, half), out_w).astype(BF)
        took = swap_x(after(partial[chunk:], *took_before))
        took_before = [took]
        attn_out = [
            add_low(mine, other) for mine, other in zip(pieces_of(partial[:chunk]), pieces_of(took))
        ]
        attn_pairs += z_rounds(attn_out, 1)
    attn_pairs, act_back = lax.optimization_barrier((attn_pairs, act_back))

    x_in = x_low.astype(F32)
    normed_one = normed_all[0]
    attn_gates = gate_values(normed_one, route_one, attn_idx)
    attn_weight = attn_gates * attn_keep
    attn_mix = weigh(attn_hot, attn_weight)
    mix_high, mix_low = in_two(attn_mix)
    hidden, normed_two, mlp_gates, mlp_mix, *rows_sends = combine(
        x_low, mix_high, mix_low, norm_two, route_two, mlp_idx, mlp_flat, attn_pairs
    )

    expert_out, rows_before = [], []
    for c in range(2):
        rows_send = after(rows_sends[c * experts : (c + 1) * experts], *rows_before)
        rows_took = jnp.concatenate(z_rounds(rows_send, -1), axis=0)
        rows_before = [rows_took]
        rows = square_gather(rows_took)
        expert_out.append(
            (rows,) + tuple(expert_mlp(rows, act_back[c], gate_wt, up_wt))
        )
    in_pairs, out_parts = [], []
    grads = []
    for c in range(2):
        found, g_part = expert_out[c], g_rows[c]
        if c == 1:
            found, g_part = after((found, g_part), in_pairs)
        grads.append(
            [
                t_dot(found[0][:, :width], found[2]),
                t_dot(found[0][:, :width], found[3]),
                t_dot(found[4], g_part),
            ]
        )
        if c == 1:
            grads = [low + high for low, high in zip(*grads)]
        in_sum = square_scatter(expert_out[c][1])
        out_parts.append(dot(after(expert_out[c][5], expert_out[1][1]), down_w).astype(BF))
        in_sum, grads, out_parts = lax.optimization_barrier((in_sum, grads, out_parts))
        dots = tiny_scatter(expert_out[c][6].reshape(dps, seqs, chunk))
        in_sum = jnp.concatenate([in_sum, in_columns(dots[:, None])], axis=1)
        in_pairs += z_rounds(pieces_of(in_sum), 1)
    grad_gate, grad_up, grad_down = grads

    attn_columns = jnp.sum(attn_mix, axis=0)[:, None]
    hidden_total, total_high, norm_two_grad, logit_grad, *dh_sends = between(
        hidden, normed_two, g_low, norm_two, route_two, mlp_idx, mlp_flat, mlp_gates, attn_pick,
        attn_columns, in_pairs,
    )
    router_two_grad = jnp.dot(
        normed_two.astype(F32).T, logit_grad[:, :experts], precision=HIGH
    )

    dh_own, dh_other = [], []
    for c in range(2):
        dh_send = after(dh_sends[c * experts : (c + 1) * experts], *dh_own)
        dh_own.append(jnp.concatenate(z_rounds(dh_send, -1), axis=0))
        dh_other.append(swap_x(after(dh_own[-1], *dh_other)))
    dh_rows = jnp.stack([jnp.stack(dh_own), jnp.stack(dh_other)])
    dh_rows = dh_rows.reshape(seqs, 2, experts, part, width).transpose(0, 2, 1, 3, 4)
    dh_rows = dh_rows.reshape(total * cap, width)

    out_sums = [
        square_scatter(out_parts[0]),
        square_scatter(after(out_parts[1], dh_rows)),
    ]

    slot_dots = dot_t(total_high, jnp.concatenate(attn_pairs, axis=0))
    attn_gate_grad = jnp.concatenate(
        [jnp.sum(jnp.where(hot, slot_dots, 0.0), axis=1, keepdims=True) for hot in attn_hot], axis=1
    )
    mixed_grad = dot_t(dh_rows, out_w).astype(BF).reshape(total, cap, half)
    mixed_grad = after(mixed_grad, out_sums[0])
    out_pairs = z_rounds(pieces_of(out_sums[0]), 1)
    q_grad, *both_grad = attend_back(index, info, query, both, logs, mixed_grad)
    both_grad = after(both_grad, out_pairs)

    flat_normed = normed_all.reshape(total * tok, width)
    both_dots = [
        t_dot(flat_normed, array.reshape(total * tok, half))
        .astype(BF)
        .reshape(dps, seqs * rows_own, half)
        for array in both_grad
    ]
    q_grad, both_grad = after((q_grad, both_grad), out_sums[1])
    if is_small():
        firsts = [dp_first(dots) for dots in both_dots]
        q_grad, both_grad = after((q_grad, both_grad), [far for _, far in firsts])
    out_pairs += z_rounds(pieces_of(out_sums[1]), 1)
    q_grad = after(q_grad, out_pairs)
    q_slots = jnp.einsum("bct,bch->bth", pick, q_grad, preferred_element_type=F32).astype(BF)

    in_other = project_back(s_at, both_grad, q_slots, w_keep, w_took, experts, experts, dps)
    far_took = far_swap(in_other)
    if is_small():
        both_grads = [add_low(mine, after(swap_y(far), in_other)) for mine, far in firsts]
    else:
        both_grads = [
            lax.psum_scatter(dots, "dp", scatter_dimension=0, tiled=False) for dots in both_dots
        ]
    q_slots = after(q_slots, both_grads, far_took)
    in_own = project_back(s_at, both_grad, q_slots, w_keep, w_took, 0, experts, dps)
    one_sum, _ = group_scatter(in_own, in_other, far_took)
    shared = lax.psum(jnp.stack(both_grads), "expert")
    query_grads = t_dot(flat_normed, after(q_slots, in_own).reshape(total * tok, half)).astype(BF)
    query_grads = lax.psum_scatter(query_grads, "dp", scatter_dimension=0, tiled=True)
    dh_rows = after(dh_rows, in_own)
    grad_out_w = t_dot(mixed.reshape(total * cap, half), dh_rows).astype(BF)
    grad_out_w = lax.psum_scatter(grad_out_w, "dp", scatter_dimension=0, tiled=True)

    out_pairs = jnp.concatenate(out_pairs, axis=0)
    mlp_high, mlp_low = in_two(mlp_mix)
    output = hidden + dot(mlp_high, out_pairs) + dot(mlp_low, out_pairs)
    result_out = output.astype(BF).reshape(seq_count, stretch, width)

    def both_halves(arrays):
        arrays = [array.reshape(seqs, rows_own, half) for array in arrays]
        mine = [lax.dynamic_index_in_dim(array, s_at, 0, keepdims=False) for array in arrays]
        give = [lax.dynamic_index_in_dim(array, 1 - s_at, 0, keepdims=False) for array in arrays]
        return mine, [swap_x(array) for array in give]

    shared_mine, shared_took = both_halves([shared[0], shared[1]])
    one_sum = after(one_sum, shared_took)
    shared_grads = join_columns(s_at, shared_mine, shared_took, dps, F32)
    query_mine, query_took = both_halves([query_grads])
    (grad_query,) = join_columns(s_at, query_mine, query_took, dps, F32)

    router_one_grad, router_one_input = gate_grads(
        normed_one, route_one, attn_idx, attn_gates, attn_gate_grad
    )
    normed_one_grad = one_sum + router_one_input
    input_grad, norm_one_grad = norm_back(x_in, norm_one, normed_one_grad)
    grad_x = (hidden_total + input_grad).astype(BF).reshape(seq_count, stretch, width)

    norm_one_grad = after(norm_one_grad, query_took)
    little = little_sum(
        jnp.concatenate(
            [norm_one_grad[None], router_one_grad.T, norm_two_grad, router_two_grad.T], axis=0
        )
    )
    return (
        result_out,
        grad_x,
        little[0],
        little[1 : 1 + experts].T,
        shared_grads[0],
        shared_grads[1],
        grad_query[None],
        grad_out_w.astype(F32)[None],
        little[1 + experts],
        little[2 + experts :].T,
        grad_gate[None],
        grad_up[None],
        grad_down[None],
    )


def solution(mesh):
    in_specs = (
        P("dp", ("expert", "seq"), None),
        P("dp"),
        P("dp", ("expert", "seq"), None),
        P("dp", ("expert", "seq"), None),
        P("dp", ("expert", "seq"), None),
        P(("dp", "seq")),
        P(("dp", "seq"), None),
        P(("dp", "seq"), None),
        P(("dp", "seq"), None),
        P("expert", ("dp", "seq"), None),
        P("expert", ("dp", "seq"), None),
        P(("dp", "seq")),
        P(("dp", "seq"), None),
        P("expert", None, ("dp", "seq")),
        P("expert", None, ("dp", "seq")),
        P("expert", ("dp", "seq"), None),
        P("dp", ("expert", "seq"), None),
    )
    out_specs = (
        P("dp", ("expert", "seq"), None),
        P("dp", ("expert", "seq"), None),
        P(("dp", "seq")),
        P(("dp", "seq"), None),
        P(("dp", "seq"), None),
        P(("dp", "seq"), None),
        P("expert", ("dp", "seq"), None),
        P("expert", ("dp", "seq"), None),
        P(("dp", "seq")),
        P(("dp", "seq"), None),
        P("expert", None, ("dp", "seq")),
        P("expert", None, ("dp", "seq")),
        P("expert", ("dp", "seq"), None),
    )
    return jax.shard_map(body, mesh=mesh, in_specs=in_specs, out_specs=out_specs, check_vma=False)
```
